32 devices in a mesh: dp: 8 (over z, x), head: 4 (over y, core).
Axes of the slice: x: 2, y: 2, z: 4, core: 2. Of those that a mesh axis runs over, the one named last changes fastest.
Arguments:
- hidden_in: bfloat16 [32, 512, 768], P('dp', 'head'), may hold values from -6 to 6
- seq_lengths: int32 [8, 4], P('dp'), may hold values from 1 to 512, 1280 in all within a row
- batch_order: int32 [8, 4], P('dp'), may hold values from 0 to 3, each once within a row
- clip_ranges: float32 [1, 4], replicated, may hold values from 0.75 to 2.5
- proj_weight: bfloat16 [1, 3, 768, 768], P(None, None, None, 'head'), may hold values from -0.3125 to 0.3125
- proj_bias: bfloat16 [1, 2, 768], P(None, None, 'head'), may hold values from -1.796875 to 1.796875
- out_weight: bfloat16 [1, 768, 768], P(None, 'head'), may hold values from -0.875 to 0.875
- up_weight: bfloat16 [1, 768, 3072], P(None, None, 'head'), may hold values from -0.21875 to 0.21875
- up_bias: bfloat16 [1, 3072], P(None, 'head'), may hold values from -1.796875 to 1.796875
- down_weight: bfloat16 [1, 3072, 768], P(None, 'head'), may hold values from -0.109375 to 0.109375
- norm_gains: bfloat16 [1, 2, 768], replicated, may hold values from 0.5 to 1.5
- out_biases: bfloat16 [1, 4, 768], replicated, may hold values from -1.796875 to 1.796875
- cotangent: bfloat16 [32, 512, 768], P('dp', 'head'), may hold values from -6 to 6
Outputs:
- hidden_out: float32 [32, 512, 768], P('dp', 'head')
- input_grad: float32 [32, 512, 768], P('dp', 'head')
- proj_grad: float32 [1, 3, 768, 768], P(None, None, 'dp', 'head')
- bias_grad: float32 [1, 2, 768], replicated
- out_grad: float32 [1, 768, 768], P(None, 'head', 'dp')
- up_grad: float32 [1, 768, 3072], P(None, 'dp', 'head')
- offset_grad: float32 [1, 3072], replicated
- down_grad: float32 [1, 3072, 768], P(None, 'head', 'dp')
- gain_grad: float32 [1, 2, 768], replicated
- shift_grad: float32 [1, 4, 768], replicated
- new_ranges: float32 [1, 4], replicated
The draws below stay inside these ranges and needn't reach their ends.
Inputs may be any that keep to these rules, and one draw needn't show every extreme that they name: `seq_lengths`: each row holds the lengths of one dp group's 4 sequence slots; one of them is exactly 512, and a row sums to 1280. `batch_order`: each row is a permutation of the slots 0 .. 3.
All inputs are finite; a program needn't handle non-finite values.
Results may differ from the reference program's by a relative error of at most 0.013.
The reference program's roundings to bfloat16 on the way count: a program that leaves them out, or rounds other values in their place, can miss the bound.
Values may be sent and summed in bfloat16 or wider, within the bound.
A program may use at most 128 MiB of HBM per device.

```python
import math
import jax
import jax.numpy as jnp
import numpy as np
from jax import lax

D = 768
HEAD_DIM = 64
FF = 3072
LAYERS = 1
SLOT = 512
MB = 4
SEQS = 32
N_DP = 8


def levels(stream_key, extent, cuts, smallest, high):
    loudness = 1.0
    for dim, blocks in cuts:
        draws = jax.random.uniform(jax.random.fold_in(jax.random.fold_in(stream_key, 6), dim), (blocks,), jnp.float32, smallest / len(cuts), high / len(cuts))
        loudness = loudness * jnp.repeat(jnp.exp(draws), extent[dim] // blocks).reshape((-1,) + (1,) * (len(extent) - 1 - dim))
    return loudness


def profile(amount, total, reach, slope):
    portions = [(1 << 20) // math.isqrt(rank ** slope) + 1 for rank in range(2, amount + 1)]
    rest, counts = total - reach - (amount - 1), [1] * (amount - 1)
    while rest > 0:
        free = [i for i in range(amount - 1) if counts[i] < reach]
        whole, remaining = sum([portions[i] for i in free]), rest
        for i in free:
            extra = min(reach - counts[i], max(1, remaining * portions[i] // whole), rest)
            counts[i] = counts[i] + extra
            rest = rest - extra
    return np.array([reach] + counts)


def ragged(stream_key, number_of, total, limit, lean):
    if number_of == 2:
        one = jax.random.randint(stream_key, (), max(1, total - limit), min(limit, total - 1) + 1)
        return jnp.stack([one, total - one])
    tallies = jnp.asarray(profile(number_of, total, limit, lean), jnp.int32)
    pairs = (number_of - 1) // 2
    giver, taker = tallies[1:1 + 2 * pairs:2], tallies[2:2 + 2 * pairs:2]
    slack = jnp.minimum(giver - 1, limit - taker)
    passed = jax.random.randint(jax.random.fold_in(stream_key, 1), (pairs,), 0, 1 << 20) % (slack + 1)
    tallies = tallies.at[1:1 + 2 * pairs:2].set(giver - passed).at[2:2 + 2 * pairs:2].set(taker + passed)
    return tallies[jax.random.permutation(jax.random.fold_in(stream_key, 2), number_of)]


def gaussian(own_key, shape, scale, reach, cuts=(), kind=jnp.bfloat16):
    values = scale * jax.random.normal(own_key, shape, jnp.float32)
    if cuts:
        values = values * levels(own_key, shape, cuts, -0.22, 0.18)
    return jnp.clip(values, -reach, reach).astype(kind)


def setup_inputs(seed: int = 0) -> dict:
    key_of = jax.random.split(jax.random.key(seed), 14)
    hidden_in = gaussian(key_of[0], (SEQS, SLOT, D), 1.0, 6.0, ((0, 8), (1, 4)))
    seq_lengths = jax.vmap(lambda own: ragged(own, MB, SLOT + (MB - 1) * SLOT // 2, SLOT, 0))(jax.random.split(key_of[1], N_DP)).reshape((N_DP, MB)).astype(jnp.int32)
    batch_order = jax.vmap(lambda own: jax.random.permutation(own, MB))(jax.random.split(key_of[2], N_DP)).reshape((N_DP, MB)).astype(jnp.int32)
    clip_ranges = jnp.clip(jnp.exp(jax.random.uniform(key_of[3], (LAYERS, 4), jnp.float32, math.log(0.75), math.log(2.5))), 0.75, 2.5)
    proj_weight = gaussian(key_of[4], (LAYERS, 3, D, D), (D // 2) ** -0.5, 0.3125, ((3, 4),))
    proj_bias = gaussian(key_of[5], (LAYERS, 2, D), 0.3, 1.796875, ((2, 4),))
    out_weight = gaussian(key_of[6], (LAYERS, D, D), (D // 16) ** -0.5, 0.875, ((1, 4),))
    up_weight = gaussian(key_of[7], (LAYERS, D, FF), D ** -0.5, 0.21875, ((2, 4),))
    up_bias = gaussian(key_of[8], (LAYERS, FF), 0.3, 1.796875, ((1, 4),))
    down_weight = gaussian(key_of[9], (LAYERS, FF, D), FF ** -0.5, 0.109375, ((1, 4),))
    norm_gains = jnp.clip(1.0 + 0.1 * jax.random.normal(key_of[10], (LAYERS, 2, D), jnp.float32), 0.5, 1.5).astype(jnp.bfloat16)
    out_biases = gaussian(key_of[11], (LAYERS, 4, D), 0.3, 1.796875)
    cotangent = gaussian(key_of[12], (SEQS, SLOT, D), 1.0, 6.0, ((0, 8), (1, 4)))
    return dict(hidden_in=hidden_in, seq_lengths=seq_lengths, batch_order=batch_order, clip_ranges=clip_ranges, proj_weight=proj_weight, proj_bias=proj_bias, out_weight=out_weight, up_weight=up_weight, up_bias=up_bias, down_weight=down_weight, norm_gains=norm_gains, out_biases=out_biases, cotangent=cotangent)


@jax.custom_vjp
def low(v):
    return lax.optimization_barrier(v.astype(jnp.bfloat16)).astype(jnp.float32)

@jax.custom_vjp
def low_back(v):
    return v

def low_keep(v):
    return (low(v), None)

def low_pass(kept, grad):
    return (grad,)

def back_keep(v):
    return (v, None)

def back_low(kept, grad):
    return (low(grad),)
low.defvjp(low_keep, low_pass)
low_back.defvjp(back_keep, back_low)
EPSILON = 1e-06
MASK_FILL = -1e+30
DECAY = 0.9
HIGH = lax.Precision.HIGHEST

def soft_clip(values, ceiling):
    return ceiling * jnp.tanh(values / ceiling)

def layer_norm(hidden, norm_gain, norm_shift):
    centred = hidden - lax.optimization_barrier(jnp.mean(hidden, axis=-1, keepdims=True))
    spread = lax.optimization_barrier(jnp.mean(centred * centred, axis=-1, keepdims=True))
    return centred * lax.rsqrt(spread + EPSILON) * norm_gain + norm_shift

def dot_high(left, right):
    return jnp.dot(left, right, precision=HIGH, preferred_element_type=jnp.float32)

def peak_of(values, live):
    return jnp.max(jnp.where(live[:, None], jnp.abs(values), 0.0))

def attend_one(packed):
    queries, key_rows, value_rows, length = packed
    head_count = D // HEAD_DIM
    query_heads = queries.reshape(SLOT, head_count, HEAD_DIM)
    key_heads = key_rows.reshape(SLOT, head_count, HEAD_DIM)
    value_heads = value_rows.reshape(SLOT, head_count, HEAD_DIM)
    scores = low_back(jnp.einsum('qhd,khd->hqk', query_heads, key_heads, precision=HIGH) * HEAD_DIM ** (-0.5))
    key_live = jnp.arange(SLOT, dtype=jnp.int32) < length
    scores = jnp.where(key_live[None, None, :], scores, MASK_FILL)
    weights_soft = low(jax.nn.softmax(scores, axis=-1))
    context = jnp.einsum('hqk,khd->qhd', weights_soft, value_heads, precision=HIGH)
    return low_back(context).reshape(SLOT, D)

def forward_layer(hidden, weights, limits, lengths):
    proj_w, proj_b, out_w, up_w, up_b, down_w, gain_rows, shifts = weights
    count = hidden.shape[0]
    flat = hidden.reshape(count * SLOT, D)
    live = (jnp.arange(SLOT, dtype=jnp.int32)[None, :] < lengths[:, None]).reshape(-1)
    clipped = low(soft_clip(flat, limits[0]))
    queries = low(low_back(dot_high(clipped, proj_w[0]) + proj_b[0]))
    key_rows = low(low_back(dot_high(clipped, proj_w[1])))
    value_rows = low(low_back(dot_high(clipped, proj_w[2]) + proj_b[1]))
    context = lax.map(jax.checkpoint(attend_one), (queries.reshape(count, SLOT, D), key_rows.reshape(count, SLOT, D), value_rows.reshape(count, SLOT, D), lengths)).reshape(count * SLOT, D)
    ctx_clip = low(soft_clip(context, limits[1]))
    mixed = flat + (low_back(dot_high(ctx_clip, out_w)) + shifts[0])
    normed = layer_norm(mixed, gain_rows[0], shifts[1])
    norm_clip = low(soft_clip(normed, limits[2]))
    pre_act = low_back(dot_high(norm_clip, up_w) + up_b)
    activation = jax.nn.gelu(pre_act, approximate=False)
    act_clip = low(soft_clip(activation, limits[3]))
    summed = normed + (low_back(dot_high(act_clip, down_w)) + shifts[2])
    result = layer_norm(summed, gain_rows[1], shifts[3])
    peaks = jnp.stack([peak_of(flat, live), peak_of(context, live), peak_of(normed, live), peak_of(activation, live)])
    return (result.reshape(count, SLOT, D), peaks)

def reference(hidden_in, seq_lengths, batch_order, clip_ranges, proj_weight, proj_bias, out_weight, up_weight, up_bias, down_weight, norm_gains, out_biases, cotangent):
    params = tuple((item.astype(jnp.float32) for item in (proj_weight, proj_bias, out_weight, up_weight, up_bias, down_weight, norm_gains, out_biases)))
    inputs = hidden_in.astype(jnp.float32)
    grads_in = cotangent.astype(jnp.float32)
    limits = clip_ranges
    results = jnp.zeros_like(inputs)
    input_grads = jnp.zeros_like(inputs)
    totals = tuple((jnp.zeros_like(item) for item in params))
    starts = jnp.arange(N_DP, dtype=jnp.int32) * MB
    flat_lengths = seq_lengths.reshape(-1)
    for micro_step in range(MB):
        order_index = (starts + batch_order[:, micro_step]).astype(jnp.int32)
        lengths = flat_lengths[order_index]
        ranges_now = limits

        def model(current, weights):
            peak_rows = []
            for layer_idx in range(LAYERS):
                layer_params = tuple((item[layer_idx] for item in weights))
                current, peaks = forward_layer(current, layer_params, ranges_now[layer_idx], lengths)
                peak_rows.append(peaks)
            return (current, jnp.stack(peak_rows))
        output, back_fn, peak_table = jax.vjp(model, inputs[order_index], params, has_aux=True)
        grad_input, grad_params = back_fn(grads_in[order_index])
        results = results.at[order_index].set(output)
        input_grads = input_grads.at[order_index].set(grad_input)
        totals = tuple((first + second for first, second in zip(totals, grad_params)))
        limits = DECAY * limits + (1.0 - DECAY) * peak_table
    return (results, input_grads, totals[0], totals[1], totals[2], totals[3], totals[4], totals[5], totals[6], totals[7], limits)
```

```python
import functools
import jax
import jax.numpy as jnp
from jax import lax
from jax.experimental import pallas as pl
from jax.experimental.pallas import tpu as pltpu
from jax.sharding import PartitionSpec as P

HEAD_DIM = 64
EPSILON = 1e-06
MASK_FILL = -1e30
DECAY = 0.9
MESH = pl.DeviceIdType.MESH
BF16 = jnp.bfloat16
F32 = jnp.float32
ANY = pl.BlockSpec(memory_space=pl.ANY)
VM = pl.BlockSpec(memory_space=pltpu.VMEM)


def soft_clip(values, ceiling):
    return ceiling * jnp.tanh(values / ceiling)


def clip_slope(values, ceiling):
    tangent = jnp.tanh(values / ceiling)
    return 1.0 - tangent * tangent


def remote(src, dst, send_sem, recv_sem, where):
    return pltpu.make_async_remote_copy(
        src_ref=src, dst_ref=dst, send_sem=send_sem, recv_sem=recv_sem,
        device_id=where, device_id_type=MESH,
    )


def greet(peers):
    bar = pltpu.get_barrier_semaphore()
    for peer in peers:
        pl.semaphore_signal(bar, inc=1, device_id=peer, device_id_type=MESH)
    pl.semaphore_wait(bar, len(peers))


def top_kernel(nd, nh, v_ref, o_ref, slots, send_sem, recv_sem):
    n = nd * nh
    g = lax.axis_index("dp")
    h = lax.axis_index("head")

    def peer(d):
        return (lax.rem(g + d // nh, nd), lax.rem(h + lax.rem(d, nh), nh))

    bar = pltpu.get_barrier_semaphore()

    def hello(d, carry):
        pl.semaphore_signal(bar, inc=1, device_id=peer(d), device_id_type=MESH)
        return carry

    lax.fori_loop(1, n, hello, 0)
    pl.semaphore_wait(bar, n - 1)

    def send(d, carry):
        remote(v_ref, slots.at[d - 1], send_sem, recv_sem, peer(d)).start()
        return carry

    lax.fori_loop(1, n, send, 0)
    pltpu.make_async_copy(slots, slots, recv_sem).wait()
    pltpu.make_async_copy(slots, slots, send_sem).wait()
    o_ref[...] = jnp.maximum(v_ref[...], jnp.max(slots[...], axis=0))


def top_all(values, collective_id):
    nd, nh = lax.axis_size("dp"), lax.axis_size("head")
    return pl.pallas_call(
        functools.partial(top_kernel, nd, nh),
        out_shape=jax.ShapeDtypeStruct(values.shape, values.dtype),
        in_specs=[VM],
        out_specs=VM,
        scratch_shapes=[
            pltpu.VMEM((nd * nh - 1,) + values.shape, values.dtype),
            pltpu.SemaphoreType.DMA,
            pltpu.SemaphoreType.DMA,
        ],
        compiler_params=pltpu.CompilerParams(collective_id=collective_id, has_side_effects=True),
    )(values)


def bring_kernel(x_in, dy_in, wa, wu, wd, bias, x_out, dy_out, wa_out, wu_out, wd_out, bias_out,
                 local_sem, send_sem, recv_sem):
    g = lax.axis_index("dp")
    h = lax.axis_index("head")
    peers = [(g, h ^ k) for k in (1, 2, 3)]
    greet(peers)
    count = [0]
    sent = []

    def go(src, dst, k):
        i = count[0]
        count[0] += 1
        copy = remote(src, dst, send_sem.at[i], recv_sem.at[i], (g, h ^ k))
        copy.start()
        sent.append(copy)
        return copy

    own = []

    def keep(src, dst):
        copy = pltpu.make_async_copy(src, dst, local_sem.at[len(own)])
        copy.start()
        own.append(copy)

    keep(x_in.at[h], x_out.at[0])
    keep(dy_in.at[h], dy_out.at[0])
    waits = []
    for k in (2, 3, 1):
        waits.append(go(x_in.at[h ^ k], x_out.at[k], k))
    relays = []
    for src, dst in ((wa, wa_out), (wu, wu_out), (wd, wd_out)):
        keep(src, dst.at[0])
        waits.append(go(src, dst.at[1], 1))
        relays.append((go(src, dst.at[2], 2), dst))
    keep(bias, bias_out.at[0])
    for k in (1, 2, 3):
        waits.append(go(bias, bias_out.at[k], k))
    for k in (2, 3, 1):
        waits.append(go(dy_in.at[h ^ k], dy_out.at[k], k))
    for copy, dst in relays:
        copy.wait_recv()
        waits.append(go(dst.at[2], dst.at[3], 1))
    for copy in own:
        copy.wait()
    for copy in waits:
        copy.wait_recv()
    for copy in sent:
        copy.wait_send()


def bring(x_in, dy_in, wa, wu, wd, bias):
    nh = lax.axis_size("head")

    def times(a):
        return jax.ShapeDtypeStruct((nh,) + a.shape, a.dtype)

    return pl.pallas_call(
        bring_kernel,
        out_shape=(
            jax.ShapeDtypeStruct(x_in.shape, x_in.dtype),
            jax.ShapeDtypeStruct(dy_in.shape, dy_in.dtype),
            times(wa), times(wu), times(wd), times(bias),
        ),
        in_specs=[ANY] * 6,
        out_specs=[ANY] * 6,
        scratch_shapes=[
            pltpu.SemaphoreType.DMA((6,)),
            pltpu.SemaphoreType.DMA((18,)),
            pltpu.SemaphoreType.DMA((18,)),
        ],
        compiler_params=pltpu.CompilerParams(collective_id=0, has_side_effects=True),
    )(x_in, dy_in, wa, wu, wd, bias)


def settle_kernel(nz, rows, cols, grads, small, rows_out, rows_in,
                  sums, small_sum, rows_back_out, rows_back_in,
                  own1, got1, s1, got_a, got_b, s2a, s2b, got_c, got_d, s3, got4,
                  small_now, small_got, small_z,
                  local_sem, send_sem, recv_sem):
    g = lax.axis_index("dp")
    h = lax.axis_index("head")
    z = g // 2
    p = lax.rem(g, 2)
    half = cols // 2
    core, across, xside = (g, h ^ 1), (g, h ^ 2), (z * 2 + (1 - p), h)
    zpeers = [(lax.rem(z + d, nz) * 2 + p, h) for d in range(1, nz)]
    greet([core, across, (g, h ^ 3), xside] + zpeers)
    count = [0]
    sent = []

    def go(src, dst, where):
        i = count[0]
        count[0] += 1
        copy = remote(src, dst, send_sem.at[i], recv_sem.at[i], where)
        copy.start()
        sent.append(copy)
        return copy

    chunks = range(3)
    first = []
    own = []
    for c in chunks:
        first.append([go(grads[c].at[2 * j + 1], got1.at[c, j], core) for j in (0, 1)])
        pair = []
        for j in (0, 1):
            copy = pltpu.make_async_copy(grads[c].at[2 * j], own1.at[c, j], local_sem.at[2 * c + j])
            copy.start()
            pair.append(copy)
        own.append(pair)
    small_now[0] = small[...]
    small_copy = go(small_now.at[0], small_got.at[0], core)
    tail = []
    for src, dst in ((rows_out, rows_back_out), (rows_in, rows_back_in)):
        for k in (1, 2, 3):
            tail.append(go(src.at[k], dst.at[k], (g, h ^ k)))
    ya, xa = [], []
    for c in chunks:
        for copy in first[c]:
            copy.wait_recv()
        for copy in own[c]:
            copy.wait()

        def add1(i, carry):
            zz, xx = i // 2, lax.rem(i, 2)
            for j in (0, 1):
                s1[c, j, zz, xx] = (
                    own1[c, j, zz, xx].astype(F32) + got1[c, j, zz, xx].astype(F32)
                ).astype(BF16)
            return carry

        lax.fori_loop(0, 2 * nz, add1, 0)
        ya.append(go(s1.at[c, 1, :, :, :, pl.ds(0, half)], got_a.at[c], across))
        xa.append(go(s1.at[c, :, :, 1 - p, :, pl.ds(half, half)], got_b.at[c], xside))
        if c == 0:
            small_copy.wait_recv()
            small_now[1] = small_now[0] + small_got[0]
            small_copy = go(small_now.at[1], small_got.at[1], across)
    xb, yb = [], []
    for c in chunks:
        ya[c].wait_recv()

        def add2(i, carry):
            for xx in (0, 1):
                s2a[c, i, xx] = (
                    s1[c, 0, i, xx, :, :half].astype(F32) + got_a[c, i, xx].astype(F32)
                ).astype(BF16)
            return carry

        lax.fori_loop(0, nz, add2, 0)
        xb.append(go(s2a.at[c, :, 1 - p], got_c.at[c], xside))
        xa[c].wait_recv()

        def add3(i, carry):
            for j in (0, 1):
                s2b[c, j, i] = (
                    s1[c, j, i, p, :, half:].astype(F32) + got_b[c, j, i].astype(F32)
                ).astype(BF16)
            return carry

        lax.fori_loop(0, nz, add3, 0)
        yb.append(go(s2b.at[c, 1], got_d.at[c], across))
        if c == 0:
            small_copy.wait_recv()
            small_now[2] = small_now[1] + small_got[1]
            small_copy = go(small_now.at[2], small_got.at[2], xside)
    zs = []
    for c in chunks:
        xb[c].wait_recv()
        yb[c].wait_recv()

        def add4(i, carry):
            s3[c, i, :, :half] = (
                s2a[c, i, p].astype(F32) + got_c[c, i].astype(F32)
            ).astype(BF16)
            s3[c, i, :, half:] = (
                s2b[c, 0, i].astype(F32) + got_d[c, i].astype(F32)
            ).astype(BF16)
            return carry

        lax.fori_loop(0, nz, add4, 0)
        zs.append([
            go(s3.at[c, lax.rem(z + d, nz)], got4.at[c, d - 1], zpeers[d - 1]) for d in range(1, nz)
        ])
        if c == 0:
            small_copy.wait_recv()
            small_now[3] = small_now[2] + small_got[2]
            small_last = [
                go(small_now.at[3], small_z.at[d - 1], zpeers[d - 1]) for d in range(1, nz)
            ]
    for c in chunks:
        for copy in zs[c]:
            copy.wait_recv()
        total = s3[c, z].astype(F32)
        for d in range(1, nz):
            total = total + got4[c, d - 1].astype(F32)
        sums[c] = total
    for copy in small_last:
        copy.wait_recv()
    total = small_now[3]
    for d in range(1, nz):
        total = total + small_z[d - 1]
    small_sum[...] = total
    for copy in tail:
        copy.wait_recv()
    for copy in sent:
        copy.wait_send()


def settle(grads, small, rows_out, rows_in):
    nd = lax.axis_size("dp")
    nz = nd // 2
    nh, depth, cols = grads[0].shape
    rows = depth // nd
    half = cols // 2
    cut = [item.reshape(nh, nz, 2, rows, cols) for item in grads]
    copies = 3 * (2 + 2 + 2 + nz - 1) + 3 + (nz - 1) + 6

    def kernel(g0, g1, g2, *rest):
        settle_kernel(nz, rows, cols, (g0, g1, g2), *rest)

    return pl.pallas_call(
        kernel,
        out_shape=(
            jax.ShapeDtypeStruct((3, rows, cols), F32),
            jax.ShapeDtypeStruct(small.shape, F32),
            jax.ShapeDtypeStruct(rows_out.shape, rows_out.dtype),
            jax.ShapeDtypeStruct(rows_in.shape, rows_in.dtype),
        ),
        in_specs=[ANY] * 3 + [VM] + [ANY] * 2,
        out_specs=[VM, VM, ANY, ANY],
        scratch_shapes=[
            pltpu.VMEM((3, 2, nz, 2, rows, cols), BF16),
            pltpu.VMEM((3, 2, nz, 2, rows, cols), BF16),
            pltpu.VMEM((3, 2, nz, 2, rows, cols), BF16),
            pltpu.VMEM((3, nz, 2, rows, half), BF16),
            pltpu.VMEM((3, 2, nz, rows, half), BF16),
            pltpu.VMEM((3, nz, 2, rows, half), BF16),
            pltpu.VMEM((3, 2, nz, rows, half), BF16),
            pltpu.VMEM((3, nz, rows, half), BF16),
            pltpu.VMEM((3, nz, rows, half), BF16),
            pltpu.VMEM((3, nz, rows, cols), BF16),
            pltpu.VMEM((3, nz - 1, rows, cols), BF16),
            pltpu.VMEM((4,) + small.shape, F32),
            pltpu.VMEM((3,) + small.shape, F32),
            pltpu.VMEM((nz - 1,) + small.shape, F32),
            pltpu.SemaphoreType.DMA((6,)),
            pltpu.SemaphoreType.DMA((copies,)),
            pltpu.SemaphoreType.DMA((copies,)),
        ],
        compiler_params=pltpu.CompilerParams(
            collective_id=1, has_side_effects=True, vmem_limit_bytes=60 * 1024 * 1024
        ),
    )(*cut, small, rows_out, rows_in)


def settle_plain(grads, small, rows_out, rows_in, head_pos):
    nh, depth, cols = grads[0].shape
    stacked = jnp.stack(grads)
    order = head_pos ^ jnp.arange(nh)
    stacked = stacked[:, order].astype(F32)
    part = lax.psum_scatter(stacked, "head", scatter_dimension=1, tiled=True)[:, 0]
    sums = lax.psum_scatter(part, "dp", scatter_dimension=1, tiled=True)

    def swap(rows):
        return jnp.stack([rows[0]] + [
            lax.ppermute(rows[k], "head", [(i, i ^ k) for i in range(nh)]) for k in range(1, nh)
        ])

    return sums, lax.psum(small, ("dp", "head")), swap(rows_out), swap(rows_in)


def dot(a, b, dims):
    return lax.dot_general(a, b, (dims, ((), ())), preferred_element_type=F32)


NN = ((1,), (0,))
NT = ((1,), (1,))
TN = ((0,), (0,))


def norm_parts(z):
    centred = z - jnp.mean(z, axis=-1, keepdims=True)
    inv = lax.rsqrt(jnp.mean(centred * centred, axis=-1, keepdims=True) + EPSILON)
    return centred * inv, inv


def norm_back(dn, n, inv):
    return (dn - jnp.mean(dn, axis=-1, keepdims=True)
            - n * jnp.mean(dn * n, axis=-1, keepdims=True)) * inv


def body(hidden_in, seq_lengths, batch_order, clip_ranges, proj_weight, proj_bias, out_weight,
         up_weight, up_bias, down_weight, norm_gains, out_biases, cotangent):
    nd, nh = lax.axis_size("dp"), lax.axis_size("head")
    h = lax.axis_index("head")
    slots, part, width = hidden_in.shape
    lengths = seq_lengths[0]
    order = batch_order[0]
    hcols = proj_bias.shape[2]
    fcols = up_bias.shape[1]
    heads = hcols // HEAD_DIM
    local_pos = h * part + jnp.arange(part, dtype=jnp.int32)
    mine = jnp.max(
        jnp.where((local_pos[None, :] < lengths[:, None])[:, :, None], jnp.abs(hidden_in), 0.0).astype(F32),
        axis=(1, 2),
    )
    wa = jnp.concatenate(
        [proj_weight[0].transpose(0, 2, 1).reshape(3 * hcols, width), out_weight[0]], axis=0
    )
    bias = jnp.zeros((8, fcols), F32).at[0:2, :hcols].set(proj_bias[0].astype(F32)).at[2].set(
        up_bias[0].astype(F32)
    )
    xs, dys, was, wus, wds, biases = bring(hidden_in, cotangent, wa, up_weight[0], down_weight[0], bias)

    m_own = jnp.argmax(order == h).astype(jnp.int32)
    length = lengths[h]
    blocks = h ^ jnp.arange(nh, dtype=jnp.int32)
    pos = (blocks[:, None] * part + jnp.arange(part, dtype=jnp.int32)[None, :]).reshape(-1)
    live = pos < length

    def top(cand, cid):
        row = jnp.zeros((1, 128), F32).at[0, : cand.shape[0]].set(cand)
        return top_all(row, cid)[0, : cand.shape[0]]

    def at_own(value):
        return jnp.where(jnp.arange(slots) == m_own, value, 0.0)

    def ranges(start, tops):
        now, rows = start, []
        for m in range(slots):
            rows.append(now)
            now = DECAY * now + (1.0 - DECAY) * tops[m]
        return jnp.stack(rows)[m_own], now

    def peak(values):
        return jnp.max(jnp.where(live[:, None], jnp.abs(values), 0.0))

    r0, new0 = ranges(clip_ranges[0, 0], top(mine[order], 2))
    x = xs.reshape(slots * part, width).astype(F32)
    a = soft_clip(x, r0).astype(BF16)
    gain1, gain2 = norm_gains[0].astype(F32)
    bo, ca, bd, cb = out_biases[0].astype(F32)
    q_rows, c_parts, lses = [], [], []
    scale = HEAD_DIM ** -0.5
    for k in range(nh):
        qkv = dot(a, was[k, : 3 * hcols], NT)
        qkv = qkv + jnp.concatenate([biases[k, 0, :hcols], jnp.zeros((hcols,), F32), biases[k, 1, :hcols]])
        qkv = qkv.astype(BF16)
        q_rows.append(qkv)
        q, kk, v = [qkv[:, i * hcols:(i + 1) * hcols].reshape(-1, heads, HEAD_DIM) for i in range(3)]
        s = jnp.einsum("qhd,khd->hqk", q, kk, preferred_element_type=F32) * scale
        s = jnp.where(live[None, None, :], s, MASK_FILL)
        topv = jnp.max(s, axis=-1, keepdims=True)
        e = jnp.exp(s - topv)
        den = jnp.sum(e, axis=-1, keepdims=True)
        lses.append(topv + jnp.log(den))
        pb = (e / den).astype(BF16)
        c_parts.append(jnp.einsum("hqk,khd->qhd", pb, v, preferred_element_type=F32).reshape(-1, hcols))
    c = jnp.concatenate(c_parts, axis=1)
    r1, new1 = ranges(clip_ranges[0, 1], top(at_own(peak(c)), 2))
    cq = soft_clip(c, r1).astype(BF16)
    o1 = sum(dot(cq[:, k * hcols:(k + 1) * hcols], was[k, 3 * hcols:], NN) for k in range(nh))
    n1, inv1 = norm_parts(x + (o1 + bo))
    y1 = n1 * gain1 + ca
    r2, new2 = ranges(clip_ranges[0, 2], top(at_own(peak(y1)), 2))
    b = soft_clip(y1, r2).astype(BF16)
    fs = [dot(b, wus[k], NN) + biases[k, 2] for k in range(nh)]
    gs = [jax.nn.gelu(f, approximate=False) for f in fs]
    gmax = functools.reduce(jnp.maximum, [peak(v) for v in gs])
    r3, new3 = ranges(clip_ranges[0, 3], top(at_own(gmax), 2))
    gq = [soft_clip(v, r3).astype(BF16) for v in gs]
    o2 = sum(dot(gq[k], wds[k], NN) for k in range(nh))
    n2, inv2 = norm_parts(y1 + (o2 + bd))
    out = n2 * gain2 + cb
    dy = dys.reshape(slots * part, width).astype(F32)
    dz = norm_back(dy * gain2, n2, inv2)
    dzb = dz.astype(BF16)
    d_gb, d_cb, d_bd = jnp.sum(dy * n2, axis=0), jnp.sum(dy, axis=0), jnp.sum(dz, axis=0)
    g_down, g_up, g_bu, db = [], [], [], 0.0
    for k in range(nh):
        g_down.append(dot(dzb, gq[k], TN).astype(BF16))
        f = fs[k]
        cdf = 0.5 * (1.0 + lax.erf(f * 0.5 ** 0.5))
        slope = cdf + f * (jnp.exp(-0.5 * f * f) * (1.0 / (2.0 * jnp.pi) ** 0.5))
        df = (dot(dzb, wds[k], NT) * clip_slope(gs[k], r3) * slope).astype(BF16)
        g_up.append(dot(b, df, TN).astype(BF16))
        g_bu.append(jnp.sum(df.astype(F32), axis=0))
        db = db + dot(df, wus[k], NT)
    dy1 = dz + db * clip_slope(y1, r2)
    d_ga, d_ca = jnp.sum(dy1 * n1, axis=0), jnp.sum(dy1, axis=0)
    dh = norm_back(dy1 * gain1, n1, inv1)
    d_bo = jnp.sum(dh, axis=0)
    dhb = dh.astype(BF16)
    g_attn, g_pb, da = [], [], 0.0
    for k in range(nh):
        g_o = dot(dhb, cq[:, k * hcols:(k + 1) * hcols], TN).astype(BF16)
        dc = (dot(dhb, was[k, 3 * hcols:], NT) * clip_slope(c_parts[k], r1)).astype(BF16)
        dc = dc.reshape(-1, heads, HEAD_DIM)
        q, kk, v = [q_rows[k][:, i * hcols:(i + 1) * hcols].reshape(-1, heads, HEAD_DIM) for i in range(3)]
        s = jnp.einsum("qhd,khd->hqk", q, kk, preferred_element_type=F32) * scale
        s = jnp.where(live[None, None, :], s, MASK_FILL)
        pp = jnp.exp(s - lses[k])
        dv = jnp.einsum("hqk,qhd->khd", pp.astype(BF16), dc, preferred_element_type=F32)
        dp = jnp.einsum("qhd,khd->hqk", dc, v, preferred_element_type=F32)
        ds = (pp * (dp - jnp.sum(dp * pp, axis=-1, keepdims=True))).astype(BF16)
        dq = jnp.einsum("hqk,khd->qhd", ds, kk, preferred_element_type=F32) * scale
        dk = jnp.einsum("hqk,qhd->khd", ds, q, preferred_element_type=F32) * scale
        dqkv = jnp.concatenate([t.reshape(-1, hcols) for t in (dq, dk, dv)], axis=1).astype(BF16)
        g_attn.append(jnp.concatenate([dot(a, dqkv, TN).astype(BF16), g_o], axis=1))
        sums = jnp.sum(dqkv.astype(F32), axis=0)
        g_pb.append(jnp.stack([sums[:hcols], sums[2 * hcols:]]))
        da = da + dot(dqkv, was[k, : 3 * hcols], NN)
    dx = dh + da * clip_slope(x, r0)
    inverse = h ^ jnp.arange(nh)
    bias_rows = jnp.stack(g_pb)[inverse].transpose(1, 0, 2).reshape(2, nh * hcols)
    off_rows = jnp.stack(g_bu)[inverse].reshape(nh * fcols // width, width)
    small = jnp.concatenate(
        [bias_rows, off_rows, jnp.stack([d_ga, d_gb, d_bo, d_ca, d_bd, d_cb])], axis=0
    )
    pad = -small.shape[0] % 8
    small = jnp.concatenate([small, jnp.zeros((pad, width), F32)], axis=0)
    grads = (jnp.stack(g_down), jnp.stack(g_up), jnp.stack(g_attn))
    out_rows = out.reshape(slots, part, width)
    dx_rows = dx.reshape(slots, part, width)
    if width % (16 * nd) == 0 and nd >= 4:
        settled = settle(grads, small, out_rows.astype(BF16), dx_rows.astype(BF16))
    else:
        settled = settle_plain(grads, small, out_rows.astype(BF16), dx_rows.astype(BF16), h)
    sums, small_sum, out_back, dx_back = settled
    index = h ^ jnp.arange(nh)
    hidden_out = jnp.concatenate([out_rows[:1], out_back[1:].astype(F32)])[index]
    input_grad = jnp.concatenate([dx_rows[:1], dx_back[1:].astype(F32)])[index]
    proj_grad = sums[2][:, : 3 * hcols].reshape(1, -1, 3, hcols).transpose(0, 2, 1, 3)
    out_grad = sums[2][:, 3 * hcols:].T[None]
    nb = nh * fcols // width
    return (
        hidden_out,
        input_grad,
        proj_grad,
        small_sum[None, 0:2],
        out_grad,
        sums[1][None],
        small_sum[2:2 + nb].reshape(1, nb * width),
        sums[0].T[None],
        small_sum[None, 2 + nb:4 + nb],
        small_sum[None, 4 + nb:8 + nb],
        jnp.stack([new0, new1, new2, new3])[None],
    )


def solution(mesh):
    in_specs = (
        P("dp", "head", None), P("dp", None), P("dp", None), P(),
        P(None, None, None, "head"), P(None, None, "head"), P(None, "head", None),
        P(None, None, "head"), P(None, "head"), P(None, "head", None), P(), P(),
        P("dp", "head", None),
    )
    out_specs = (
        P("dp", "head", None), P("dp", "head", None), P(None, None, "dp", "head"), P(),
        P(None, "head", "dp"), P(None, "dp", "head"), P(), P(None, "head", "dp"), P(), P(), P(),
    )
    return jax.shard_map(body, mesh=mesh, in_specs=in_specs, out_specs=out_specs, check_vma=False)
```

```python
import functools
import jax
import jax.numpy as jnp
from jax import lax
from jax.experimental import pallas as pl
from jax.experimental.pallas import tpu as pltpu
from jax.sharding import PartitionSpec as P

HEAD_DIM = 64
EPSILON = 1e-06
MASK_FILL = -1e30
DECAY = 0.9
ROOT = 0.3989422804014327
MESH = pl.DeviceIdType.MESH
BF16 = jnp.bfloat16
F32 = jnp.float32
ANY = pl.BlockSpec(memory_space=pl.ANY)
VM = pl.BlockSpec(memory_space=pltpu.VMEM)


def remote(src, dst, send_sem, recv_sem, where):
    return pltpu.make_async_remote_copy(
        src_ref=src, dst_ref=dst, send_sem=send_sem, recv_sem=recv_sem,
        device_id=where, device_id_type=MESH,
    )


def greet(peers):
    bar = pltpu.get_barrier_semaphore()
    for peer in peers:
        pl.semaphore_signal(bar, inc=1, device_id=peer, device_id_type=MESH)
    pl.semaphore_wait(bar, len(peers))


def settle_kernel(nz, rows, cols, grads, small, rows_out, rows_in,
                  sums, small_sum, rows_back_out, rows_back_in,
                  own1, got1, s1, got_a, got_b, s2a, s2b, got_c, got_d, s3, got4,
                  small_now, small_got, small_z,
                  local_sem, send_sem, recv_sem):
    g = lax.axis_index("dp")
    h = lax.axis_index("head")
    z = g // 2
    p = lax.rem(g, 2)
    half = cols // 2
    core, across, xside = (g, h ^ 1), (g, h ^ 2), (z * 2 + (1 - p), h)
    zpeers = [(lax.rem(z + d, nz) * 2 + p, h) for d in range(1, nz)]
    greet([core, across, (g, h ^ 3), xside] + zpeers)
    count = [0]
    sent = []

    def go(src, dst, where):
        i = count[0]
        count[0] += 1
        copy = remote(src, dst, send_sem.at[i], recv_sem.at[i], where)
        copy.start()
        sent.append(copy)
        return copy

    chunks = range(3)
    first = []
    own = []
    for c in chunks:
        first.append([go(grads[c].at[2 * j + 1], got1.at[c, j], core) for j in (0, 1)])
        pair = []
        for j in (0, 1):
            copy = pltpu.make_async_copy(grads[c].at[2 * j], own1.at[c, j], local_sem.at[2 * c + j])
            copy.start()
            pair.append(copy)
        own.append(pair)
    small_now[0] = small[...]
    small_copy = go(small_now.at[0], small_got.at[0], core)
    tail = []
    for src, dst in ((rows_out, rows_back_out), (rows_in, rows_back_in)):
        for k in (1, 2, 3):
            tail.append(go(src.at[k], dst.at[k], (g, h ^ k)))
    ya, xa = [], []
    for c in chunks:
        for copy in first[c]:
            copy.wait_recv()
        for copy in own[c]:
            copy.wait()

        def add1(i, carry):
            zz, xx = i // 2, lax.rem(i, 2)
            for j in (0, 1):
                s1[c, j, zz, xx] = (
                    own1[c, j, zz, xx].astype(F32) + got1[c, j, zz, xx].astype(F32)
                ).astype(BF16)
            return carry

        lax.fori_loop(0, 2 * nz, add1, 0)
        ya.append(go(s1.at[c, 1, :, :, :, pl.ds(0, half)], got_a.at[c], across))
        xa.append(go(s1.at[c, :, :, 1 - p, :, pl.ds(half, half)], got_b.at[c], xside))
        if c == 0:
            small_copy.wait_recv()
            small_now[1] = small_now[0] + small_got[0]
            small_copy = go(small_now.at[1], small_got.at[1], across)
    xb, yb = [], []
    for c in chunks:
        ya[c].wait_recv()

        def add2(i, carry):
            for xx in (0, 1):
                s2a[c, i, xx] = (
                    s1[c, 0, i, xx, :, :half].astype(F32) + got_a[c, i, xx].astype(F32)
                ).astype(BF16)
            return carry

        lax.fori_loop(0, nz, add2, 0)
        xb.append(go(s2a.at[c, :, 1 - p], got_c.at[c], xside))
        xa[c].wait_recv()

        def add3(i, carry):
            for j in (0, 1):
                s2b[c, j, i] = (
                    s1[c, j, i, p, :, half:].astype(F32) + got_b[c, j, i].astype(F32)
                ).astype(BF16)
            return carry

        lax.fori_loop(0, nz, add3, 0)
        yb.append(go(s2b.at[c, 1], got_d.at[c], across))
        if c == 0:
            small_copy.wait_recv()
            small_now[2] = small_now[1] + small_got[1]
            small_copy = go(small_now.at[2], small_got.at[2], xside)
    zs = []
    for c in chunks:
        xb[c].wait_recv()
        yb[c].wait_recv()

        def add4(i, carry):
            s3[c, i, :, :half] = (
                s2a[c, i, p].astype(F32) + got_c[c, i].astype(F32)
            ).astype(BF16)
            s3[c, i, :, half:] = (
                s2b[c, 0, i].astype(F32) + got_d[c, i].astype(F32)
            ).astype(BF16)
            return carry

        lax.fori_loop(0, nz, add4, 0)
        zs.append([
            go(s3.at[c, lax.rem(z + d, nz)], got4.at[c, d - 1], zpeers[d - 1]) for d in range(1, nz)
        ])
        if c == 0:
            small_copy.wait_recv()
            small_now[3] = small_now[2] + small_got[2]
            small_last = [
                go(small_now.at[3], small_z.at[d - 1], zpeers[d - 1]) for d in range(1, nz)
            ]
    for c in chunks:
        for copy in zs[c]:
            copy.wait_recv()
        total = s3[c, z].astype(F32)
        for d in range(1, nz):
            total = total + got4[c, d - 1].astype(F32)
        sums[c] = total
    for copy in small_last:
        copy.wait_recv()
    total = small_now[3]
    for d in range(1, nz):
        total = total + small_z[d - 1]
    small_sum[...] = total
    for copy in tail:
        copy.wait_recv()
    for copy in sent:
        copy.wait_send()


def settle(grads, small, rows_out, rows_in):
    nd = lax.axis_size("dp")
    nz = nd // 2
    nh, depth, cols = grads[0].shape
    rows = depth // nd
    half = cols // 2
    cut = [item.reshape(nh, nz, 2, rows, cols) for item in grads]
    copies = 3 * (2 + 2 + 2 + nz - 1) + 3 + (nz - 1) + 6

    def kernel(g0, g1, g2, *rest):
        settle_kernel(nz, rows, cols, (g0, g1, g2), *rest)

    return pl.pallas_call(
        kernel,
        out_shape=(
            jax.ShapeDtypeStruct((3, rows, cols), F32),
            jax.ShapeDtypeStruct(small.shape, F32),
            jax.ShapeDtypeStruct(rows_out.shape, rows_out.dtype),
            jax.ShapeDtypeStruct(rows_in.shape, rows_in.dtype),
        ),
        in_specs=[ANY] * 3 + [VM] + [ANY] * 2,
        out_specs=[VM, VM, ANY, ANY],
        scratch_shapes=[
            pltpu.VMEM((3, 2, nz, 2, rows, cols), BF16),
            pltpu.VMEM((3, 2, nz, 2, rows, cols), BF16),
            pltpu.VMEM((3, 2, nz, 2, rows, cols), BF16),
            pltpu.VMEM((3, nz, 2, rows, half), BF16),
            pltpu.VMEM((3, 2, nz, rows, half), BF16),
            pltpu.VMEM((3, nz, 2, rows, half), BF16),
            pltpu.VMEM((3, 2, nz, rows, half), BF16),
            pltpu.VMEM((3, nz, rows, half), BF16),
            pltpu.VMEM((3, nz, rows, half), BF16),
            pltpu.VMEM((3, nz, rows, cols), BF16),
            pltpu.VMEM((3, nz - 1, rows, cols), BF16),
            pltpu.VMEM((4,) + small.shape, F32),
            pltpu.VMEM((3,) + small.shape, F32),
            pltpu.VMEM((nz - 1,) + small.shape, F32),
            pltpu.SemaphoreType.DMA((6,)),
            pltpu.SemaphoreType.DMA((copies,)),
            pltpu.SemaphoreType.DMA((copies,)),
        ],
        compiler_params=pltpu.CompilerParams(
            collective_id=1, has_side_effects=True, vmem_limit_bytes=60 * 1024 * 1024
        ),
    )(*cut, small, rows_out, rows_in)


def settle_plain(grads, small, rows_out, rows_in, head_pos):
    nh, depth, cols = grads[0].shape
    stacked = jnp.stack(grads)
    order = head_pos ^ jnp.arange(nh)
    stacked = stacked[:, order].astype(F32)
    part = lax.psum_scatter(stacked, "head", scatter_dimension=1, tiled=True)[:, 0]
    sums = lax.psum_scatter(part, "dp", scatter_dimension=1, tiled=True)

    def swap(rows):
        return jnp.stack([rows[0]] + [
            lax.ppermute(rows[k], "head", [(i, i ^ k) for i in range(nh)]) for k in range(1, nh)
        ])

    return sums, lax.psum(small, ("dp", "head")), swap(rows_out), swap(rows_in)


NN = ((1,), (0,))
NT = ((1,), (1,))
TN = ((0,), (0,))
LIMIT = 60 * 1024 * 1024


def dot(a, b, dims):
    return lax.dot_general(a, b, (dims, ((), ())), preferred_element_type=F32)


def tiles(count, rows, step):
    def one(i, carry):
        step(pl.ds(pl.multiple_of(i * rows, rows), rows))
        return carry

    lax.fori_loop(0, count // rows, one, 0)


def norm_parts(z):
    centred = z - jnp.mean(z, axis=-1, keepdims=True)
    inv = lax.rsqrt(jnp.mean(centred * centred, axis=-1, keepdims=True) + EPSILON)
    return centred * inv, inv


def norm_back(dn, n, inv):
    return (dn - jnp.mean(dn, axis=-1, keepdims=True)
            - n * jnp.mean(dn * n, axis=-1, keepdims=True)) * inv


def span_top(values, live):
    return jnp.max(jnp.abs(values) * live, axis=0, keepdims=True)


def lane_top(row):
    return jnp.max(row, axis=1, keepdims=True)


class Wires:
    def __init__(self, send_sem, recv_sem):
        self.send_sem, self.recv_sem = send_sem, recv_sem
        self.sent = []

    def go(self, src, dst, where):
        i = len(self.sent)
        copy = remote(src, dst, self.send_sem.at[i], self.recv_sem.at[i], where)
        copy.start()
        self.sent.append(copy)
        return copy

    def finish(self):
        for copy in self.sent:
            copy.wait_send()


class Spool:
    def __init__(self, sem):
        self.sem = sem
        self.count = 0
        self.open = []

    def go(self, src, dst):
        copy = pltpu.make_async_copy(src, dst, self.sem.at[self.count])
        self.count += 1
        copy.start()
        self.open.append(copy)
        return copy

    def wait(self, copy):
        copy.wait()
        self.open.remove(copy)

    def finish(self):
        for copy in self.open:
            copy.wait()


def own_micro(order_s, h, count):
    m_own = jnp.int32(0)
    for m in range(count):
        m_own = m_own + jnp.where(order_s[0, m] == h, jnp.int32(m), jnp.int32(0))
    return m_own


def range_of(start, tops, m_own, count):
    now = jnp.full((1, 1), start, F32)
    own = now
    for m in range(1, count):
        now = DECAY * now + (1.0 - DECAY) * tops[:, m - 1: m]
        own = jnp.where(m_own == m, now, own)
    return own


def front_kernel(nd, nh, part, len_s, order_s, range_s, x_in, dy_in, pw_ref, ow_ref, wu_in, wd_in, pb_ref, ub_ref,
                 gain_ref, shift_ref,
                 x_o, dy_o, wa_o, wu_o, wd_o, a_o, qkv_o, c_o, cq_o, lse_o, n1_o, inv1_o, y1_o, b_o, g_o, gp_o,
                 tops_o, own_o,
                 xl, xs, wa, wu, bias, a_ref, qkv, c_ref, cq, lse, lse_t, n1, inv1, y1, b_ref, g_ref, gp_ref,
                 acc, live, mask, cand, slots,
                 spool_sem, send_sem, recv_sem, top_send, top_recv):
    g = lax.axis_index("dp")
    h = lax.axis_index("head")
    n = nd * nh
    hc = ow_ref.shape[0]
    width = ow_ref.shape[1]
    micro = 4
    lanes = lax.broadcasted_iota(jnp.int32, (1, 128), 1)

    def peer(d):
        return (lax.rem(g + d // nh, nd), lax.rem(h + lax.rem(d, nh), nh))

    bar = pltpu.get_barrier_semaphore()

    def hello(d, carry):
        pl.semaphore_signal(bar, inc=1, device_id=peer(d), device_id_type=MESH)
        return carry

    lax.fori_loop(1, n, hello, 0)
    spool = Spool(spool_sem)
    wires = Wires(send_sem, recv_sem)
    load_x = spool.go(x_in, xl)
    own_x = spool.go(x_in.at[h], xs.at[0])
    own_wu = spool.go(wu_in, wu.at[0])
    spool.go(wd_in, wd_o.at[0])
    spool.go(dy_in.at[h], dy_o.at[0])

    m_own = own_micro(order_s, h, micro)
    length = len_s[0, h]
    for k in range(nh):
        start = (h ^ k) * part
        rows = start + lax.broadcasted_iota(jnp.int32, (part, 1), 0)
        live[k * part:(k + 1) * part, :] = jnp.where(rows < length, 1.0, 0.0)
        cols = start + lax.broadcasted_iota(jnp.int32, (1, part), 1)
        mask[:, k * part:(k + 1) * part] = jnp.where(cols < length, 0.0, MASK_FILL)
    bias[0] = jnp.zeros_like(bias[0])
    bias[0, 0:1, :hc] = pb_ref[0:1, :].astype(F32)
    bias[0, 0:1, 2 * hc:3 * hc] = pb_ref[1:2, :].astype(F32)
    bias[0, 1:2, :] = ub_ref[...].astype(F32)
    for i in range(3):
        wa[0, i * hc:(i + 1) * hc, :] = pw_ref[i].astype(F32).T.astype(BF16)
    wa[0, 3 * hc:, :] = ow_ref[...]

    def exchange_start(stage, row):
        cand[stage] = row

        def send(d, carry):
            remote(cand.at[stage], slots.at[stage, d - 1], top_send.at[stage], top_recv.at[stage], peer(d)).start()
            return carry

        lax.fori_loop(1, n, send, 0)

    def exchange_end(stage):
        pltpu.make_async_copy(slots.at[stage], slots.at[stage], top_recv.at[stage]).wait()
        top = jnp.maximum(cand[stage], jnp.max(slots[stage], axis=0))
        tops_o[stage:stage + 1, :] = top
        own = range_of(range_s[0, stage], top, m_own, micro)
        own_o[stage:stage + 1, :] = jnp.broadcast_to(own, (1, 128))
        return own

    def own_lane(value):
        return jnp.where(lanes == m_own, value, 0.0)

    spool.wait(load_x)
    row0 = jnp.zeros((1, 128), F32)
    local_rows = h * part + lax.broadcasted_iota(jnp.int32, (part, 1), 0)
    for s in range(micro):
        lit = jnp.where(local_rows < len_s[0, s], 1.0, 0.0)
        top = lane_top(span_top(xl[s].astype(F32), lit))
        row0 = jnp.maximum(row0, jnp.where(lanes == own_micro(order_s, s, micro), top, 0.0))

    pl.semaphore_wait(bar, n - 1)
    quarter = width // 4
    sibling, across = (g, h ^ 1), (g, h ^ 2)

    def part_of(q):
        return pl.ds(pl.multiple_of(q * quarter, quarter), quarter)

    mine = lax.rem(g, 4)
    x_wait = [wires.go(x_in.at[h ^ k], xs.at[k], (g, h ^ k)) for k in (2, 3, 1)]
    exchange_start(0, row0)
    bias_wait = [wires.go(bias.at[0], bias.at[k], (g, h ^ k)) for k in (1, 2, 3)]

    class Weight:
        def __init__(self, own, land):
            self.own, self.land = own, land

        def first(self):
            self.core = wires.go(self.own, self.land.at[1], sibling)
            self.leap = wires.go(self.own.at[part_of(mine), :], self.land.at[2, part_of(mine), :], across)

        def second(self):
            self.leap.wait_recv()
            here = self.land.at[2, part_of(mine), :]
            self.round = [
                (wires.go(here, self.land.at[2, part_of(mine), :], (g ^ e, h)), mine ^ e) for e in (1, 2, 3)
            ]
            self.last = [wires.go(here, self.land.at[3, part_of(mine), :], sibling)]

        def third(self):
            for copy, q in self.round:
                copy.wait_recv()
                self.last.append(
                    wires.go(self.land.at[2, part_of(q), :], self.land.at[3, part_of(q), :], sibling))

        def fourth(self):
            for copy in self.last:
                copy.wait_recv()

    way_a = Weight(wa.at[0], wa)
    way_u = Weight(wu.at[0], wu)
    way_d = Weight(wd_in, wd_o)
    way_a.first()
    r0 = exchange_end(0)
    spool.wait(own_x)
    for copy in x_wait:
        copy.wait_recv()
    ri0 = 1.0 / r0
    for k in range(nh):
        a_ref[k * part:(k + 1) * part, :] = (r0 * jnp.tanh(xs[k].astype(F32) * ri0)).astype(BF16)
    spool.go(xs, x_o)
    spool.go(a_ref, a_o)
    for copy in bias_wait:
        copy.wait_recv()

    def block(k):
        qkv[k] = (dot(a_ref[...], wa[k, : 3 * hc, :], NT) + bias[k, 0:1, : 3 * hc]).astype(BF16)
        for j in range(hc // HEAD_DIM):
            lo = j * HEAD_DIM
            keys = qkv[k, :, hc + lo: hc + lo + HEAD_DIM]
            vals = qkv[k, :, 2 * hc + lo: 2 * hc + lo + HEAD_DIM]
            q = qkv[k, :, lo: lo + HEAD_DIM] * BF16(HEAD_DIM ** -0.5)
            s = dot(q, keys, NT) + mask[...]
            top = jnp.max(s, axis=1, keepdims=True)
            e = jnp.exp(s - top)
            den = jnp.sum(e, axis=1, keepdims=True)
            p = (e * (1.0 / den)).astype(BF16)
            c_ref[k, :, lo: lo + HEAD_DIM] = dot(p, vals, NN)
            at = k * 8 + j
            lse[:, at: at + 1] = top + jnp.log(den)
        spool.go(qkv.at[k], qkv_o.at[k])
        spool.go(c_ref.at[k], c_o.at[k])
        return span_top(c_ref[k], live[...])

    lse[...] = jnp.zeros_like(lse)
    best = block(0)
    way_a.core.wait_recv()
    best = jnp.maximum(best, block(1))
    spool.wait(own_wu)
    way_a.second()
    way_u.first()
    way_a.third()
    best = jnp.maximum(best, block(2))
    way_a.fourth()
    best = jnp.maximum(best, block(3))
    exchange_start(1, own_lane(lane_top(best)))
    turned = lse[...].T
    for k in range(nh):
        lse_t[k] = turned[k * 8:(k + 1) * 8, :]
    spool.go(lse_t, lse_o)
    spool.go(wa, wa_o)
    way_u.second()
    way_d.first()
    r1 = exchange_end(1)
    ri1 = 1.0 / r1
    for k in range(nh):
        cq[k] = (r1 * jnp.tanh(c_ref[k] * ri1)).astype(BF16)
        o1 = dot(cq[k], wa[k, 3 * hc:, :], NN)
        if k == 0:
            acc[...] = o1
        else:
            acc[...] += o1
    spool.go(cq, cq_o)
    bo, ca = shift_ref[0:1, :].astype(F32), shift_ref[1:2, :].astype(F32)
    ga = gain_ref[0:1, :].astype(F32)

    def norm_step(i, best):
        rows = pl.ds(pl.multiple_of(i * part, part), part)
        nn, inv = norm_parts(xs[i].astype(F32) + (acc[rows, :] + bo))
        n1[rows, :] = nn
        inv1[rows, :] = inv
        y = nn * ga + ca
        y1[rows, :] = y
        return jnp.maximum(best, span_top(y, live[rows, :]))

    best = lax.fori_loop(0, nh, norm_step, jnp.zeros((1, width), F32))
    exchange_start(2, own_lane(lane_top(best)))
    for src, dst in ((n1, n1_o), (inv1, inv1_o), (y1, y1_o)):
        spool.go(src, dst)
    dy_wait = [wires.go(dy_in.at[h ^ k], dy_o.at[k], (g, h ^ k)) for k in (2, 3, 1)]
    way_u.third()
    r2 = exchange_end(2)
    b_ref[...] = (r2 * jnp.tanh(y1[...] * (1.0 / r2))).astype(BF16)
    spool.go(b_ref, b_o)

    def units(k):
        f = dot(b_ref[...], wu[k], NN) + bias[k, 1:2, :]
        cdf = 0.5 * (1.0 + lax.erf(f * (0.5 ** 0.5)))
        gg = f * cdf
        g_ref[k] = gg
        gp_ref[k] = cdf + f * (jnp.exp(-0.5 * f * f) * ROOT)
        spool.go(g_ref.at[k], g_o.at[k])
        spool.go(gp_ref.at[k], gp_o.at[k])
        return span_top(gg, live[...])

    best = units(0)
    way_u.core.wait_recv()
    best = jnp.maximum(best, units(1))
    way_d.second()
    best = jnp.maximum(best, units(2))
    way_u.fourth()
    best = jnp.maximum(best, units(3))
    exchange_start(3, own_lane(lane_top(best)))
    spool.go(wu, wu_o)
    way_d.third()
    exchange_end(3)
    way_d.core.wait_recv()
    way_d.fourth()
    for copy in dy_wait:
        copy.wait_recv()
    for stage in range(4):
        pltpu.make_async_copy(slots.at[stage], slots.at[stage], top_send.at[stage]).wait()
    tops_o[4:8, :] = jnp.zeros((4, 128), F32)
    own_o[4:8, :] = jnp.zeros((4, 128), F32)
    wires.finish()
    spool.finish()


def front(lengths, order, ranges, x_in, dy_in, pw, ow, wu, wd, pb, ub, gains, shifts):
    nd, nh = lax.axis_size("dp"), lax.axis_size("head")
    slots, part, width = x_in.shape
    count = slots * part
    hc, fc = ow.shape[0], wu.shape[1]

    def shape(*dims, kind=F32):
        return jax.ShapeDtypeStruct(dims, kind)

    outs = (
        shape(slots, part, width, kind=BF16), shape(slots, part, width, kind=BF16),
        shape(nh, 4 * hc, width, kind=BF16), shape(nh, width, fc, kind=BF16), shape(nh, fc, width, kind=BF16),
        shape(count, width, kind=BF16), shape(nh, count, 3 * hc, kind=BF16), shape(nh, count, hc),
        shape(nh, count, hc, kind=BF16), shape(nh, 8, count), shape(count, width), shape(count, 1),
        shape(count, width), shape(count, width, kind=BF16), shape(nh, count, fc), shape(nh, count, fc),
        shape(8, 128), shape(8, 128),
    )
    scratch = [pltpu.VMEM(o.shape, o.dtype) for o in (
        outs[0], outs[0], outs[2], outs[3], shape(nh, 8, fc), outs[5], outs[6], outs[7], outs[8], shape(count, 128),
        outs[9], outs[10], outs[11], outs[12], outs[13], outs[14], outs[15], shape(count, width),
        shape(count, 1), shape(1, count), shape(4, 1, 128), shape(4, nd * nh - 1, 1, 128))]
    smem = pl.BlockSpec(memory_space=pltpu.SMEM)
    return pl.pallas_call(
        functools.partial(front_kernel, nd, nh, part),
        out_shape=outs,
        in_specs=[smem] * 3 + [ANY] * 2 + [VM] * 2 + [ANY] * 2 + [VM] * 4,
        out_specs=[ANY] * 16 + [VM] * 2,
        scratch_shapes=scratch + [
            pltpu.SemaphoreType.DMA((40,)), pltpu.SemaphoreType.DMA((40,)), pltpu.SemaphoreType.DMA((40,)),
            pltpu.SemaphoreType.DMA((4,)), pltpu.SemaphoreType.DMA((4,)),
        ],
        compiler_params=pltpu.CompilerParams(collective_id=0, has_side_effects=True, vmem_limit_bytes=LIMIT),
    )(lengths, order, ranges, x_in, dy_in, pw, ow, wu, wd, pb, ub, gains, shifts)


def turn_kernel(g_hbm, gp_hbm, wd_hbm, wu_hbm, y1_ref, b_ref, dy_ref, n1_ref, inv1_ref, vec_ref,
                r2_ref, r3_ref,
                out_ref, dh_ref, dhb_ref, gdown_hbm, gup_hbm, sums_ref, gbu_ref,
                g_ref, gp_ref, wd_ref, wu_ref, gq_ref, acc_ref, dz_ref, dzb_ref, tr_ref,
                df_ref, stage, sem, out_sem):
    nh, count, cols = g_ref.shape
    part = dy_ref.shape[1]
    loads = ((g_hbm, g_ref), (gp_hbm, gp_ref), (wd_hbm, wd_ref), (wu_hbm, wu_ref))

    def load(i, k):
        return pltpu.make_async_copy(loads[i][0].at[k], loads[i][1].at[k], sem.at[i, k])

    for k in range(nh):
        for i in (0, 1, 2):
            load(i, k).start()
    for k in range(nh):
        load(3, k).start()
    r3 = r3_ref[...]
    ri3 = 1.0 / r3
    acc_ref[...] = jnp.zeros_like(acc_ref)

    def down(k, carry):
        load(0, k).wait()
        load(1, k).wait()

        def one(rows):
            t = jnp.tanh(g_ref[k, rows, :] * ri3)
            gq_ref[k, rows, :] = (r3 * t).astype(BF16)
            gp_ref[k, rows, :] = gp_ref[k, rows, :] * (1.0 - t * t)

        tiles(count, 64, one)
        load(2, k).wait()
        acc_ref[...] += dot(gq_ref[k], wd_ref[k], NN)
        return carry

    lax.fori_loop(0, nh, down, 0)
    wide = acc_ref.shape[1]

    def norm_two(i, carry):
        s_gb, s_cb, s_bd = carry
        rows = pl.ds(pl.multiple_of(i * part, part), part)
        n, inv = norm_parts(y1_ref[rows, :] + (acc_ref[rows, :] + vec_ref[4:5, :]))
        out_ref[rows, :] = n * vec_ref[1:2, :] + vec_ref[5:6, :]
        dy = dy_ref[i].astype(F32)
        dz = norm_back(dy * vec_ref[1:2, :], n, inv)
        dz_ref[rows, :] = dz
        dzb_ref[rows, :] = dz.astype(BF16)
        tr_ref[:, rows] = dz.T.astype(BF16)
        return (s_gb + jnp.sum(dy * n, axis=0, keepdims=True),
                s_cb + jnp.sum(dy, axis=0, keepdims=True),
                s_bd + jnp.sum(dz, axis=0, keepdims=True))

    zero = jnp.zeros((1, wide), F32)
    s_gb, s_cb, s_bd = lax.fori_loop(0, count // part, norm_two, (zero, zero, zero))

    def put(slot, dst):
        return pltpu.make_async_copy(stage.at[slot], dst, out_sem.at[slot])

    def grad_down(k, carry):
        slot = lax.rem(k, 2)

        @pl.when(k >= 2)
        def _():
            put(slot, gdown_hbm.at[k]).wait()

        stage[slot] = dot(tr_ref[...], gq_ref[k], NN).astype(BF16)
        put(slot, gdown_hbm.at[k]).start()
        return carry

    lax.fori_loop(0, nh, grad_down, 0)
    acc_ref[...] = jnp.zeros_like(acc_ref)
    def turn_b(rows):
        tr_ref[:, rows] = b_ref[rows, :].astype(F32).T.astype(BF16)

    tiles(count, part, turn_b)

    def units(k, carry):
        slot = lax.rem(k, 2)
        g_ref[k] = dot(dzb_ref[...], wd_ref[k], NT)

        def one(i, total):
            rows = pl.ds(pl.multiple_of(i * 64, 64), 64)
            df = (g_ref[k, rows, :] * gp_ref[k, rows, :]).astype(BF16)
            df_ref[rows, :] = df
            return total + jnp.sum(df.astype(F32), axis=0, keepdims=True)

        gbu_ref[k] = lax.fori_loop(0, count // 64, one, jnp.zeros((1, cols), F32))
        put(slot, gup_hbm.at[k]).wait()
        stage[slot] = dot(tr_ref[...], df_ref[...], NN).astype(BF16)
        put(slot, gup_hbm.at[k]).start()
        load(3, k).wait()
        acc_ref[...] += dot(df_ref[...], wu_ref[k], NT)
        return carry

    lax.fori_loop(0, nh, units, 0)
    r2 = r2_ref[...]
    ri2 = 1.0 / r2

    def norm_one(i, carry):
        s_ga, s_ca, s_bo = carry
        rows = pl.ds(pl.multiple_of(i * part, part), part)
        t = jnp.tanh(y1_ref[rows, :] * ri2)
        dy1 = dz_ref[rows, :] + acc_ref[rows, :] * (1.0 - t * t)
        n = n1_ref[rows, :]
        dh = norm_back(dy1 * vec_ref[0:1, :], n, inv1_ref[rows, :])
        dh_ref[rows, :] = dh
        dhb_ref[rows, :] = dh.astype(BF16)
        return (s_ga + jnp.sum(dy1 * n, axis=0, keepdims=True),
                s_ca + jnp.sum(dy1, axis=0, keepdims=True),
                s_bo + jnp.sum(dh, axis=0, keepdims=True))

    s_ga, s_ca, s_bo = lax.fori_loop(0, count // part, norm_one, (zero, zero, zero))
    for i, row in enumerate((s_ga, s_gb, s_bo, s_ca, s_bd, s_cb)):
        sums_ref[i: i + 1, :] = row
    sums_ref[6:8, :] = jnp.zeros((2, wide), F32)
    for slot in (0, 1):
        put(slot, gup_hbm.at[nh - 2 + slot]).wait()


def attend_back(k, a_t, dhb_ref, dhb_t, w, c, cq, qkv_ref, lse_t, live_col, r1, dc_ref, kt_ref, dqt_ref, dqkv_ref):
    hc = cq.shape[1]
    count = dhb_ref.shape[0]
    ri = 1.0 / r1
    u = dot(dhb_ref[...], w[3 * hc:, :], NT)
    t = jnp.tanh(c[...] * ri)
    dc_ref[...] = (u * (1.0 - t * t)).astype(BF16)
    kt_ref[...] = qkv_ref[k, :, hc: 2 * hc].astype(F32).T.astype(BF16)
    scale = HEAD_DIM ** -0.5
    for j in range(hc // HEAD_DIM):
        lo = j * HEAD_DIM
        keys = qkv_ref[k, :, hc + lo: hc + lo + HEAD_DIM]
        vals = qkv_ref[k, :, 2 * hc + lo: 2 * hc + lo + HEAD_DIM]
        dk = dv = None
        for q0 in range(0, count, 512):
            rows = slice(q0, q0 + 512)
            q = qkv_ref[k, rows, lo: lo + HEAD_DIM] * BF16(scale)
            dc = dc_ref[rows, lo: lo + HEAD_DIM]
            s = dot(keys, q, NT)
            p = jnp.where(live_col > 0.0, jnp.exp(s - lse_t[j: j + 1, rows]), 0.0)
            dp = dot(vals, dc, NT)
            pd = p * dp
            delta = jnp.sum(pd, axis=0, keepdims=True)
            ds = (pd - p * delta).astype(BF16)
            dv_part = dot(p.astype(BF16), dc, NN)
            dk_part = dot(ds, q, NN)
            dv = dv_part if dv is None else dv + dv_part
            dk = dk_part if dk is None else dk + dk_part
            dqt_ref[lo: lo + HEAD_DIM, rows] = dot(kt_ref[lo: lo + HEAD_DIM, :], ds, NN) * scale
        dqkv_ref[:, hc + lo: hc + lo + HEAD_DIM] = dk.astype(BF16)
        dqkv_ref[:, 2 * hc + lo: 2 * hc + lo + HEAD_DIM] = dv.astype(BF16)
    dqkv_ref[:, :hc] = dqt_ref[...].T.astype(BF16)


def back_kernel(a_ref, dhb_ref, dh_ref, x_ref, wa_ref, c_ref, cq_ref, qkv_ref, lse_ref, live_ref, r0_ref, r1_ref,
                dx_ref, ga_hbm, gpb_ref, a_t, dhb_t, dc_ref, kt_ref, dqt_ref, dqkv_ref, acc_ref, stage, out_sem):
    nh, count, hc = c_ref.shape
    part = x_ref.shape[1]

    def turn(rows):
        a_t[:, rows] = a_ref[rows, :].astype(F32).T.astype(BF16)
        dhb_t[:, rows] = dhb_ref[rows, :].astype(F32).T.astype(BF16)

    tiles(count, part, turn)
    acc_ref[...] = jnp.zeros_like(acc_ref)

    def put(slot, k):
        return pltpu.make_async_copy(stage.at[slot], ga_hbm.at[k], out_sem.at[slot])

    def one(k, carry):
        slot = lax.rem(k, 2)
        lse_t = lse_ref[k]
        attend_back(k, a_t, dhb_ref, dhb_t, wa_ref.at[k], c_ref.at[k], cq_ref.at[k], qkv_ref, lse_t,
                    live_ref[...], r1_ref[...], dc_ref, kt_ref, dqt_ref, dqkv_ref)
        gpb_ref[k] = jnp.sum(dqkv_ref[...].astype(F32), axis=0, keepdims=True)

        @pl.when(k >= 2)
        def _():
            put(slot, k).wait()

        stage[slot, :, : 3 * hc] = dot(a_t[...], dqkv_ref[...], NN).astype(BF16)
        stage[slot, :, 3 * hc:] = dot(dhb_t[...], cq_ref[k], NN).astype(BF16)
        put(slot, k).start()
        acc_ref[...] += dot(dqkv_ref[...], wa_ref[k, : 3 * hc, :], NN)
        return carry

    lax.fori_loop(0, nh, one, 0)
    r = r0_ref[...]
    ri = 1.0 / r

    def last(i, carry):
        rows = pl.ds(pl.multiple_of(i * part, part), part)
        t = jnp.tanh(x_ref[i].astype(F32) * ri)
        dx_ref[rows, :] = dh_ref[rows, :] + acc_ref[rows, :] * (1.0 - t * t)
        return carry

    lax.fori_loop(0, nh, last, 0)
    for slot in (0, 1):
        put(slot, nh - 2 + slot).wait()


def local(kernel, outs, out_specs, in_specs, scratch, *args):
    return pl.pallas_call(
        kernel,
        out_shape=outs,
        in_specs=in_specs,
        out_specs=out_specs,
        scratch_shapes=scratch,
        compiler_params=pltpu.CompilerParams(vmem_limit_bytes=LIMIT),
    )(*args)


def body(hidden_in, seq_lengths, batch_order, clip_ranges, proj_weight, proj_bias, out_weight,
         up_weight, up_bias, down_weight, norm_gains, out_biases, cotangent):
    nd, nh = lax.axis_size("dp"), lax.axis_size("head")
    h = lax.axis_index("head")
    slots, part, width = hidden_in.shape
    hcols = proj_bias.shape[2]
    fcols = up_bias.shape[1]
    count = slots * part
    (xs, dys, was, wus, wds, a, qkv, c, cq, lse_t, n1, inv1, y1, b, g, gp, tops, owns) = front(
        seq_lengths, batch_order, clip_ranges, hidden_in, cotangent, proj_weight[0], out_weight[0], up_weight[0],
        down_weight[0], proj_bias[0], up_bias, norm_gains[0], out_biases[0])
    blocks = h ^ jnp.arange(nh, dtype=jnp.int32)
    pos = (blocks[:, None] * part + jnp.arange(part, dtype=jnp.int32)[None, :]).reshape(-1)
    live_col = (pos < seq_lengths[0, h]).astype(F32)[:, None]
    r0, r1, r2, r3 = [owns[i: i + 1, 0:1] for i in range(4)]
    now = clip_ranges
    for m in range(slots):
        now = DECAY * now + (1.0 - DECAY) * tops[None, :4, m]

    def shape(*dims, kind=F32):
        return jax.ShapeDtypeStruct(dims, kind)

    gains = norm_gains[0].astype(F32)
    shifts = out_biases[0].astype(F32)
    vec = jnp.concatenate([gains, shifts, jnp.zeros((2, width), F32)], axis=0)
    out, dh, dhb, g_down, g_up, norm_sums, g_bu = local(
        turn_kernel,
        (shape(count, width), shape(count, width), shape(count, width, kind=BF16),
         shape(nh, width, fcols, kind=BF16), shape(nh, width, fcols, kind=BF16), shape(8, width), shape(nh, 1, fcols)),
        [VM, VM, VM, ANY, ANY, VM, VM], [ANY] * 4 + [VM] * 8,
        [pltpu.VMEM((nh, count, fcols), F32), pltpu.VMEM((nh, count, fcols), F32),
         pltpu.VMEM(wds.shape, BF16), pltpu.VMEM(wus.shape, BF16), pltpu.VMEM((nh, count, fcols), BF16),
         pltpu.VMEM((count, width), F32), pltpu.VMEM((count, width), F32), pltpu.VMEM((count, width), BF16),
         pltpu.VMEM((width, count), BF16), pltpu.VMEM((count, fcols), BF16), pltpu.VMEM((2, width, fcols), BF16),
         pltpu.SemaphoreType.DMA((4, nh)), pltpu.SemaphoreType.DMA((2,))],
        g, gp, wds, wus, y1, b, dys, n1, inv1, vec, r2, r3)
    dx, g_attn, g_pb = local(
        back_kernel,
        (shape(count, width), shape(nh, width, 4 * hcols, kind=BF16), shape(nh, 1, 3 * hcols)),
        [VM, ANY, VM], [VM] * 12,
        [pltpu.VMEM((width, count), BF16), pltpu.VMEM((width, count), BF16), pltpu.VMEM((count, hcols), BF16),
         pltpu.VMEM((hcols, count), BF16), pltpu.VMEM((hcols, count), F32), pltpu.VMEM((count, 3 * hcols), BF16),
         pltpu.VMEM((count, width), F32), pltpu.VMEM((2, width, 4 * hcols), BF16), pltpu.SemaphoreType.DMA((2,))],
        a, dhb, dh, xs, was, c, cq, qkv, lse_t, live_col, r0, r1)
    g_pb = jnp.stack([g_pb[:, 0, :hcols], g_pb[:, 0, 2 * hcols:]], axis=1)
    g_bu = g_bu[:, 0]
    inverse = h ^ jnp.arange(nh)
    bias_rows = g_pb[inverse].transpose(1, 0, 2).reshape(2, nh * hcols)
    off_rows = g_bu[inverse].reshape(nh * fcols // width, width)
    small = jnp.concatenate(
        [bias_rows, off_rows, norm_sums[:6]], axis=0
    )
    pad = -small.shape[0] % 8
    small = jnp.concatenate([small, jnp.zeros((pad, width), F32)], axis=0)
    grads = (g_down, g_up, g_attn)
    out_rows = out.reshape(slots, part, width)
    dx_rows = dx.reshape(slots, part, width)
    if width % (16 * nd) == 0 and nd >= 4:
        settled = settle(grads, small, out_rows.astype(BF16), dx_rows.astype(BF16))
    else:
        settled = settle_plain(grads, small, out_rows.astype(BF16), dx_rows.astype(BF16), h)
    sums, small_sum, out_back, dx_back = settled
    index = h ^ jnp.arange(nh)
    hidden_out = jnp.concatenate([out_rows[:1], out_back[1:].astype(F32)])[index]
    input_grad = jnp.concatenate([dx_rows[:1], dx_back[1:].astype(F32)])[index]
    proj_grad = sums[2][:, : 3 * hcols].reshape(1, -1, 3, hcols).transpose(0, 2, 1, 3)
    out_grad = sums[2][:, 3 * hcols:].T[None]
    nb = nh * fcols // width
    return (
        hidden_out,
        input_grad,
        proj_grad,
        small_sum[None, 0:2],
        out_grad,
        sums[1][None],
        small_sum[2:2 + nb].reshape(1, nb * width),
        sums[0].T[None],
        small_sum[None, 2 + nb:4 + nb],
        small_sum[None, 4 + nb:8 + nb],
        now,
    )


def solution(mesh):
    in_specs = (
        P("dp", "head", None), P("dp", None), P("dp", None), P(),
        P(None, None, None, "head"), P(None, None, "head"), P(None, "head", None),
        P(None, None, "head"), P(None, "head"), P(None, "head", None), P(), P(),
        P("dp", "head", None),
    )
    out_specs = (
        P("dp", "head", None), P("dp", "head", None), P(None, None, "dp", "head"), P(),
        P(None, "head", "dp"), P(None, "dp", "head"), P(), P(None, "head", "dp"), P(), P(), P(),
    )
    return jax.shard_map(body, mesh=mesh, in_specs=in_specs, out_specs=out_specs, check_vma=False)
```

```python
import functools
import jax
import jax.numpy as jnp
from jax import lax
from jax.experimental import pallas as pl
from jax.experimental.pallas import tpu as pltpu
from jax.sharding import PartitionSpec as P

HEAD_DIM = 64
EPSILON = 1e-06
MASK_FILL = -1e30
DECAY = 0.9
ROOT = 0.3989422804014327
MESH = pl.DeviceIdType.MESH
BF16 = jnp.bfloat16
F32 = jnp.float32
ANY = pl.BlockSpec(memory_space=pl.ANY)
VM = pl.BlockSpec(memory_space=pltpu.VMEM)


def remote(src, dst, send_sem, recv_sem, where):
    return pltpu.make_async_remote_copy(
        src_ref=src, dst_ref=dst, send_sem=send_sem, recv_sem=recv_sem,
        device_id=where, device_id_type=MESH,
    )


def greet(peers):
    bar = pltpu.get_barrier_semaphore()
    for peer in peers:
        pl.semaphore_signal(bar, inc=1, device_id=peer, device_id_type=MESH)
    pl.semaphore_wait(bar, len(peers))


def settle_plain(grads, small, head_pos):
    order = head_pos ^ jnp.arange(grads.shape[1])
    part = lax.psum_scatter(grads[:, order].astype(F32), "head", scatter_dimension=1, tiled=True)[:, 0]
    return lax.psum_scatter(part, "dp", scatter_dimension=1, tiled=True), lax.psum(small, ("dp", "head"))


NN = ((1,), (0,))
NT = ((1,), (1,))
TN = ((0,), (0,))
LIMIT = 60 * 1024 * 1024
REAR_LIMIT = 63 * 1024 * 1024


def dot(a, b, dims):
    return lax.dot_general(a, b, (dims, ((), ())), preferred_element_type=F32)


def tiles(count, rows, step):
    def one(i, carry):
        step(pl.ds(pl.multiple_of(i * rows, rows), rows))
        return carry

    lax.fori_loop(0, count // rows, one, 0)


def norm_parts(z):
    centred = z - jnp.mean(z, axis=-1, keepdims=True)
    inv = lax.rsqrt(jnp.mean(centred * centred, axis=-1, keepdims=True) + EPSILON)
    return centred * inv, inv


def norm_back(dn, n, inv):
    return (dn - jnp.mean(dn, axis=-1, keepdims=True)
            - n * jnp.mean(dn * n, axis=-1, keepdims=True)) * inv


def span_top(values, live):
    return jnp.max(jnp.abs(values) * live, axis=0, keepdims=True)


def lane_top(row):
    return jnp.max(row, axis=1, keepdims=True)


class Wires:
    def __init__(self, send_sem, recv_sem):
        self.send_sem, self.recv_sem = send_sem, recv_sem
        self.sent = []
        self.count = 0

    def go(self, src, dst, where):
        i = self.count
        self.count += 1
        copy = remote(src, dst, self.send_sem.at[i], self.recv_sem.at[i], where)
        copy.start()
        self.sent.append(copy)
        return copy

    def finish(self):
        for copy in self.sent:
            copy.wait_send()


class Spool:
    def __init__(self, sem):
        self.sem = sem
        self.count = 0
        self.open = []

    def go(self, src, dst):
        copy = pltpu.make_async_copy(src, dst, self.sem.at[self.count])
        self.count += 1
        copy.start()
        self.open.append(copy)
        return copy

    def wait(self, copy):
        copy.wait()
        self.open = [item for item in self.open if item is not copy]

    def finish(self):
        for copy in self.open:
            copy.wait()


def own_micro(order_s, h, count):
    m_own = jnp.int32(0)
    for m in range(count):
        m_own = m_own + jnp.where(order_s[0, m] == h, jnp.int32(m), jnp.int32(0))
    return m_own


def range_of(start, tops, m_own, count):
    now = jnp.full((1, 1), start, F32)
    own = now
    for m in range(1, count):
        now = DECAY * now + (1.0 - DECAY) * tops[:, m - 1: m]
        own = jnp.where(m_own == m, now, own)
    return own


def front_kernel(nd, nh, part, len_s, order_s, range_s, x_in, dy_in, pw_ref, ow_ref, wu_in, wd_in, pb_ref, ub_ref,
                 gain_ref, shift_ref,
                 x_o, dy_o, wa_o, wu_o, wd_o, a_o, qkv_o, c_o, cq_o, lse_o, n1_o, inv1_o, y1_o, b_o, f_o,
                 tops_o, own_o,
                 xl, xs, wa, wu, bias, a_ref, qkv, c_ref, cq, lse, lse_t, n1, inv1, y1, b_ref, f_ref,
                 acc, live, mask, cand, slots,
                 spool_sem, send_sem, recv_sem, top_send, top_recv):
    g = lax.axis_index("dp")
    h = lax.axis_index("head")
    n = nd * nh
    hc = ow_ref.shape[0]
    width = ow_ref.shape[1]
    micro = 4
    lanes = lax.broadcasted_iota(jnp.int32, (1, 128), 1)

    def peer(d):
        return (lax.rem(g + d // nh, nd), lax.rem(h + lax.rem(d, nh), nh))

    bar = pltpu.get_barrier_semaphore()

    def hello(d, carry):
        pl.semaphore_signal(bar, inc=1, device_id=peer(d), device_id_type=MESH)
        return carry

    lax.fori_loop(1, n, hello, 0)
    spool = Spool(spool_sem)
    wires = Wires(send_sem, recv_sem)
    load_x = spool.go(x_in, xl)
    own_x = spool.go(x_in.at[h], xs.at[0])
    own_wu = spool.go(wu_in, wu.at[0])
    spool.go(wd_in, wd_o.at[0])
    spool.go(dy_in.at[h], dy_o.at[0])

    m_own = own_micro(order_s, h, micro)
    length = len_s[0, h]
    for k in range(nh):
        start = (h ^ k) * part
        rows = start + lax.broadcasted_iota(jnp.int32, (part, 1), 0)
        live[k * part:(k + 1) * part, :] = jnp.where(rows < length, 1.0, 0.0)
        cols = start + lax.broadcasted_iota(jnp.int32, (1, part), 1)
        mask[:, k * part:(k + 1) * part] = jnp.where(cols < length, 0.0, MASK_FILL)
    bias[0] = jnp.zeros_like(bias[0])
    bias[0, 0:1, :hc] = pb_ref[0:1, :].astype(F32)
    bias[0, 0:1, 2 * hc:3 * hc] = pb_ref[1:2, :].astype(F32)
    bias[0, 1:2, :] = ub_ref[...].astype(F32)
    for i in range(3):
        wa[0, i * hc:(i + 1) * hc, :] = pw_ref[i].astype(F32).T.astype(BF16)
    wa[0, 3 * hc:, :] = ow_ref[...]

    def exchange_start(stage, row):
        cand[stage] = row

        def send(d, carry):
            remote(cand.at[stage], slots.at[stage, d - 1], top_send.at[stage], top_recv.at[stage], peer(d)).start()
            return carry

        lax.fori_loop(1, n, send, 0)

    def exchange_end(stage):
        pltpu.make_async_copy(slots.at[stage], slots.at[stage], top_recv.at[stage]).wait()
        top = jnp.maximum(cand[stage], jnp.max(slots[stage], axis=0))
        tops_o[stage:stage + 1, :] = top
        own = range_of(range_s[0, stage], top, m_own, micro)
        own_o[stage:stage + 1, :] = jnp.broadcast_to(own, (1, 128))
        return own

    def own_lane(value):
        return jnp.where(lanes == m_own, value, 0.0)

    spool.wait(load_x)
    row0 = jnp.zeros((1, 128), F32)
    local_rows = h * part + lax.broadcasted_iota(jnp.int32, (part, 1), 0)
    for s in range(micro):
        lit = jnp.where(local_rows < len_s[0, s], 1.0, 0.0)
        top = lane_top(span_top(xl[s].astype(F32), lit))
        row0 = jnp.maximum(row0, jnp.where(lanes == own_micro(order_s, s, micro), top, 0.0))

    pl.semaphore_wait(bar, n - 1)
    quarter = width // 4
    sibling, across = (g, h ^ 1), (g, h ^ 2)

    def part_of(q):
        return pl.ds(pl.multiple_of(q * quarter, quarter), quarter)

    mine = lax.rem(g, 4)
    x_wait = [wires.go(x_in.at[h ^ k], xs.at[k], (g, h ^ k)) for k in (2, 3, 1)]
    exchange_start(0, row0)
    bias_wait = [wires.go(bias.at[0], bias.at[k], (g, h ^ k)) for k in (1, 2, 3)]

    class Weight:
        def __init__(self, own, land):
            self.own, self.land = own, land

        def first(self):
            self.core = wires.go(self.own, self.land.at[1], sibling)
            self.leap = wires.go(self.own.at[part_of(mine), :], self.land.at[2, part_of(mine), :], across)

        def second(self):
            self.leap.wait_recv()
            here = self.land.at[2, part_of(mine), :]
            self.round = [
                (wires.go(here, self.land.at[2, part_of(mine), :], (g ^ e, h)), mine ^ e) for e in (1, 2, 3)
            ]
            self.last = [wires.go(here, self.land.at[3, part_of(mine), :], sibling)]

        def third(self):
            for copy, q in self.round:
                copy.wait_recv()
                self.last.append(
                    wires.go(self.land.at[2, part_of(q), :], self.land.at[3, part_of(q), :], sibling))

        def fourth(self):
            for copy in self.last:
                copy.wait_recv()

    way_a = Weight(wa.at[0], wa)
    way_u = Weight(wu.at[0], wu)
    way_d = Weight(wd_in, wd_o)
    spool.wait(own_wu)
    way_a.first()
    way_u.first()
    way_d.first()
    dy_wait = [wires.go(dy_in.at[h ^ k], dy_o.at[k], (g, h ^ k)) for k in (2, 3, 1)]
    r0 = exchange_end(0)
    spool.wait(own_x)
    for copy in x_wait:
        copy.wait_recv()
    ri0 = 1.0 / r0
    for k in range(nh):
        a_ref[k * part:(k + 1) * part, :] = (r0 * jnp.tanh(xs[k].astype(F32) * ri0)).astype(BF16)
    spool.go(xs, x_o)
    spool.go(a_ref, a_o)
    for copy in bias_wait:
        copy.wait_recv()

    def block(k):
        qkv[k] = (dot(a_ref[...], wa[k, : 3 * hc, :], NT) + bias[k, 0:1, : 3 * hc]).astype(BF16)
        for j in range(hc // HEAD_DIM):
            lo = j * HEAD_DIM
            keys = qkv[k, :, hc + lo: hc + lo + HEAD_DIM]
            vals = qkv[k, :, 2 * hc + lo: 2 * hc + lo + HEAD_DIM]
            q = qkv[k, :, lo: lo + HEAD_DIM] * BF16(HEAD_DIM ** -0.5)
            s = dot(q, keys, NT) + mask[...]
            top = jnp.max(s, axis=1, keepdims=True)
            e = jnp.exp(s - top)
            den = jnp.sum(e, axis=1, keepdims=True)
            p = (e * (1.0 / den)).astype(BF16)
            c_ref[k, :, lo: lo + HEAD_DIM] = dot(p, vals, NN)
            at = k * 8 + j
            lse[:, at: at + 1] = top + jnp.log(den)
        spool.go(qkv.at[k], qkv_o.at[k])
        spool.go(c_ref.at[k], c_o.at[k])
        return span_top(c_ref[k], live[...])

    lse[...] = jnp.zeros_like(lse)
    best = block(0)
    way_a.core.wait_recv()
    best = jnp.maximum(best, block(1))
    way_a.second()
    way_u.second()
    way_a.third()
    best = jnp.maximum(best, block(2))
    way_a.fourth()
    best = jnp.maximum(best, block(3))
    exchange_start(1, own_lane(lane_top(best)))
    turned = lse[...].T
    for k in range(nh):
        lse_t[k] = turned[k * 8:(k + 1) * 8, :]
    spool.go(lse_t, lse_o)
    spool.go(wa, wa_o)
    way_d.second()
    r1 = exchange_end(1)
    ri1 = 1.0 / r1
    for k in range(nh):
        cq[k] = (r1 * jnp.tanh(c_ref[k] * ri1)).astype(BF16)
        o1 = dot(cq[k], wa[k, 3 * hc:, :], NN)
        if k == 0:
            acc[...] = o1
        else:
            acc[...] += o1
    spool.go(cq, cq_o)
    bo, ca = shift_ref[0:1, :].astype(F32), shift_ref[1:2, :].astype(F32)
    ga = gain_ref[0:1, :].astype(F32)

    def norm_step(i, best):
        rows = pl.ds(pl.multiple_of(i * part, part), part)
        nn, inv = norm_parts(xs[i].astype(F32) + (acc[rows, :] + bo))
        n1[rows, :] = nn
        inv1[rows, :] = inv
        y = nn * ga + ca
        y1[rows, :] = y
        return jnp.maximum(best, span_top(y, live[rows, :]))

    best = lax.fori_loop(0, nh, norm_step, jnp.zeros((1, width), F32))
    exchange_start(2, own_lane(lane_top(best)))
    for src, dst in ((n1, n1_o), (inv1, inv1_o), (y1, y1_o)):
        spool.go(src, dst)
    way_u.third()
    r2 = exchange_end(2)
    b_ref[...] = (r2 * jnp.tanh(y1[...] * (1.0 / r2))).astype(BF16)
    spool.go(b_ref, b_o)

    def units(k):
        f = dot(b_ref[...], wu[k], NN) + bias[k, 1:2, :]
        cdf = 0.5 * (1.0 + lax.erf(f * (0.5 ** 0.5)))
        gg = f * cdf
        f_ref[k] = f
        spool.go(f_ref.at[k], f_o.at[k])
        return span_top(gg, live[...])

    best = units(0)
    way_u.core.wait_recv()
    best = jnp.maximum(best, units(1))
    best = jnp.maximum(best, units(2))
    way_u.fourth()
    best = jnp.maximum(best, units(3))
    exchange_start(3, own_lane(lane_top(best)))
    spool.go(wu, wu_o)
    way_d.third()
    exchange_end(3)
    way_d.core.wait_recv()
    way_d.fourth()
    for copy in dy_wait:
        copy.wait_recv()
    for stage in range(4):
        pltpu.make_async_copy(slots.at[stage], slots.at[stage], top_send.at[stage]).wait()
    tops_o[4:8, :] = jnp.zeros((4, 128), F32)
    own_o[4:8, :] = jnp.zeros((4, 128), F32)
    wires.finish()
    spool.finish()


def front(lengths, order, ranges, x_in, dy_in, pw, ow, wu, wd, pb, ub, gains, shifts):
    nd, nh = lax.axis_size("dp"), lax.axis_size("head")
    slots, part, width = x_in.shape
    count = slots * part
    hc, fc = ow.shape[0], wu.shape[1]

    def shape(*dims, kind=F32):
        return jax.ShapeDtypeStruct(dims, kind)

    outs = (
        shape(slots, part, width, kind=BF16), shape(slots, part, width, kind=BF16),
        shape(nh, 4 * hc, width, kind=BF16), shape(nh, width, fc, kind=BF16), shape(nh, fc, width, kind=BF16),
        shape(count, width, kind=BF16), shape(nh, count, 3 * hc, kind=BF16), shape(nh, count, hc),
        shape(nh, count, hc, kind=BF16), shape(nh, 8, count), shape(count, width), shape(count, 1),
        shape(count, width), shape(count, width, kind=BF16), shape(nh, count, fc),
        shape(8, 128), shape(8, 128),
    )
    scratch = [pltpu.VMEM(o.shape, o.dtype) for o in (
        outs[0], outs[0], outs[2], outs[3], shape(nh, 8, fc), outs[5], outs[6], outs[7], outs[8], shape(count, 128),
        outs[9], outs[10], outs[11], outs[12], outs[13], outs[14], shape(count, width),
        shape(count, 1), shape(1, count), shape(4, 1, 128), shape(4, nd * nh - 1, 1, 128))]
    smem = pl.BlockSpec(memory_space=pltpu.SMEM)
    return pl.pallas_call(
        functools.partial(front_kernel, nd, nh, part),
        out_shape=outs,
        in_specs=[smem] * 3 + [ANY] * 2 + [VM] * 2 + [ANY] * 2 + [VM] * 4,
        out_specs=[ANY] * 15 + [VM] * 2,
        scratch_shapes=scratch + [
            pltpu.SemaphoreType.DMA((40,)), pltpu.SemaphoreType.DMA((40,)), pltpu.SemaphoreType.DMA((40,)),
            pltpu.SemaphoreType.DMA((4,)), pltpu.SemaphoreType.DMA((4,)),
        ],
        compiler_params=pltpu.CompilerParams(collective_id=0, has_side_effects=True, vmem_limit_bytes=LIMIT),
    )(lengths, order, ranges, x_in, dy_in, pw, ow, wu, wd, pb, ub, gains, shifts)


AXES = ("y", "z2", "z1", "x")
WAYS = (("y", "x", "z1", "z2"), ("x", "z1", "y", "z2"), ("z1", "y", "x", "z2"))


def rear_kernel(joined, part, len_s, own_ref, gain_ref, shift_ref, f_in, wd_in, wu_in, wa_in, y1_in, n1_in, inv1_ref, b_in,
                dy_in, x_in, a_in, c_in, cq_in, qkv_in, lse_ref,
                out_own, out_got, dx_own, dx_got, sums, small_sum,
                f_ref, w1, wu, gq, y1, n1, acc, dz, rows_a, rows_b, dzb, tr, tr_b, df, c_ring, cq_ring, qkv_ring,
                dc_ref, kt_ref, dqt_ref, dqkv, live, kept, stage, got_core, got1, got2, got3, got4,
                out_stage, small_now, small_got, spool_sem, send_sem, recv_sem, free_sem, plain_sem):
    g = lax.axis_index("dp")
    h = lax.axis_index("head")
    nh, count, fc = f_ref.shape
    hc = c_ring.shape[2]
    width = y1.shape[1]
    third = width // 3
    bit = {"x": lax.rem(g, 2), "z1": lax.rem(g // 2, 2), "z2": g // 4, "y": 0}
    where = {"y": (g, h ^ 2), "core": (g, h ^ 1)}
    if joined:
        where.update({"x": (g ^ 1, h), "z1": (g ^ 2, h), "z2": (g ^ 4, h)})
    bar = pltpu.get_barrier_semaphore()
    friends = list(where.values()) + [(g, h ^ 3)]
    for friend in friends:
        pl.semaphore_signal(bar, inc=1, device_id=friend, device_id_type=MESH)
    spool = Spool(spool_sem)
    wires = Wires(send_sem, recv_sem)
    order = (1, 3, 0, 2)
    load_f, load_d, load_u = {}, {}, {}
    for k in range(nh):
        load_f[k] = spool.go(f_in.at[k], f_ref.at[k])
        load_d[k] = spool.go(wd_in.at[k], w1.at[k])
    load_y1 = spool.go(y1_in, y1)
    load_dy = spool.go(dy_in, rows_a)
    load_b = spool.go(b_in, rows_b)
    for k in order:
        load_u[k] = spool.go(wu_in.at[k], wu.at[k])
    load_n1 = spool.go(n1_in, n1)
    load_c = {}

    def load_heads(i):
        k = order[i]
        load_c[k] = [
            spool.go(c_in.at[k], c_ring.at[i % 2]), spool.go(cq_in.at[k], cq_ring.at[i % 2]),
            spool.go(qkv_in.at[k], qkv_ring.at[i % 2]),
        ]

    load_heads(0)
    load_heads(1)
    r0, r1, r2, r3 = [own_ref[i:i + 1, 0:1] for i in range(4)]
    ga, gb = gain_ref[0:1, :].astype(F32), gain_ref[1:2, :].astype(F32)
    bd, cb = shift_ref[2:3, :].astype(F32), shift_ref[3:4, :].astype(F32)
    length = len_s[0, h]
    for k in range(nh):
        at = (h ^ k) * part + lax.broadcasted_iota(jnp.int32, (part, 1), 0)
        live[k * part:(k + 1) * part, :] = jnp.where(at < length, 1.0, 0.0)
    small_now[0] = jnp.zeros_like(small_now[0])

    ri3 = 1.0 / r3
    for k in range(nh):
        spool.wait(load_f[k])
        f = f_ref[k]
        cdf = 0.5 * (1.0 + lax.erf(f * (0.5 ** 0.5)))
        t = jnp.tanh(f * cdf * ri3)
        gq[k] = (r3 * t).astype(BF16)
        f_ref[k] = (cdf + f * (jnp.exp(-0.5 * f * f) * ROOT)) * (1.0 - t * t)
        spool.wait(load_d[k])
        o2 = dot(gq[k], w1[k], NN)
        if k == 0:
            acc[...] = o2
        else:
            acc[...] += o2
    spool.wait(load_y1)
    spool.wait(load_dy)
    zero = jnp.zeros((1, width), F32)
    s_gb = s_cb = s_bd = zero
    for k in range(nh):
        rows = slice(k * part, (k + 1) * part)
        n, inv = norm_parts(y1[rows, :] + (acc[rows, :] + bd))
        out = n * gb + cb
        if k == 0:
            out_own[...] = out
        else:
            out_stage[0, k - 1] = out.astype(BF16)
        dy = rows_a[k].astype(F32)
        d = norm_back(dy * gb, n, inv)
        dz[rows, :] = d
        dzb[rows, :] = d.astype(BF16)
        tr[:, rows] = d.T.astype(BF16)
        s_gb = s_gb + jnp.sum(dy * n, axis=0, keepdims=True)
        s_cb = s_cb + jnp.sum(dy, axis=0, keepdims=True)
        s_bd = s_bd + jnp.sum(d, axis=0, keepdims=True)
    load_x = spool.go(x_in, rows_a)
    pl.semaphore_wait(bar, len(friends))
    tail = [wires.go(out_stage.at[0, k - 1], out_got.at[k - 1], (g, h ^ k)) for k in (2, 3, 1)]

    core = {}

    eighths = [(r * (width // 8), (r // 4, (r // 2) % 2, r % 2)) for r in range(8)]

    def spread(ref, slot, value):
        for at, spot in eighths:
            ref[(*slot, *spot)] = value[at: at + width // 8, :].astype(BF16)

    def plain(chunk, k, value):
        spread(stage, (0,), value)
        copy = pltpu.make_async_copy(stage.at[0], sums.at[chunk, k], plain_sem)
        copy.start()
        copy.wait()

    def give(chunk, j, buf):
        core[chunk, j] = wires.go(buf, got_core.at[chunk % 2, j], where["core"])

    def keep(chunk, j, k, value):
        if not joined:
            plain(chunk, k, value)
            return
        if chunk == 2:
            core[1, j].wait_send()
        core[chunk, j].wait_recv()
        for at, spot in eighths:
            kept[(chunk, j, *spot)] = (
                value[at: at + width // 8, :] + got_core[(chunk % 2, j, *spot)].astype(F32)
            ).astype(BF16)

    got = (None, got1, got2, got3, got4)
    pending = {}

    def region(way, step, last):
        index = []
        for axis in AXES:
            at = way.index(axis)
            if at == step:
                index.append(last)
            else:
                index.append(bit[axis] if at < step else slice(None))
        return index

    def send_step(chunk, step):
        if not joined:
            return
        pending[chunk, step] = []
        for i, way in enumerate(WAYS):
            axis = way[step]
            other = 1 if axis == "y" else 1 - bit[axis]
            index = (chunk, *region(way, step, other), slice(None), pl.ds(i * third, third))
            pending[chunk, step].append(wires.go(kept.at[index], got[step + 1].at[chunk, i], where[axis]))

    def pump(chunk, step):
        if not joined:
            return
        for i, way in enumerate(WAYS):
            pending[chunk, step][i].wait_recv()
            cols = slice(i * third, (i + 1) * third)
            index = region(way, step, bit[way[step]])
            spots = [()]
            for item in index:
                if isinstance(item, slice):
                    spots = [s + (v,) for s in spots for v in (0, 1)]
            for spot in spots:
                left = iter(spot)
                full = tuple(next(left) if isinstance(item, slice) else item for item in index)
                value = (kept[(chunk, *full, slice(None), cols)].astype(F32)
                         + got[step + 1][(chunk, i, *spot)].astype(F32))
                if step == 3:
                    sums[chunk, :, cols] = value
                else:
                    kept[(chunk, *full, slice(None), cols)] = value.astype(BF16)
        if step < 3:
            send_step(chunk, step + 1)

    for j, k in enumerate((1, 3)):
        value = dot(tr[...], gq[k], NN)
        if joined:
            spread(stage, (j,), value)
            give(0, j, stage.at[j])
        else:
            plain(0, k, value)
    spool.wait(load_b)
    for k in range(nh):
        rows = slice(k * part, (k + 1) * part)
        tr_b[:, rows] = rows_b[rows, :].astype(F32).T.astype(BF16)
    load_a = spool.go(a_in, rows_b)
    load_w = {}

    def units(k, first):
        d = (dot(dzb[...], w1[k], NT) * f_ref[k]).astype(BF16)
        df[...] = d
        small_now[0, pl.ds(4 + (h ^ k), 1), :] = jnp.sum(d.astype(F32), axis=0, keepdims=True)
        load_w[k] = spool.go(wa_in.at[k], w1.at[k])
        spool.wait(load_u[k])
        part_sum = dot(df[...], wu[k], NT)
        if first:
            acc[...] = part_sum
        else:
            acc[...] += part_sum
        return dot(tr_b[...], df[...], NN)

    for j, k in enumerate((1, 3)):
        value = units(k, j == 0)
        if joined:
            spread(kept, (2, j), value)
            give(1, j, kept.at[2, j])
        else:
            plain(1, k, value)
    for j, k in enumerate((0, 2)):
        keep(0, j, k, dot(tr[...], gq[k], NN))
    if joined:
        pl.semaphore_signal(free_sem, inc=1, device_id=where["core"], device_id_type=MESH)
    send_step(0, 0)
    for j, k in enumerate((0, 2)):
        keep(1, j, k, units(k, False))
    send_step(1, 0)

    ri2 = 1.0 / r2
    spool.wait(load_n1)
    s_ga = s_ca = s_bo = zero
    for k in range(nh):
        rows = slice(k * part, (k + 1) * part)
        t = jnp.tanh(y1[rows, :] * ri2)
        dy1 = dz[rows, :] + acc[rows, :] * (1.0 - t * t)
        n = n1[rows, :]
        d = norm_back(dy1 * ga, n, inv1_ref[rows, :])
        dz[rows, :] = d
        dzb[rows, :] = d.astype(BF16)
        tr[:, rows] = d.T.astype(BF16)
        s_ga = s_ga + jnp.sum(dy1 * n, axis=0, keepdims=True)
        s_ca = s_ca + jnp.sum(dy1, axis=0, keepdims=True)
        s_bo = s_bo + jnp.sum(d, axis=0, keepdims=True)
    for i, row in enumerate((s_ga, s_gb, s_bo, s_ca, s_bd, s_cb)):
        small_now[0, 8 + i: 9 + i, :] = row
    spool.wait(load_a)
    for k in range(nh):
        rows = slice(k * part, (k + 1) * part)
        tr_b[:, rows] = rows_b[rows, :].astype(F32).T.astype(BF16)

    ri1 = 1.0 / r1
    scale = HEAD_DIM ** -0.5

    def heads(i):
        k = order[i]
        slot = i % 2
        for copy in load_c[k]:
            spool.wait(copy)
        spool.wait(load_w[k])
        qkv = qkv_ring.at[slot]
        t = jnp.tanh(c_ring[slot] * ri1)
        dc_ref[...] = (dot(dzb[...], w1[k, 3 * hc:, :], NT) * (1.0 - t * t)).astype(BF16)
        kt_ref[...] = qkv[:, hc: 2 * hc].astype(F32).T.astype(BF16)
        for j in range(hc // HEAD_DIM):
            lo = j * HEAD_DIM
            keys = qkv[:, hc + lo: hc + lo + HEAD_DIM]
            vals = qkv[:, 2 * hc + lo: 2 * hc + lo + HEAD_DIM]
            q = qkv[:, lo: lo + HEAD_DIM] * BF16(scale)
            dc = dc_ref[:, lo: lo + HEAD_DIM]
            s = dot(keys, q, NT)
            p = jnp.where(live[...] > 0.0, jnp.exp(s - lse_ref[k, j: j + 1, :]), 0.0)
            pd = p * dot(vals, dc, NT)
            delta = jnp.sum(pd, axis=0, keepdims=True)
            ds = (pd - p * delta).astype(BF16)
            dqkv[:, 2 * hc + lo: 2 * hc + lo + HEAD_DIM] = dot(p.astype(BF16), dc, NN).astype(BF16)
            dqkv[:, hc + lo: hc + lo + HEAD_DIM] = dot(ds, q, NN).astype(BF16)
            dqt_ref[lo: lo + HEAD_DIM, :] = dot(kt_ref[lo: lo + HEAD_DIM, :], ds, NN) * scale
        dqkv[:, :hc] = dqt_ref[...].T.astype(BF16)
        small_now[0, pl.ds(h ^ k, 1), : 3 * hc] = jnp.sum(dqkv[...].astype(F32), axis=0, keepdims=True)
        da = dot(dqkv[...], w1[k, : 3 * hc, :], NN)
        if i == 0:
            acc[...] = da
        else:
            acc[...] += da
        value = jnp.concatenate(
            [dot(tr_b[...], dqkv[...], NN), dot(tr[...], cq_ring[slot], NN)], axis=1)
        if i + 2 < nh:
            load_heads(i + 2)
        return value

    for i in (0, 1):
        value = heads(i)
        if joined:
            core[0, i].wait_send()
            spread(stage, (i,), value)
            if i == 0:
                pl.semaphore_wait(free_sem, 1)
            give(2, i, stage.at[i])
        else:
            plain(2, order[i], value)
        if i == 0:
            pump(0, 0)
    keep(2, 0, 0, heads(2))
    pump(1, 0)
    pump(0, 1)
    keep(2, 1, 2, heads(3))
    send_step(2, 0)
    small_ways = ("core", "y", "x", "z1", "z2")
    small_copy = {}

    def small_step(i):
        if not joined:
            return
        if i > 0:
            small_copy[i - 1].wait_recv()
            small_now[i] = small_now[i - 1] + small_got[i - 1]
        if i < 5:
            small_copy[i] = wires.go(small_now.at[i], small_got.at[i], where[small_ways[i]])

    small_step(0)
    ri0 = 1.0 / r0
    spool.wait(load_x)
    for k in range(nh):
        rows = slice(k * part, (k + 1) * part)
        t = jnp.tanh(rows_a[k].astype(F32) * ri0)
        d = dz[rows, :] + acc[rows, :] * (1.0 - t * t)
        if k == 0:
            dx_own[...] = d
        else:
            out_stage[1, k - 1] = d.astype(BF16)

    def send_dx(k):
        tail.append(wires.go(out_stage.at[1, k - 1], dx_got.at[k - 1], (g, h ^ k)))

    pump(0, 2)
    pump(1, 1)
    small_step(1)
    pump(2, 0)
    send_dx(2)
    small_step(2)
    pump(1, 2)
    pump(0, 3)
    pump(2, 1)
    send_dx(3)
    send_dx(1)
    small_step(3)
    pump(1, 3)
    pump(2, 2)
    small_step(4)
    pump(2, 3)
    small_step(5)
    small_sum[...] = small_now[5 if joined else 0]
    for copy in tail:
        copy.wait_recv()
    if joined:
        for chunk in (0, 1):
            for j in (0, 1):
                wires.sent = [item for item in wires.sent if item is not core[chunk, j]]
    wires.finish()
    spool.finish()


def rear(joined, lengths, owns, gains, shifts, f, wd, wu, wa, y1, n1, inv1, b, dy, x, a, c, cq, qkv, lse):
    nh, count, fc = f.shape
    part = x.shape[1]
    width = y1.shape[1]
    hc = c.shape[2]
    rows, third = width // 8, width // 3

    def shape(*dims, kind=F32):
        return jax.ShapeDtypeStruct(dims, kind)

    def vmem(*dims, kind=BF16):
        return pltpu.VMEM(dims, kind)

    smem = pl.BlockSpec(memory_space=pltpu.SMEM)
    return pl.pallas_call(
        functools.partial(rear_kernel, joined, part),
        out_shape=(
            shape(part, width), shape(nh - 1, part, width, kind=BF16), shape(part, width),
            shape(nh - 1, part, width, kind=BF16),
            shape(3, rows, width) if joined else shape(3, nh, 2, 2, 2, rows, width, kind=BF16),
            shape(16, width),
        ),
        in_specs=[smem] + [VM] * 3 + [ANY] * 6 + [VM] + [ANY] * 7 + [VM],
        out_specs=[VM, ANY, VM, ANY, VM if joined else ANY, VM],
        scratch_shapes=[
            vmem(nh, count, fc, kind=F32), vmem(nh, width, width), vmem(nh, width, fc), vmem(nh, count, fc),
            vmem(count, width, kind=F32), vmem(count, width, kind=F32), vmem(count, width, kind=F32),
            vmem(count, width, kind=F32), vmem(nh, part, width), vmem(count, width), vmem(count, width),
            vmem(width, count), vmem(width, count), vmem(count, fc),
            vmem(2, count, hc, kind=F32), vmem(2, count, hc), vmem(2, count, 3 * hc),
            vmem(count, hc), vmem(hc, count), vmem(hc, count, kind=F32), vmem(count, 3 * hc), vmem(count, 1, kind=F32),
            vmem(3, 2, 2, 2, 2, rows, width), vmem(2, 2, 2, 2, rows, width), vmem(2, 2, 2, 2, 2, rows, width),
            vmem(3, 3, 2, 2, 2, rows, third), vmem(3, 3, 2, 2, rows, third), vmem(3, 3, 2, rows, third),
            vmem(3, 3, rows, third), vmem(2, nh - 1, part, width),
            vmem(6, 16, width, kind=F32), vmem(5, 16, width, kind=F32),
            pltpu.SemaphoreType.DMA((48,)), pltpu.SemaphoreType.DMA((56,)), pltpu.SemaphoreType.DMA((56,)),
            pltpu.SemaphoreType.REGULAR, pltpu.SemaphoreType.DMA,
        ],
        compiler_params=pltpu.CompilerParams(collective_id=1, has_side_effects=True, vmem_limit_bytes=REAR_LIMIT),
    )(lengths, owns, gains, shifts, f, wd, wu, wa, y1, n1, inv1, b, dy, x, a, c, cq, qkv, lse)


def finish_kernel(range_s, tops, out_own, out_got, dx_own, dx_got, sums, small,
                  out_o, dx_o, proj_o, bias_o, outw_o, up_o, off_o, down_o, gain_o, shift_o, range_o):
    h = lax.axis_index("head")
    nh = out_o.shape[0]
    hc = proj_o.shape[3]
    for own, got, dst in ((out_own, out_got, out_o), (dx_own, dx_got, dx_o)):
        dst[h] = own[...]
        for k in range(1, nh):
            dst[h ^ k] = got[k - 1].astype(F32)
    for i in range(3):
        proj_o[0, i] = sums[2, :, i * hc:(i + 1) * hc]

    def turned(value):
        rows = value.shape[0]
        filled = jnp.concatenate([value, jnp.zeros((-rows % 128, value.shape[1]), F32)], axis=0)
        return filled.T[:, :rows]

    outw_o[0] = turned(sums[2, :, 3 * hc:])
    up_o[0] = sums[1]
    down_o[0] = turned(sums[0])
    width = small.shape[1]
    for k in range(nh):
        bias_o[0, 0:1, k * hc:(k + 1) * hc] = small[k:k + 1, :hc]
        bias_o[0, 1:2, k * hc:(k + 1) * hc] = small[k:k + 1, 2 * hc:3 * hc]
        off_o[0:1, k * width:(k + 1) * width] = small[4 + k:5 + k, :]
    gain_o[0] = small[8:10, :]
    shift_o[0] = small[10:14, :]
    for i in range(4):
        now = jnp.full((1, 1), range_s[0, i], F32)
        for m in range(4):
            now = DECAY * now + (1.0 - DECAY) * tops[i:i + 1, m:m + 1]
        range_o[0:1, i:i + 1] = now


def local(kernel, outs, out_specs, in_specs, scratch, *args):
    return pl.pallas_call(
        kernel,
        out_shape=outs,
        in_specs=in_specs,
        out_specs=out_specs,
        scratch_shapes=scratch,
        compiler_params=pltpu.CompilerParams(vmem_limit_bytes=LIMIT),
    )(*args)


def body(hidden_in, seq_lengths, batch_order, clip_ranges, proj_weight, proj_bias, out_weight,
         up_weight, up_bias, down_weight, norm_gains, out_biases, cotangent):
    nd, nh = lax.axis_size("dp"), lax.axis_size("head")
    slots, part, width = hidden_in.shape
    hc = proj_bias.shape[2]
    fc = up_bias.shape[1]
    joined = nd == 8
    gains, shifts = norm_gains[0], out_biases[0]
    (xs, dys, was, wus, wds, a, qkv, c, cq, lse, n1, inv1, y1, b, f, tops, owns) = front(
        seq_lengths, batch_order, clip_ranges, hidden_in, cotangent, proj_weight[0], out_weight[0], up_weight[0],
        down_weight[0], proj_bias[0], up_bias, gains, shifts)
    out_own, out_got, dx_own, dx_got, sums, small = rear(
        joined, seq_lengths, owns, gains, shifts, f, wds, wus, was, y1, n1, inv1, b, dys, xs, a, c, cq, qkv, lse)

    def shape(*dims):
        return jax.ShapeDtypeStruct(dims, F32)

    if joined:
        return local(
            finish_kernel,
            (shape(slots, part, width), shape(slots, part, width), shape(1, 3, width // nd, hc),
             shape(1, 2, nh * hc), shape(1, hc, width // nd), shape(1, width // nd, fc), shape(1, nh * fc),
             shape(1, fc, width // nd), shape(1, 2, width), shape(1, 4, width), shape(1, 4)),
            [VM] * 11, [pl.BlockSpec(memory_space=pltpu.SMEM)] + [VM] * 7, [],
            clip_ranges, tops, out_own, out_got, dx_own, dx_got, sums, small)
    h = lax.axis_index("head")
    sums, small = settle_plain(sums.reshape(3, nh, width, width), small, h)
    index = h ^ jnp.arange(nh)
    hidden_out = jnp.concatenate([out_own[None], out_got.astype(F32)])[index]
    input_grad = jnp.concatenate([dx_own[None], dx_got.astype(F32)])[index]
    now = clip_ranges
    for m in range(slots):
        now = DECAY * now + (1.0 - DECAY) * tops[None, :4, m]
    return (
        hidden_out, input_grad, sums[2][:, : 3 * hc].reshape(1, -1, 3, hc).transpose(0, 2, 1, 3),
        jnp.stack([small[:4, :hc].reshape(-1), small[:4, 2 * hc: 3 * hc].reshape(-1)])[None],
        sums[2][:, 3 * hc:].T[None], sums[1][None], small[4:8].reshape(1, -1), sums[0].T[None],
        small[None, 8:10], small[None, 10:14], now,
    )


def solution(mesh):
    in_specs = (
        P("dp", "head", None), P("dp", None), P("dp", None), P(),
        P(None, None, None, "head"), P(None, None, "head"), P(None, "head", None),
        P(None, None, "head"), P(None, "head"), P(None, "head", None), P(), P(),
        P("dp", "head", None),
    )
    out_specs = (
        P("dp", "head", None), P("dp", "head", None), P(None, None, "dp", "head"), P(),
        P(None, "head", "dp"), P(None, "dp", "head"), P(), P(None, "head", "dp"), P(), P(), P(),
    )
    return jax.shard_map(body, mesh=mesh, in_specs=in_specs, out_specs=out_specs, check_vma=False)
```

```python
import functools
import jax
import jax.numpy as jnp
from jax import lax
from jax.experimental import pallas as pl
from jax.experimental.pallas import tpu as pltpu
from jax.sharding import PartitionSpec as P

HEAD_DIM = 64
EPSILON = 1e-06
MASK_FILL = -1e30
DECAY = 0.9
ROOT = 0.3989422804014327
MESH = pl.DeviceIdType.MESH
BF16 = jnp.bfloat16
F32 = jnp.float32
ANY = pl.BlockSpec(memory_space=pl.ANY)
VM = pl.BlockSpec(memory_space=pltpu.VMEM)


def remote(src, dst, send_sem, recv_sem, where):
    return pltpu.make_async_remote_copy(
        src_ref=src, dst_ref=dst, send_sem=send_sem, recv_sem=recv_sem,
        device_id=where, device_id_type=MESH,
    )


def settle_plain(grads, small, head_pos):
    order = head_pos ^ jnp.arange(grads.shape[1])
    part = lax.psum_scatter(grads[:, order].astype(F32), "head", scatter_dimension=1, tiled=True)[:, 0]
    return lax.psum_scatter(part, "dp", scatter_dimension=1, tiled=True), lax.psum(small, ("dp", "head"))


NN = ((1,), (0,))
NT = ((1,), (1,))
TN = ((0,), (0,))
LIMIT = 63 * 1024 * 1024


def dot(a, b, dims):
    return lax.dot_general(a, b, (dims, ((), ())), preferred_element_type=F32)


def norm_parts(z):
    centred = z - jnp.mean(z, axis=-1, keepdims=True)
    inv = lax.rsqrt(jnp.mean(centred * centred, axis=-1, keepdims=True) + EPSILON)
    return centred * inv, inv


def norm_back(dn, n, inv):
    return (dn - jnp.mean(dn, axis=-1, keepdims=True)
            - n * jnp.mean(dn * n, axis=-1, keepdims=True)) * inv


def span_top(values, live):
    return jnp.max(jnp.abs(values) * live, axis=0, keepdims=True)


def lane_top(row):
    return jnp.max(row, axis=1, keepdims=True)


class Wires:
    def __init__(self, send_sem, recv_sem):
        self.send_sem, self.recv_sem = send_sem, recv_sem
        self.sent = []
        self.count = 0

    def go(self, src, dst, where):
        i = self.count
        self.count += 1
        copy = remote(src, dst, self.send_sem.at[i], self.recv_sem.at[i], where)
        copy.start()
        self.sent.append(copy)
        return copy

    def leave(self, copy):
        copy.wait_send()
        self.sent = [item for item in self.sent if item is not copy]

    def finish(self):
        for copy in self.sent:
            copy.wait_send()


class Spool:
    def __init__(self, sem):
        self.sem = sem
        self.count = 0
        self.open = []

    def go(self, src, dst):
        copy = pltpu.make_async_copy(src, dst, self.sem.at[self.count])
        self.count += 1
        copy.start()
        self.open.append(copy)
        return copy

    def wait(self, copy):
        copy.wait()
        self.open = [item for item in self.open if item is not copy]

    def finish(self):
        for copy in self.open:
            copy.wait()


def own_micro(order_s, h, count):
    m_own = jnp.int32(0)
    for m in range(count):
        m_own = m_own + jnp.where(order_s[0, m] == h, jnp.int32(m), jnp.int32(0))
    return m_own


def range_of(start, tops, m_own, count):
    now = jnp.full((1, 1), start, F32)
    own = now
    for m in range(1, count):
        now = DECAY * now + (1.0 - DECAY) * tops[:, m - 1: m]
        own = jnp.where(m_own == m, now, own)
    return own


AXES = ("y", "z2", "z1", "x")
WAYS = (("y", "x", "z1", "z2"), ("x", "z1", "y", "z2"), ("z1", "y", "x", "z2"))


def layer_kernel(joined, nd, nh, part, len_s, order_s, range_s, x_in, dy_in, pw_in, ow_in, wu_in, wd_in, pb_ref, ub_ref,
                 gain_ref, shift_ref,
                 out_own, out_got, dx_own, dx_got, sums, small_sum, tops_o, wa_h, n1_h, a_h,
                 xl, xs, wa, wu, wd, bias, ab, qkv, c_ref, cq, lse, lse_t, inv1, y1, f_ref, gq, acc, dz, dzb, tr, tr_b,
                 df, dc_ref, kt_ref, dqt_ref, dqkv, live, mask, kept, got_core, got1, got2, got3, got4, out_stage,
                 small_now, small_got, cand, slots,
                 spool_sem, send_sem, recv_sem, top_send, top_recv, free_sem, plain_sem):
    g = lax.axis_index("dp")
    h = lax.axis_index("head")
    n = nd * nh
    count, width = y1.shape
    hc = c_ref.shape[2]
    fc = f_ref.shape[2]
    heads = hc // HEAD_DIM
    micro = nh
    third = width // 3
    eighth = width // 8
    scale = HEAD_DIM ** -0.5
    lanes = lax.broadcasted_iota(jnp.int32, (1, 128), 1)
    bit = {"x": lax.rem(g, 2), "z1": lax.rem(g // 2, 2), "z2": g // 4, "y": 0}
    where = {"x": (g ^ 1, h), "z1": (g ^ 2, h), "z2": (g ^ 4, h), "y": (g, h ^ 2), "core": (g, h ^ 1)}
    sibling, across = where["core"], where["y"]

    def peer(d):
        return (g ^ (d // nh), h ^ lax.rem(d, nh))

    bar = pltpu.get_barrier_semaphore()

    def hello(d, carry):
        pl.semaphore_signal(bar, inc=1, device_id=peer(d), device_id_type=MESH)
        return carry

    lax.fori_loop(1, n, hello, 0)
    spool = Spool(spool_sem)
    wires = Wires(send_sem, recv_sem)
    load_x = spool.go(x_in, xl)
    load_w = []
    for i in range(4):
        for x in (0, 1):
            rows = pl.ds(x * eighth, eighth)
            load_w.append(spool.go(ow_in.at[rows, :] if i == 3 else pw_in.at[i, rows, :], wa.at[0, i // 2, i % 2, x]))
    own_x = spool.go(x_in.at[h], xs.at[0])
    own_wu = spool.go(wu_in, wu.at[0])
    own_wd = spool.go(wd_in, wd.at[0])

    def block_rows(k):
        return slice(k * part, (k + 1) * part)

    m_own = own_micro(order_s, h, micro)
    length = len_s[0, h]
    for k in range(nh):
        start = (h ^ k) * part
        rows = start + lax.broadcasted_iota(jnp.int32, (part, 1), 0)
        live[block_rows(k), :] = jnp.where(rows < length, 1.0, 0.0)
        cols = start + lax.broadcasted_iota(jnp.int32, (1, part), 1)
        mask[:, block_rows(k)] = jnp.where(cols < length, 0.0, MASK_FILL)
    bias[0] = jnp.zeros_like(bias[0])
    bias[0, 0:1, :hc] = pb_ref[0:1, :].astype(F32)
    bias[0, 0:1, 2 * hc:3 * hc] = pb_ref[1:2, :].astype(F32)
    bias[0, 1:2, :] = ub_ref[...].astype(F32)
    ga, gb = gain_ref[0:1, :].astype(F32), gain_ref[1:2, :].astype(F32)
    bo, ca, bd, cb = [shift_ref[i:i + 1, :].astype(F32) for i in range(4)]
    lse[...] = jnp.zeros_like(lse)
    small_now[0] = jnp.zeros_like(small_now[0])
    tops_o[4:8, :] = jnp.zeros((4, 128), F32)

    def exchange_start(stage, row):
        cand[stage] = row

        def send(d, carry):
            remote(cand.at[stage], slots.at[stage, d - 1], top_send.at[stage], top_recv.at[stage], peer(d)).start()
            return carry

        lax.fori_loop(1, n, send, 0)

    def exchange_end(stage):
        pltpu.make_async_copy(slots.at[stage], slots.at[stage], top_recv.at[stage]).wait()
        top = jnp.maximum(cand[stage], jnp.max(slots[stage], axis=0))
        tops_o[stage:stage + 1, :] = top
        return range_of(range_s[0, stage], top, m_own, micro)

    def own_lane(value):
        return jnp.where(lanes == m_own, value, 0.0)

    spool.wait(load_x)
    row0 = jnp.zeros((1, 128), F32)
    local_rows = h * part + lax.broadcasted_iota(jnp.int32, (part, 1), 0)
    for s in range(micro):
        lit = jnp.where(local_rows < len_s[0, s], 1.0, 0.0)
        top = lane_top(span_top(xl[s].astype(F32), lit))
        row0 = jnp.maximum(row0, jnp.where(lanes == own_micro(order_s, s, micro), top, 0.0))
    for copy in load_w:
        spool.wait(copy)

    pl.semaphore_wait(bar, n - 1)

    mine = lax.rem(g, 4)

    def cut_view(ref):
        return lambda slot, q, i: ref.at[slot, q // 2, lax.rem(q, 2)] if i is None else ref.at[
            slot, q // 2, lax.rem(q, 2), i]

    def flat_view(ref):
        def view(slot, q, i):
            size = 2 * eighth if i is None else eighth
            start = pl.multiple_of(q * (2 * eighth) + (0 if i is None else i) * eighth, eighth)
            return ref.at[slot, pl.ds(start, size), :]

        return view

    class Weight:
        def __init__(self, land, view):
            self.land, self.view = land, view
            self.leaps, self.round, self.last = {}, {}, []

        def hand(self):
            self.core = wires.go(self.land.at[0], self.land.at[1], sibling)

        def leap(self, i):
            self.leaps[i] = wires.go(self.view(0, mine, i), self.view(2, mine, i), across)

        def pass_on(self, q, i, to):
            return wires.go(self.view(2, q, i), self.view(2, q, i), to)

        def relay(self, q, i):
            self.last.append(wires.go(self.view(2, q, i), self.view(3, q, i), sibling))

        def first(self, i):
            self.leaps[i].wait_recv()
            for e in (1, 2):
                self.round[e, i] = self.pass_on(mine, i, (g ^ e, h))
            self.relay(mine, i)

        def second(self):
            self.round[1, 0].wait_recv()
            self.round[3, 0] = self.pass_on(mine ^ 1, 0, (g ^ 2, h))
            self.round[2, 1].wait_recv()
            self.round[3, 1] = self.pass_on(mine ^ 2, 1, (g ^ 1, h))

        def third(self):
            self.round[1, 1].wait_recv()
            self.relay(mine ^ 1, None)
            self.round[2, 0].wait_recv()
            self.relay(mine ^ 2, None)

        def fourth(self):
            self.round[3, 0].wait_recv()
            self.round[3, 1].wait_recv()
            self.relay(mine ^ 3, None)

        def done(self):
            for copy in self.last:
                copy.wait_recv()

        def drained(self):
            for copy in [self.core, *self.leaps.values(), *self.round.values(), *self.last]:
                wires.leave(copy)

    way_a = Weight(wa, cut_view(wa))
    way_u = Weight(wu, flat_view(wu))
    way_d = Weight(wd, flat_view(wd))
    exchange_start(0, row0)
    way_a.hand()
    way_a.leap(0)
    way_a.leap(1)
    x_wait = [wires.go(x_in.at[h ^ k], xs.at[k], (g, h ^ k)) for k in (2, 3, 1)]
    bias_wait = [wires.go(bias.at[0], bias.at[k], (g, h ^ k)) for k in (1, 2, 3)]
    spool.wait(own_wu)
    way_u.hand()
    way_u.leap(0)
    way_u.leap(1)
    r0 = exchange_end(0)
    way_a.first(0)
    way_a.first(1)
    way_a.second()
    way_a.third()
    way_a.fourth()
    spool.wait(own_x)
    for copy in x_wait:
        copy.wait_recv()
    ri0 = 1.0 / r0
    for k in range(nh):
        ab[block_rows(k), :] = (r0 * jnp.tanh(xs[k].astype(F32) * ri0)).astype(BF16)
    save_a = spool.go(ab, a_h)
    for copy in bias_wait:
        copy.wait_recv()

    def weight_a(k):
        return wa[k].reshape(width, width)

    def block(k):
        qkv[k] = (dot(ab[...], weight_a(k)[: 3 * hc, :], NT) + bias[k, 0:1, : 3 * hc]).astype(BF16)
        for j in range(heads):
            lo = j * HEAD_DIM
            keys = qkv[k, :, hc + lo: hc + lo + HEAD_DIM]
            vals = qkv[k, :, 2 * hc + lo: 2 * hc + lo + HEAD_DIM]
            q = qkv[k, :, lo: lo + HEAD_DIM] * BF16(scale)
            s = dot(q, keys, NT) + mask[...]
            top = jnp.max(s, axis=1, keepdims=True)
            e = jnp.exp(s - top)
            den = jnp.sum(e, axis=1, keepdims=True)
            p = (e * (1.0 / den)).astype(BF16)
            c_ref[k, :, lo: lo + HEAD_DIM] = dot(p, vals, NN)
            at = k * 8 + j
            lse[:, at: at + 1] = top + jnp.log(den)
        return span_top(c_ref[k], live[...])

    best = block(0)
    way_a.core.wait_recv()
    best = jnp.maximum(best, block(1))
    best = jnp.maximum(best, block(2))
    way_u.first(0)
    way_a.done()
    best = jnp.maximum(best, block(3))
    exchange_start(1, own_lane(lane_top(best)))
    way_u.first(1)
    spool.wait(own_wd)
    way_d.leap(0)
    way_d.leap(1)
    way_d.hand()
    save_wa = spool.go(wa, wa_h)
    turned = lse[...].T
    for k in range(nh):
        lse_t[k] = turned[k * 8:(k + 1) * 8, :]
    r1 = exchange_end(1)

    ri1 = 1.0 / r1
    for k in range(nh):
        cq[k] = (r1 * jnp.tanh(c_ref[k] * ri1)).astype(BF16)
        o1 = dot(cq[k], weight_a(k)[3 * hc:, :], NN)
        if k == 0:
            acc[...] = o1
        else:
            acc[...] += o1
    best = jnp.zeros((1, width), F32)
    for k in range(nh):
        rows = block_rows(k)
        nn, inv = norm_parts(xs[k].astype(F32) + (acc[rows, :] + bo))
        dz[rows, :] = nn
        inv1[rows, :] = inv
        y = nn * ga + ca
        y1[rows, :] = y
        best = jnp.maximum(best, span_top(y, live[rows, :]))
    way_u.second()
    exchange_start(2, own_lane(lane_top(best)))
    save_n1 = spool.go(dz, n1_h)
    way_u.third()
    way_d.first(0)
    spool.wait(save_a)
    r2 = exchange_end(2)
    ri2 = 1.0 / r2
    ab[...] = (r2 * jnp.tanh(y1[...] * ri2)).astype(BF16)

    def widen(k):
        f = dot(ab[...], wu[k], NN) + bias[k, 1:2, :]
        f_ref[k] = f
        return span_top(f * (0.5 * (1.0 + lax.erf(f * (0.5 ** 0.5)))), live[...])

    best = widen(0)
    way_u.core.wait_recv()
    best = jnp.maximum(best, widen(1))
    way_u.fourth()
    best = jnp.maximum(best, widen(2))
    way_u.done()
    best = jnp.maximum(best, widen(3))
    exchange_start(3, own_lane(lane_top(best)))
    way_d.first(1)
    own_dy = spool.go(dy_in.at[h], xl.at[0])
    dy_wait = [wires.go(dy_in.at[h ^ k], xl.at[k], (g, h ^ k)) for k in (2, 3, 1)]
    for k in range(nh):
        tr_b[:, block_rows(k)] = ab[block_rows(k), :].astype(F32).T.astype(BF16)
    load_a = spool.go(a_h, ab)
    r3 = exchange_end(3)
    ri3 = 1.0 / r3

    def squash(k):
        f = f_ref[k]
        cdf = 0.5 * (1.0 + lax.erf(f * (0.5 ** 0.5)))
        t = jnp.tanh(f * cdf * ri3)
        gq[k] = (r3 * t).astype(BF16)
        f_ref[k] = (cdf + f * (jnp.exp(-0.5 * f * f) * ROOT)) * (1.0 - t * t)

    def lower(k):
        o2 = dot(gq[k], wd[k], NN)
        if k == 0:
            acc[...] = o2
        else:
            acc[...] += o2

    squash(0)
    lower(0)
    squash(1)
    way_d.second()
    way_d.core.wait_recv()
    lower(1)
    way_d.third()
    squash(2)
    way_d.fourth()
    lower(2)
    squash(3)
    way_d.done()
    lower(3)
    spool.wait(own_dy)
    for copy in dy_wait:
        copy.wait_recv()
    spool.wait(save_n1)

    zero = jnp.zeros((1, width), F32)
    s_gb = s_cb = s_bd = zero
    for k in range(nh):
        rows = block_rows(k)
        nn, inv = norm_parts(y1[rows, :] + (acc[rows, :] + bd))
        out = nn * gb + cb
        if k == 0:
            out_own[...] = out
        else:
            out_stage[0, k - 1] = out.astype(BF16)
        dy = xl[k].astype(F32)
        d = norm_back(dy * gb, nn, inv)
        dz[rows, :] = d
        dzb[rows, :] = d.astype(BF16)
        tr[:, rows] = d.T.astype(BF16)
        s_gb = s_gb + jnp.sum(dy * nn, axis=0, keepdims=True)
        s_cb = s_cb + jnp.sum(dy, axis=0, keepdims=True)
        s_bd = s_bd + jnp.sum(d, axis=0, keepdims=True)
    tail = [wires.go(out_stage.at[0, k - 1], out_got.at[k - 1], (g, h ^ k)) for k in (2, 3, 1)]

    way_a.drained()
    spool.wait(save_wa)
    core = {}
    eighths = [(r * eighth, (r // 4, (r // 2) % 2, r % 2)) for r in range(8)]

    def spread(block_no, value):
        for at, spot in eighths:
            wa[(block_no, *spot)] = value[at: at + eighth, :].astype(BF16)

    def plain(chunk, k, value):
        spread(0, value)
        copy = pltpu.make_async_copy(wa.at[0], sums.at[chunk, k], plain_sem)
        copy.start()
        copy.wait()

    def home(chunk, index):
        if chunk < 2:
            return kept, (chunk, *index)
        first = pl.ds(2, 2) if isinstance(index[0], slice) else 2 + index[0]
        return wa, (first, *index[1:])

    def give(chunk, j, block_no, k, value):
        if not joined:
            plain(chunk, k, value)
            return
        spread(block_no, value)
        if (chunk, j) == (2, 0):
            pl.semaphore_wait(free_sem, 1)
        core[chunk, j] = wires.go(wa.at[block_no], got_core.at[chunk % 2, j], sibling)

    def keep(chunk, j, k, value):
        if not joined:
            plain(chunk, k, value)
            return
        core[chunk, j].wait_recv()
        for at, spot in eighths:
            ref, index = home(chunk, (j, *spot))
            ref[index] = (value[at: at + eighth, :] + got_core[(chunk % 2, j, *spot)].astype(F32)).astype(BF16)

    got = (None, got1, got2, got3, got4)
    pending = {}

    def region(way, step, last):
        index = []
        for axis in AXES:
            at = way.index(axis)
            if at == step:
                index.append(last)
            else:
                index.append(bit[axis] if at < step else slice(None))
        return index

    def send_step(chunk, step):
        if not joined:
            return
        pending[chunk, step] = []
        for i, way in enumerate(WAYS):
            axis = way[step]
            ref, index = home(chunk, region(way, step, 1 if axis == "y" else 1 - bit[axis]))
            src = ref.at[(*index, slice(None), pl.ds(i * third, third))]
            pending[chunk, step].append(wires.go(src, got[step + 1].at[chunk, i], where[axis]))

    def pump(chunk, step):
        if not joined:
            return
        for i, way in enumerate(WAYS):
            pending[chunk, step][i].wait_recv()
            cols = slice(i * third, (i + 1) * third)
            index = region(way, step, bit[way[step]])
            spots = [()]
            for item in index:
                if isinstance(item, slice):
                    spots = [s + (v,) for s in spots for v in (0, 1)]
            for spot in spots:
                left = iter(spot)
                ref, full = home(chunk, [next(left) if isinstance(item, slice) else item for item in index])
                value = (ref[(*full, slice(None), cols)].astype(F32)
                         + got[step + 1][(chunk, i, *spot)].astype(F32))
                if step == 3:
                    sums[chunk, :, cols] = value
                else:
                    ref[(*full, slice(None), cols)] = value.astype(BF16)
        if step < 3:
            send_step(chunk, step + 1)

    order = (1, 3, 0, 2)
    for j, k in enumerate((1, 3)):
        give(0, j, j, k, dot(tr[...], gq[k], NN))
    way_d.drained()
    load_wa = {}

    def units(k, first):
        d = (dot(dzb[...], wd[k], NT) * f_ref[k]).astype(BF16)
        df[...] = d
        small_now[0, pl.ds(4 + (h ^ k), 1), :] = jnp.sum(d.astype(F32), axis=0, keepdims=True)
        load_wa[k] = [
            spool.go(wa_h.at[(k, *spot)], wd.at[k, pl.ds(at, eighth), :]) for at, spot in eighths]
        part_sum = dot(df[...], wu[k], NT)
        if first:
            acc[...] = part_sum
        else:
            acc[...] += part_sum
        return dot(tr_b[...], df[...], NN)

    for j, k in enumerate((1, 3)):
        give(1, j, 2 + j, k, units(k, j == 0))
    load_n1 = spool.go(n1_h, f_ref.at[1])
    for j, k in enumerate((0, 2)):
        keep(0, j, k, dot(tr[...], gq[k], NN))
    if joined:
        pl.semaphore_signal(free_sem, inc=1, device_id=sibling, device_id_type=MESH)
    send_step(0, 0)
    for j, k in enumerate((0, 2)):
        keep(1, j, k, units(k, False))
    send_step(1, 0)

    spool.wait(load_n1)
    s_ga = s_ca = s_bo = zero
    for k in range(nh):
        rows = block_rows(k)
        t = jnp.tanh(y1[rows, :] * ri2)
        dy1 = dz[rows, :] + acc[rows, :] * (1.0 - t * t)
        nn = f_ref[1, rows, :]
        d = norm_back(dy1 * ga, nn, inv1[rows, :])
        dz[rows, :] = d
        dzb[rows, :] = d.astype(BF16)
        tr[:, rows] = d.T.astype(BF16)
        s_ga = s_ga + jnp.sum(dy1 * nn, axis=0, keepdims=True)
        s_ca = s_ca + jnp.sum(dy1, axis=0, keepdims=True)
        s_bo = s_bo + jnp.sum(d, axis=0, keepdims=True)
    for i, row in enumerate((s_ga, s_gb, s_bo, s_ca, s_bd, s_cb)):
        small_now[0, 8 + i: 9 + i, :] = row
    spool.wait(load_a)
    for k in range(nh):
        tr_b[:, block_rows(k)] = ab[block_rows(k), :].astype(F32).T.astype(BF16)

    def turn(i):
        k = order[i]
        for copy in load_wa[k]:
            spool.wait(copy)
        t = jnp.tanh(c_ref[k] * ri1)
        dc_ref[...] = (dot(dzb[...], wd[k, 3 * hc:, :], NT) * (1.0 - t * t)).astype(BF16)
        kt_ref[...] = qkv[k, :, hc: 2 * hc].astype(F32).T.astype(BF16)
        for j in range(heads):
            lo = j * HEAD_DIM
            keys = qkv[k, :, hc + lo: hc + lo + HEAD_DIM]
            vals = qkv[k, :, 2 * hc + lo: 2 * hc + lo + HEAD_DIM]
            q = qkv[k, :, lo: lo + HEAD_DIM] * BF16(scale)
            dc = dc_ref[:, lo: lo + HEAD_DIM]
            s = dot(keys, q, NT)
            p = jnp.where(live[...] > 0.0, jnp.exp(s - lse_t[k, j: j + 1, :]), 0.0)
            pd = p * dot(vals, dc, NT)
            delta = jnp.sum(pd, axis=0, keepdims=True)
            ds = (pd - p * delta).astype(BF16)
            dqkv[:, 2 * hc + lo: 2 * hc + lo + HEAD_DIM] = dot(p.astype(BF16), dc, NN).astype(BF16)
            dqkv[:, hc + lo: hc + lo + HEAD_DIM] = dot(ds, q, NN).astype(BF16)
            dqt_ref[lo: lo + HEAD_DIM, :] = dot(kt_ref[lo: lo + HEAD_DIM, :], ds, NN) * scale
        dqkv[:, :hc] = dqt_ref[...].T.astype(BF16)
        small_now[0, pl.ds(h ^ k, 1), : 3 * hc] = jnp.sum(dqkv[...].astype(F32), axis=0, keepdims=True)
        da = dot(dqkv[...], wd[k, : 3 * hc, :], NN)
        if i == 0:
            acc[...] = da
        else:
            acc[...] += da
        return jnp.concatenate([dot(tr_b[...], dqkv[...], NN), dot(tr[...], cq[k], NN)], axis=1)

    def sent(chunk, j):
        if joined:
            wires.leave(core[chunk, j])

    value = turn(0)
    sent(0, 0)
    give(2, 0, 0, order[0], value)
    pump(0, 0)
    value = turn(1)
    sent(0, 1)
    give(2, 1, 1, order[1], value)
    value = turn(2)
    sent(1, 0)
    keep(2, 0, 0, value)
    pump(1, 0)
    pump(0, 1)
    value = turn(3)
    sent(1, 1)
    keep(2, 1, 2, value)
    send_step(2, 0)
    small_ways = ("core", "y", "x", "z1", "z2")
    small_copy = {}

    def small_step(i):
        if not joined:
            return
        if i > 0:
            small_copy[i - 1].wait_recv()
            small_now[i] = small_now[i - 1] + small_got[i - 1]
        if i < 5:
            small_copy[i] = wires.go(small_now.at[i], small_got.at[i], where[small_ways[i]])

    small_step(0)
    for k in range(nh):
        rows = block_rows(k)
        t = jnp.tanh(xs[k].astype(F32) * ri0)
        d = dz[rows, :] + acc[rows, :] * (1.0 - t * t)
        if k == 0:
            dx_own[...] = d
        else:
            out_stage[1, k - 1] = d.astype(BF16)

    def send_dx(k):
        tail.append(wires.go(out_stage.at[1, k - 1], dx_got.at[k - 1], (g, h ^ k)))

    pump(0, 2)
    pump(1, 1)
    small_step(1)
    pump(2, 0)
    send_dx(2)
    small_step(2)
    pump(1, 2)
    pump(0, 3)
    pump(2, 1)
    send_dx(3)
    send_dx(1)
    small_step(3)
    pump(1, 3)
    pump(2, 2)
    small_step(4)
    pump(2, 3)
    small_step(5)
    small_sum[...] = small_now[5 if joined else 0]
    for copy in tail:
        copy.wait_recv()
    for stage in range(4):
        pltpu.make_async_copy(slots.at[stage], slots.at[stage], top_send.at[stage]).wait()
    wires.finish()
    spool.finish()


def layer(joined, lengths, order, ranges, x_in, dy_in, pw, ow, wu, wd, pb, ub, gains, shifts):
    nd, nh = lax.axis_size("dp"), lax.axis_size("head")
    slots, part, width = x_in.shape
    count = slots * part
    hc, fc = ow.shape[0], wu.shape[1]
    rows, third = width // 8, width // 3

    def shape(*dims, kind=F32):
        return jax.ShapeDtypeStruct(dims, kind)

    def half(*dims):
        return pltpu.VMEM(dims, BF16)

    def full(*dims):
        return pltpu.VMEM(dims, F32)

    smem = pl.BlockSpec(memory_space=pltpu.SMEM)
    return pl.pallas_call(
        functools.partial(layer_kernel, joined, nd, nh, part),
        out_shape=(
            shape(part, width), shape(nh - 1, part, width, kind=BF16), shape(part, width),
            shape(nh - 1, part, width, kind=BF16),
            shape(3, rows, width) if joined else shape(3, nh, 2, 2, 2, rows, width, kind=BF16),
            shape(16, width), shape(8, 128), shape(nh, 2, 2, 2, rows, width, kind=BF16), shape(count, width),
            shape(count, width, kind=BF16),
        ),
        in_specs=[smem] * 3 + [ANY] * 6 + [VM] * 4,
        out_specs=[VM, ANY, VM, ANY, VM if joined else ANY, VM, VM, ANY, ANY, ANY],
        scratch_shapes=[
            half(slots, part, width), half(slots, part, width), half(nh, 2, 2, 2, rows, width), half(nh, width, fc),
            half(nh, fc, width), full(nh, 8, fc), half(count, width), half(nh, count, 3 * hc), full(nh, count, hc),
            half(nh, count, hc), full(count, 128), full(nh, 8, count), full(count, 1), full(count, width),
            full(nh, count, fc), half(nh, count, fc), full(count, width), full(count, width), half(count, width),
            half(width, count), half(width, count), half(count, fc), half(count, hc), half(hc, count),
            full(hc, count), half(count, 3 * hc), full(count, 1), full(1, count),
            half(2, 2, 2, 2, 2, rows, width), half(2, 2, 2, 2, 2, rows, width),
            half(3, 3, 2, 2, 2, rows, third), half(3, 3, 2, 2, rows, third), half(3, 3, 2, rows, third),
            half(3, 3, rows, third), half(2, nh - 1, part, width), full(6, 16, width), full(5, 16, width),
            full(4, 1, 128), full(4, nd * nh - 1, 1, 128),
            pltpu.SemaphoreType.DMA((64,)), pltpu.SemaphoreType.DMA((112,)), pltpu.SemaphoreType.DMA((112,)),
            pltpu.SemaphoreType.DMA((4,)), pltpu.SemaphoreType.DMA((4,)), pltpu.SemaphoreType.REGULAR,
            pltpu.SemaphoreType.DMA,
        ],
        compiler_params=pltpu.CompilerParams(collective_id=0, has_side_effects=True, vmem_limit_bytes=LIMIT),
    )(lengths, order, ranges, x_in, dy_in, pw, ow, wu, wd, pb, ub, gains, shifts)


def finish_kernel(range_s, tops, out_own, out_got, dx_own, dx_got, sums, small,
                  out_o, dx_o, proj_o, bias_o, outw_o, up_o, off_o, down_o, gain_o, shift_o, range_o):
    h = lax.axis_index("head")
    nh = out_o.shape[0]
    hc = proj_o.shape[3]
    for own, got, dst in ((out_own, out_got, out_o), (dx_own, dx_got, dx_o)):
        dst[h] = own[...]
        for k in range(1, nh):
            dst[h ^ k] = got[k - 1].astype(F32)
    for i in range(3):
        proj_o[0, i] = sums[2, :, i * hc:(i + 1) * hc]

    def turned(value):
        rows = value.shape[0]
        filled = jnp.concatenate([value, jnp.zeros((-rows % 128, value.shape[1]), F32)], axis=0)
        return filled.T[:, :rows]

    outw_o[0] = turned(sums[2, :, 3 * hc:])
    up_o[0] = sums[1]
    down_o[0] = sums[0]
    width = small.shape[1]
    for k in range(nh):
        bias_o[0, 0:1, k * hc:(k + 1) * hc] = small[k:k + 1, :hc]
        bias_o[0, 1:2, k * hc:(k + 1) * hc] = small[k:k + 1, 2 * hc:3 * hc]
        off_o[0:1, k * width:(k + 1) * width] = small[4 + k:5 + k, :]
    gain_o[0] = small[8:10, :]
    shift_o[0] = small[10:14, :]
    for i in range(4):
        now = jnp.full((1, 1), range_s[0, i], F32)
        for m in range(4):
            now = DECAY * now + (1.0 - DECAY) * tops[i:i + 1, m:m + 1]
        range_o[0:1, i:i + 1] = now


def local(kernel, outs, out_specs, in_specs, scratch, *args):
    return pl.pallas_call(
        kernel,
        out_shape=outs,
        in_specs=in_specs,
        out_specs=out_specs,
        scratch_shapes=scratch,
        compiler_params=pltpu.CompilerParams(vmem_limit_bytes=LIMIT),
    )(*args)


def body(hidden_in, seq_lengths, batch_order, clip_ranges, proj_weight, proj_bias, out_weight,
         up_weight, up_bias, down_weight, norm_gains, out_biases, cotangent):
    nd, nh = lax.axis_size("dp"), lax.axis_size("head")
    slots, part, width = hidden_in.shape
    hc = proj_bias.shape[2]
    fc = up_bias.shape[1]
    joined = nd == 8
    out_own, out_got, dx_own, dx_got, sums, small, tops, _, _, _ = layer(
        joined, seq_lengths, batch_order, clip_ranges, hidden_in, cotangent, proj_weight[0].transpose(0, 2, 1),
        out_weight[0], up_weight[0], down_weight[0], proj_bias[0], up_bias, norm_gains[0], out_biases[0])

    def shape(*dims):
        return jax.ShapeDtypeStruct(dims, F32)

    if joined:
        outs = local(
            finish_kernel,
            (shape(slots, part, width), shape(slots, part, width), shape(1, 3, width // nd, hc),
             shape(1, 2, nh * hc), shape(1, hc, width // nd), shape(1, width // nd, fc), shape(1, nh * fc),
             shape(1, width // nd, fc), shape(1, 2, width), shape(1, 4, width), shape(1, 4)),
            [VM] * 11, [pl.BlockSpec(memory_space=pltpu.SMEM)] + [VM] * 7, [],
            clip_ranges, tops, out_own, out_got, dx_own, dx_got, sums, small)
        return (*outs[:7], outs[7].swapaxes(1, 2), *outs[8:])
    h = lax.axis_index("head")
    sums, small = settle_plain(sums.reshape(3, nh, width, width), small, h)
    index = h ^ jnp.arange(nh)
    hidden_out = jnp.concatenate([out_own[None], out_got.astype(F32)])[index]
    input_grad = jnp.concatenate([dx_own[None], dx_got.astype(F32)])[index]
    now = clip_ranges
    for m in range(slots):
        now = DECAY * now + (1.0 - DECAY) * tops[None, :4, m]
    return (
        hidden_out, input_grad, sums[2][:, : 3 * hc].reshape(1, -1, 3, hc).transpose(0, 2, 1, 3),
        jnp.stack([small[:4, :hc].reshape(-1), small[:4, 2 * hc: 3 * hc].reshape(-1)])[None],
        sums[2][:, 3 * hc:].T[None], sums[1][None], small[4:8].reshape(1, -1), sums[0].T[None],
        small[None, 8:10], small[None, 10:14], now,
    )


def solution(mesh):
    in_specs = (
        P("dp", "head", None), P("dp", None), P("dp", None), P(),
        P(None, None, None, "head"), P(None, None, "head"), P(None, "head", None),
        P(None, None, "head"), P(None, "head"), P(None, "head", None), P(), P(),
        P("dp", "head", None),
    )
    out_specs = (
        P("dp", "head", None), P("dp", "head", None), P(None, None, "dp", "head"), P(),
        P(None, "head", "dp"), P(None, "dp", "head"), P(), P(None, "head", "dp"), P(), P(), P(),
    )
    return jax.shard_map(body, mesh=mesh, in_specs=in_specs, out_specs=out_specs, check_vma=False)
```

```python
import functools
import jax
import jax.numpy as jnp
from jax import lax
from jax.experimental import pallas as pl
from jax.experimental.pallas import tpu as pltpu
from jax.sharding import PartitionSpec as P

HEAD_DIM = 64
EPSILON = 1e-06
MASK_FILL = -1e30
DECAY = 0.9
ROOT = 0.3989422804014327
MESH = pl.DeviceIdType.MESH
BF16 = jnp.bfloat16
F32 = jnp.float32
ANY = pl.BlockSpec(memory_space=pl.ANY)
VM = pl.BlockSpec(memory_space=pltpu.VMEM)


def remote(src, dst, send_sem, recv_sem, where):
    return pltpu.make_async_remote_copy(
        src_ref=src, dst_ref=dst, send_sem=send_sem, recv_sem=recv_sem,
        device_id=where, device_id_type=MESH,
    )


def settle_plain(grads, small, head_pos):
    order = head_pos ^ jnp.arange(grads.shape[1])
    part = lax.psum_scatter(grads[:, order].astype(F32), "head", scatter_dimension=1, tiled=True)[:, 0]
    return lax.psum_scatter(part, "dp", scatter_dimension=1, tiled=True), lax.psum(small, ("dp", "head"))


NN = ((1,), (0,))
NT = ((1,), (1,))
TN = ((0,), (0,))
LIMIT = 63 * 1024 * 1024


def dot(a, b, dims):
    return lax.dot_general(a, b, (dims, ((), ())), preferred_element_type=F32)


def norm_parts(z):
    centred = z - jnp.mean(z, axis=-1, keepdims=True)
    inv = lax.rsqrt(jnp.mean(centred * centred, axis=-1, keepdims=True) + EPSILON)
    return centred * inv, inv


def norm_back(dn, n, inv):
    return (dn - jnp.mean(dn, axis=-1, keepdims=True)
            - n * jnp.mean(dn * n, axis=-1, keepdims=True)) * inv


def span_top(values, live):
    return jnp.max(jnp.abs(values) * live, axis=0, keepdims=True)


def lane_top(row):
    return jnp.max(row, axis=1, keepdims=True)


class Wires:
    def __init__(self, send_sem, recv_sem):
        self.send_sem, self.recv_sem = send_sem, recv_sem
        self.sent = []
        self.count = 0

    def go(self, src, dst, where):
        i = self.count
        self.count += 1
        copy = remote(src, dst, self.send_sem.at[i], self.recv_sem.at[i], where)
        copy.start()
        self.sent.append(copy)
        return copy

    def leave(self, copy):
        copy.wait_send()
        self.sent = [item for item in self.sent if item is not copy]

    def finish(self):
        for copy in self.sent:
            copy.wait_send()


class Spool:
    def __init__(self, sem):
        self.sem = sem
        self.count = 0
        self.open = []

    def go(self, src, dst):
        copy = pltpu.make_async_copy(src, dst, self.sem.at[self.count])
        self.count += 1
        copy.start()
        self.open.append(copy)
        return copy

    def wait(self, copy):
        copy.wait()
        self.open = [item for item in self.open if item is not copy]

    def finish(self):
        for copy in self.open:
            copy.wait()


def own_micro(order_s, h, count):
    m_own = jnp.int32(0)
    for m in range(count):
        m_own = m_own + jnp.where(order_s[0, m] == h, jnp.int32(m), jnp.int32(0))
    return m_own


def range_of(start, tops, m_own, count):
    now = jnp.full((1, 1), start, F32)
    own = now
    for m in range(1, count):
        now = DECAY * now + (1.0 - DECAY) * tops[:, m - 1: m]
        own = jnp.where(m_own == m, now, own)
    return own


AXES = ("y", "z2", "z1", "x")
WAYS = (
    (("z1", "y", "z2", "x"), ("x", "z2", "z1", "y"), ("y", "x", "z2", "z1")),
    (("z1", "x", "y", "z2"), ("x", "y", "z1", "z2"), ("y", "x", "z2", "z1")),
    (("x", "y", "z1", "z2"), ("z1", "y", "x", "z2"), ("y", "x", "z2", "z1")),
)
SHARES = ((2, 2, 2), (2, 2, 2), (2, 2, 2))
PLAN = {
    "t3h2": ((0, 0, 0), (0, 0, 1), (0, 0, 2),),
    "t2e": ((1, 0, 1), (1, 0, 0),),
    "t1h0": ((1, 0, 2),),
    "t1h2": ((0, 1, 2),),
    "t1e": ((0, 1, 0),),
    "t0h2": ((0, 1, 1),),
}
TAIL = (
    (1, 1, 0), (0, 2, 2), (2, 0, 2), "S1", (0, 2, 1), (1, 1, 2), (0, 2, 0), (1, 1, 1), (2, 0, 1), (1, 2, 0),
    (0, 3, 2), "S2", (2, 0, 0), "dx2", (0, 3, 1), (1, 2, 1), (1, 2, 2), (2, 1, 2), "dx3", (2, 1, 1),
    (0, 3, 0), (1, 3, 0), "S3", (1, 3, 2), (1, 3, 1), (2, 2, 1), (2, 1, 0), "S4", (2, 2, 2), (2, 2, 0),
    (2, 3, 1), (2, 3, 2), "S5", (2, 3, 0),
)


def layer_kernel(joined, nd, nh, part, len_s, order_s, range_s, x_in, dy_in, pw_in, ow_in, wu_in, wd_in, pb_ref, ub_ref,
                 gain_ref, shift_ref,
                 out_own, out_got, dx_own, dx_got, sums, small_sum, tops_o, wa_h, n1_h, a_h,
                 xl, xs, wa, wu, wd, bias, ab, qkv, c_ref, cq, lse, lse_t, inv1, y1, f_ref, gq, acc, dz, dzb, tr, tr_b,
                 df, dc_ref, kt_ref, dqt_ref, dqkv, live, mask, kept, got_core, got1, got2, got3, got4, out_stage,
                 small_now, small_got, cand, slots,
                 spool_sem, send_sem, recv_sem, top_send, top_recv, free_sem, plain_sem):
    g = lax.axis_index("dp")
    h = lax.axis_index("head")
    n = nd * nh
    count, width = y1.shape
    hc = c_ref.shape[2]
    fc = f_ref.shape[2]
    heads = hc // HEAD_DIM
    micro = nh
    sixth = width // 6
    eighth = width // 8
    scale = HEAD_DIM ** -0.5
    lanes = lax.broadcasted_iota(jnp.int32, (1, 128), 1)
    bit = {"x": lax.rem(g, 2), "z1": lax.rem(g // 2, 2), "z2": g // 4, "y": 0}
    where = {"x": (g ^ 1, h), "z1": (g ^ 2, h), "z2": (g ^ 4, h), "y": (g, h ^ 2), "core": (g, h ^ 1)}
    sibling, across = where["core"], where["y"]

    def peer(d):
        return (g ^ (d // nh), h ^ lax.rem(d, nh))

    bar = pltpu.get_barrier_semaphore()

    def hello(d, carry):
        pl.semaphore_signal(bar, inc=1, device_id=peer(d), device_id_type=MESH)
        return carry

    lax.fori_loop(1, n, hello, 0)
    spool = Spool(spool_sem)
    wires = Wires(send_sem, recv_sem)
    load_x = spool.go(x_in, xl)
    load_w = []
    for i in range(4):
        for x in (0, 1):
            rows = pl.ds(x * eighth, eighth)
            load_w.append(spool.go(ow_in.at[rows, :] if i == 3 else pw_in.at[i, rows, :], wa.at[0, i // 2, i % 2, x]))
    own_x = spool.go(x_in.at[h], xs.at[0])
    own_wu = spool.go(wu_in, wu.at[0])
    own_wd = spool.go(wd_in, wd.at[0])

    def block_rows(k):
        return slice(k * part, (k + 1) * part)

    m_own = own_micro(order_s, h, micro)
    length = len_s[0, h]
    for k in range(nh):
        start = (h ^ k) * part
        rows = start + lax.broadcasted_iota(jnp.int32, (part, 1), 0)
        live[block_rows(k), :] = jnp.where(rows < length, 1.0, 0.0)
        cols = start + lax.broadcasted_iota(jnp.int32, (1, part), 1)
        mask[:, block_rows(k)] = jnp.where(cols < length, 0.0, MASK_FILL)
    bias[0] = jnp.zeros_like(bias[0])
    bias[0, 0:1, :hc] = pb_ref[0:1, :].astype(F32)
    bias[0, 0:1, 2 * hc:3 * hc] = pb_ref[1:2, :].astype(F32)
    bias[0, 1:2, :] = ub_ref[...].astype(F32)
    ga, gb = gain_ref[0:1, :].astype(F32), gain_ref[1:2, :].astype(F32)
    bo, ca, bd, cb = [shift_ref[i:i + 1, :].astype(F32) for i in range(4)]
    lse[...] = jnp.zeros_like(lse)
    small_now[0] = jnp.zeros_like(small_now[0])
    tops_o[4:8, :] = jnp.zeros((4, 128), F32)

    def exchange_start(stage, row):
        cand[stage] = row

        def send(d, carry):
            remote(cand.at[stage], slots.at[stage, d - 1], top_send.at[stage], top_recv.at[stage], peer(d)).start()
            return carry

        lax.fori_loop(1, n, send, 0)

    def exchange_end(stage):
        pltpu.make_async_copy(slots.at[stage], slots.at[stage], top_recv.at[stage]).wait()
        top = jnp.maximum(cand[stage], jnp.max(slots[stage], axis=0))
        tops_o[stage:stage + 1, :] = top
        return range_of(range_s[0, stage], top, m_own, micro)

    def own_lane(value):
        return jnp.where(lanes == m_own, value, 0.0)

    spool.wait(load_x)
    row0 = jnp.zeros((1, 128), F32)
    local_rows = h * part + lax.broadcasted_iota(jnp.int32, (part, 1), 0)
    for s in range(micro):
        lit = jnp.where(local_rows < len_s[0, s], 1.0, 0.0)
        top = lane_top(span_top(xl[s].astype(F32), lit))
        row0 = jnp.maximum(row0, jnp.where(lanes == own_micro(order_s, s, micro), top, 0.0))
    for copy in load_w:
        spool.wait(copy)

    pl.semaphore_wait(bar, n - 1)

    mine = lax.rem(g, 4)

    def cut_view(ref):
        return lambda slot, q, i: ref.at[slot, q // 2, lax.rem(q, 2)] if i is None else ref.at[
            slot, q // 2, lax.rem(q, 2), i]

    def flat_view(ref):
        def view(slot, q, i):
            size = 2 * eighth if i is None else eighth
            start = pl.multiple_of(q * (2 * eighth) + (0 if i is None else i) * eighth, eighth)
            return ref.at[slot, pl.ds(start, size), :]

        return view

    class Weight:
        def __init__(self, land, view):
            self.land, self.view = land, view
            self.leaps, self.round, self.last = {}, {}, []

        def hand(self):
            self.core = wires.go(self.land.at[0], self.land.at[1], sibling)

        def leap(self, i):
            self.leaps[i] = wires.go(self.view(0, mine, i), self.view(2, mine, i), across)

        def pass_on(self, q, i, to):
            return wires.go(self.view(2, q, i), self.view(2, q, i), to)

        def relay(self, q, i):
            self.last.append(wires.go(self.view(2, q, i), self.view(3, q, i), sibling))

        def first(self, i):
            self.leaps[i].wait_recv()
            for e in (1, 2):
                self.round[e, i] = self.pass_on(mine, i, (g ^ e, h))
            self.relay(mine, i)

        def second(self):
            self.round[1, 0].wait_recv()
            self.round[3, 0] = self.pass_on(mine ^ 1, 0, (g ^ 2, h))
            self.round[2, 1].wait_recv()
            self.round[3, 1] = self.pass_on(mine ^ 2, 1, (g ^ 1, h))

        def third(self):
            self.round[1, 1].wait_recv()
            self.relay(mine ^ 1, None)
            self.round[2, 0].wait_recv()
            self.relay(mine ^ 2, None)

        def fourth(self):
            self.round[3, 0].wait_recv()
            self.round[3, 1].wait_recv()
            self.relay(mine ^ 3, None)

        def done(self):
            for copy in self.last:
                copy.wait_recv()

        def drained(self):
            for copy in [self.core, *self.leaps.values(), *self.round.values(), *self.last]:
                wires.leave(copy)

    way_a = Weight(wa, cut_view(wa))
    way_u = Weight(wu, flat_view(wu))
    way_d = Weight(wd, flat_view(wd))
    exchange_start(0, row0)
    way_a.hand()
    way_a.leap(0)
    way_a.leap(1)
    x_wait = [wires.go(x_in.at[h ^ k], xs.at[k], (g, h ^ k)) for k in (2, 3, 1)]
    bias_wait = [wires.go(bias.at[0], bias.at[k], (g, h ^ k)) for k in (1, 2, 3)]
    spool.wait(own_wu)
    way_u.hand()
    way_u.leap(0)
    way_u.leap(1)
    r0 = exchange_end(0)
    way_a.first(0)
    way_a.first(1)
    way_a.second()
    way_a.third()
    way_a.fourth()
    spool.wait(own_x)
    for copy in x_wait:
        copy.wait_recv()
    ri0 = 1.0 / r0
    for k in range(nh):
        ab[block_rows(k), :] = (r0 * jnp.tanh(xs[k].astype(F32) * ri0)).astype(BF16)
    save_a = spool.go(ab, a_h)
    for copy in bias_wait:
        copy.wait_recv()

    def weight_a(k):
        return wa[k].reshape(width, width)

    def block(k):
        qkv[k] = (dot(ab[...], weight_a(k)[: 3 * hc, :], NT) + bias[k, 0:1, : 3 * hc]).astype(BF16)
        for j in range(heads):
            lo = j * HEAD_DIM
            keys = qkv[k, :, hc + lo: hc + lo + HEAD_DIM]
            vals = qkv[k, :, 2 * hc + lo: 2 * hc + lo + HEAD_DIM]
            q = qkv[k, :, lo: lo + HEAD_DIM] * BF16(scale)
            s = dot(q, keys, NT) + mask[...]
            top = jnp.max(s, axis=1, keepdims=True)
            e = jnp.exp(s - top)
            den = jnp.sum(e, axis=1, keepdims=True)
            p = (e * (1.0 / den)).astype(BF16)
            c_ref[k, :, lo: lo + HEAD_DIM] = dot(p, vals, NN)
            at = k * 8 + j
            lse[:, at: at + 1] = top + jnp.log(den)
        return span_top(c_ref[k], live[...])

    best = block(0)
    way_a.core.wait_recv()
    best = jnp.maximum(best, block(1))
    best = jnp.maximum(best, block(2))
    way_u.first(0)
    way_a.done()
    best = jnp.maximum(best, block(3))
    exchange_start(1, own_lane(lane_top(best)))
    way_u.first(1)
    spool.wait(own_wd)
    way_d.leap(0)
    way_d.leap(1)
    way_d.hand()
    save_wa = spool.go(wa, wa_h)
    turned = lse[...].T
    for k in range(nh):
        lse_t[k] = turned[k * 8:(k + 1) * 8, :]
    r1 = exchange_end(1)

    ri1 = 1.0 / r1
    for k in range(nh):
        cq[k] = (r1 * jnp.tanh(c_ref[k] * ri1)).astype(BF16)
        o1 = dot(cq[k], weight_a(k)[3 * hc:, :], NN)
        if k == 0:
            acc[...] = o1
        else:
            acc[...] += o1
    best = jnp.zeros((1, width), F32)
    for k in range(nh):
        rows = block_rows(k)
        nn, inv = norm_parts(xs[k].astype(F32) + (acc[rows, :] + bo))
        dz[rows, :] = nn
        inv1[rows, :] = inv
        y = nn * ga + ca
        y1[rows, :] = y
        best = jnp.maximum(best, span_top(y, live[rows, :]))
    way_u.second()
    exchange_start(2, own_lane(lane_top(best)))
    save_n1 = spool.go(dz, n1_h)
    way_u.third()
    way_d.first(0)
    own_dy = spool.go(dy_in.at[h], xl.at[0])
    dy_wait = [wires.go(dy_in.at[h ^ k], xl.at[k], (g, h ^ k)) for k in (2, 3, 1)]
    spool.wait(save_a)
    r2 = exchange_end(2)
    ri2 = 1.0 / r2
    ab[...] = (r2 * jnp.tanh(y1[...] * ri2)).astype(BF16)

    def widen(k):
        f = dot(ab[...], wu[k], NN) + bias[k, 1:2, :]
        f_ref[k] = f
        return span_top(f * (0.5 * (1.0 + lax.erf(f * (0.5 ** 0.5)))), live[...])

    best = widen(0)
    way_d.first(1)
    way_u.core.wait_recv()
    best = jnp.maximum(best, widen(1))
    way_u.fourth()
    best = jnp.maximum(best, widen(2))
    way_u.done()
    best = jnp.maximum(best, widen(3))
    exchange_start(3, own_lane(lane_top(best)))
    way_d.second()
    for k in range(nh):
        tr_b[:, block_rows(k)] = ab[block_rows(k), :].astype(F32).T.astype(BF16)
    load_a = spool.go(a_h, ab)
    r3 = exchange_end(3)
    ri3 = 1.0 / r3

    def squash(k):
        f = f_ref[k]
        cdf = 0.5 * (1.0 + lax.erf(f * (0.5 ** 0.5)))
        t = jnp.tanh(f * cdf * ri3)
        gq[k] = (r3 * t).astype(BF16)
        f_ref[k] = (cdf + f * (jnp.exp(-0.5 * f * f) * ROOT)) * (1.0 - t * t)

    def lower(k):
        o2 = dot(gq[k], wd[k], NN)
        if k == 0:
            acc[...] = o2
        else:
            acc[...] += o2

    squash(0)
    lower(0)
    squash(1)
    way_d.third()
    way_d.core.wait_recv()
    lower(1)
    squash(2)
    way_d.fourth()
    lower(2)
    squash(3)
    way_d.done()
    lower(3)
    spool.wait(own_dy)
    for copy in dy_wait:
        copy.wait_recv()
    spool.wait(save_n1)

    zero = jnp.zeros((1, width), F32)
    s_gb = s_cb = s_bd = zero
    for k in range(nh):
        rows = block_rows(k)
        nn, inv = norm_parts(y1[rows, :] + (acc[rows, :] + bd))
        out = nn * gb + cb
        if k == 0:
            out_own[...] = out
        else:
            out_stage[0, k - 1] = out.astype(BF16)
        dy = xl[k].astype(F32)
        d = norm_back(dy * gb, nn, inv)
        dz[rows, :] = d
        dzb[rows, :] = d.astype(BF16)
        tr[:, rows] = d.T.astype(BF16)
        s_gb = s_gb + jnp.sum(dy * nn, axis=0, keepdims=True)
        s_cb = s_cb + jnp.sum(dy, axis=0, keepdims=True)
        s_bd = s_bd + jnp.sum(d, axis=0, keepdims=True)
    tail = [wires.go(out_stage.at[0, k - 1], out_got.at[k - 1], (g, h ^ k)) for k in (2, 3, 1)]

    way_a.drained()
    spool.wait(save_wa)
    core = {}
    eighths = [(r * eighth, (r // 4, (r // 2) % 2, r % 2)) for r in range(8)]

    def spread(block_no, value):
        for at, spot in eighths:
            wa[(block_no, *spot)] = value[at: at + eighth, :].astype(BF16)

    def plain(chunk, k, value):
        spread(0, value)
        copy = pltpu.make_async_copy(wa.at[0], sums.at[chunk, k], plain_sem)
        copy.start()
        copy.wait()

    def home(chunk, index):
        if chunk < 2:
            return kept, (chunk, *index)
        first = pl.ds(2, 2) if isinstance(index[0], slice) else 2 + index[0]
        return wa, (first, *index[1:])

    def give(chunk, j, block_no, k, value):
        if not joined:
            plain(chunk, k, value)
            return
        spread(block_no, value)
        if (chunk, j) == (2, 1):
            pl.semaphore_wait(free_sem, 1)
        core[chunk, j] = wires.go(wa.at[block_no], got_core.at[chunk % 2, j], sibling)

    def keep(chunk, j, k, value):
        if not joined:
            plain(chunk, k, value)
            return
        core[chunk, j].wait_recv()
        for at, spot in eighths:
            ref, index = home(chunk, (j, *spot))
            ref[index] = (value[at: at + eighth, :] + got_core[(chunk % 2, j, *spot)].astype(F32)).astype(BF16)

    got = (None, got1, got2, got3, got4)
    pending = {}

    def region(way, step, last):
        index = []
        for axis in AXES:
            at = way.index(axis)
            if at == step:
                index.append(last)
            else:
                index.append(bit[axis] if at < step else slice(None))
        return index

    def columns(chunk, i):
        share = SHARES[chunk]
        return sum(share[:i]) * sixth, share[i] * sixth

    def send_way(chunk, step, i, j=None):
        axis = WAYS[chunk][i][step]
        index = region(WAYS[chunk][i], step, 1 if axis == "y" else 1 - bit[axis])
        dst = got[step + 1].at[chunk]
        if j is not None:
            index[0] = j
            dst = dst.at[j]
        ref, index = home(chunk, index)
        cols = pl.ds(*columns(chunk, i))
        dst = dst.at[(*[slice(None)] * (len(dst.shape) - 1), cols)]
        pending.setdefault((chunk, step, i), []).append(
            wires.go(ref.at[(*index, slice(None), cols)], dst, where[axis]))

    def send_first(chunk, j):
        if not joined:
            return
        for i, way in enumerate(WAYS[chunk]):
            if way[0] != "y":
                send_way(chunk, 0, i, j)
            elif j == 1:
                send_way(chunk, 0, i)

    def pump(chunk, step, *ways):
        for i in ways:
            way = WAYS[chunk][i]
            for copy in pending[chunk, step, i]:
                copy.wait_recv()
            start, size = columns(chunk, i)
            cols = slice(start, start + size)
            index = region(way, step, bit[way[step]])
            spots = [()]
            for item in index:
                if isinstance(item, slice):
                    spots = [s + (v,) for s in spots for v in (0, 1)]
            for spot in spots:
                left = iter(spot)
                ref, full = home(chunk, [next(left) if isinstance(item, slice) else item for item in index])
                value = (ref[(*full, slice(None), cols)].astype(F32)
                         + got[step + 1][(chunk, *spot, slice(None), cols)].astype(F32))
                if step == 3:
                    sums[chunk, :, cols] = value
                else:
                    ref[(*full, slice(None), cols)] = value.astype(BF16)
            if step < 3:
                send_way(chunk, step + 1, i)

    def pumps(place):
        if joined:
            for job in PLAN.get(place, ()):
                pump(*job)

    for k in (3, 1):
        give(0, k // 2, k // 2, k, dot(tr[...], gq[k], NN))
    way_d.drained()
    load_wa = {}
    turns = (3, 2, 1, 0)

    def units(k, first):
        d = (dot(dzb[...], wd[k], NT) * f_ref[k]).astype(BF16)
        df[...] = d
        small_now[0, pl.ds(4 + (h ^ k), 1), :] = jnp.sum(d.astype(F32), axis=0, keepdims=True)
        load_wa[k] = [
            spool.go(wa_h.at[(k, *spot)], wd.at[k, pl.ds(at, eighth), :]) for at, spot in eighths]
        part_sum = dot(df[...], wu[k], NT)
        if first:
            acc[...] = part_sum
        else:
            acc[...] += part_sum
        return dot(tr_b[...], df[...], NN)

    for k in (3, 1):
        give(1, k // 2, 2 + k // 2, k, units(k, k == 3))
    load_n1 = spool.go(n1_h, f_ref.at[1])
    for k in (2, 0):
        keep(0, k // 2, k, dot(tr[...], gq[k], NN))
        send_first(0, k // 2)
    if joined:
        pl.semaphore_signal(free_sem, inc=1, device_id=sibling, device_id_type=MESH)
    for k in (2, 0):
        keep(1, k // 2, k, units(k, False))
        send_first(1, k // 2)
        pumps(f"u{k}")

    spool.wait(load_n1)
    s_ga = s_ca = s_bo = zero
    for k in range(nh):
        rows = block_rows(k)
        t = jnp.tanh(y1[rows, :] * ri2)
        dy1 = dz[rows, :] + acc[rows, :] * (1.0 - t * t)
        nn = f_ref[1, rows, :]
        d = norm_back(dy1 * ga, nn, inv1[rows, :])
        dz[rows, :] = d
        dzb[rows, :] = d.astype(BF16)
        tr[:, rows] = d.T.astype(BF16)
        s_ga = s_ga + jnp.sum(dy1 * nn, axis=0, keepdims=True)
        s_ca = s_ca + jnp.sum(dy1, axis=0, keepdims=True)
        s_bo = s_bo + jnp.sum(d, axis=0, keepdims=True)
    for i, row in enumerate((s_ga, s_gb, s_bo, s_ca, s_bd, s_cb)):
        small_now[0, 8 + i: 9 + i, :] = row
    spool.wait(load_a)
    for k in range(nh):
        tr_b[:, block_rows(k)] = ab[block_rows(k), :].astype(F32).T.astype(BF16)
    pumps("norm")

    def turn(i):
        k = turns[i]
        for copy in load_wa[k]:
            spool.wait(copy)
        t = jnp.tanh(c_ref[k] * ri1)
        dc_ref[...] = (dot(dzb[...], wd[k, 3 * hc:, :], NT) * (1.0 - t * t)).astype(BF16)
        kt_ref[...] = qkv[k, :, hc: 2 * hc].astype(F32).T.astype(BF16)
        for j in range(heads):
            lo = j * HEAD_DIM
            keys = qkv[k, :, hc + lo: hc + lo + HEAD_DIM]
            vals = qkv[k, :, 2 * hc + lo: 2 * hc + lo + HEAD_DIM]
            q = qkv[k, :, lo: lo + HEAD_DIM] * BF16(scale)
            dc = dc_ref[:, lo: lo + HEAD_DIM]
            s = dot(keys, q, NT)
            p = jnp.where(live[...] > 0.0, jnp.exp(s - lse_t[k, j: j + 1, :]), 0.0)
            pd = p * dot(vals, dc, NT)
            delta = jnp.sum(pd, axis=0, keepdims=True)
            ds = (pd - p * delta).astype(BF16)
            dqkv[:, 2 * hc + lo: 2 * hc + lo + HEAD_DIM] = dot(p.astype(BF16), dc, NN).astype(BF16)
            dqkv[:, hc + lo: hc + lo + HEAD_DIM] = dot(ds, q, NN).astype(BF16)
            dqt_ref[lo: lo + HEAD_DIM, :] = dot(kt_ref[lo: lo + HEAD_DIM, :], ds, NN) * scale
            pumps(f"t{k}h{j}")
        dqkv[:, :hc] = dqt_ref[...].T.astype(BF16)
        small_now[0, pl.ds(h ^ k, 1), : 3 * hc] = jnp.sum(dqkv[...].astype(F32), axis=0, keepdims=True)
        da = dot(dqkv[...], wd[k, : 3 * hc, :], NN)
        if i == 0:
            acc[...] = da
        else:
            acc[...] += da
        return jnp.concatenate([dot(tr_b[...], dqkv[...], NN), dot(tr[...], cq[k], NN)], axis=1)

    def sent(chunk, j):
        if joined:
            wires.leave(core[chunk, j])

    for i, k in enumerate(turns):
        j = k // 2
        value = turn(i)
        if k % 2:
            sent(0, j)
            give(2, j, j, k, value)
        else:
            sent(1, j)
            keep(2, j, k, value)
            send_first(2, j)
        pumps(f"t{k}e")
    small_ways = ("core", "y", "x", "z1", "z2")
    small_copy = {}

    def small_step(i):
        if not joined:
            return
        if i > 0:
            small_copy[i - 1].wait_recv()
            small_now[i] = small_now[i - 1] + small_got[i - 1]
        if i < 5:
            small_copy[i] = wires.go(small_now.at[i], small_got.at[i], where[small_ways[i]])

    small_step(0)
    for k in range(nh):
        rows = block_rows(k)
        t = jnp.tanh(xs[k].astype(F32) * ri0)
        d = dz[rows, :] + acc[rows, :] * (1.0 - t * t)
        if k == 0:
            dx_own[...] = d
        else:
            out_stage[1, k - 1] = d.astype(BF16)

    def send_dx(k):
        tail.append(wires.go(out_stage.at[1, k - 1], dx_got.at[k - 1], (g, h ^ k)))

    for job in TAIL:
        if job == "dx2":
            send_dx(2)
        elif job == "dx3":
            send_dx(3)
            send_dx(1)
        elif isinstance(job, str):
            small_step(int(job[1:]))
        elif joined:
            pump(*job)
    small_sum[...] = small_now[5 if joined else 0]
    for copy in tail:
        copy.wait_recv()
    for stage in range(4):
        pltpu.make_async_copy(slots.at[stage], slots.at[stage], top_send.at[stage]).wait()
    wires.finish()
    spool.finish()


def layer(joined, lengths, order, ranges, x_in, dy_in, pw, ow, wu, wd, pb, ub, gains, shifts):
    nd, nh = lax.axis_size("dp"), lax.axis_size("head")
    slots, part, width = x_in.shape
    count = slots * part
    hc, fc = ow.shape[0], wu.shape[1]
    rows = width // 8

    def shape(*dims, kind=F32):
        return jax.ShapeDtypeStruct(dims, kind)

    def half(*dims):
        return pltpu.VMEM(dims, BF16)

    def full(*dims):
        return pltpu.VMEM(dims, F32)

    smem = pl.BlockSpec(memory_space=pltpu.SMEM)
    return pl.pallas_call(
        functools.partial(layer_kernel, joined, nd, nh, part),
        out_shape=(
            shape(part, width), shape(nh - 1, part, width, kind=BF16), shape(part, width),
            shape(nh - 1, part, width, kind=BF16),
            shape(3, rows, width) if joined else shape(3, nh, 2, 2, 2, rows, width, kind=BF16),
            shape(16, width), shape(8, 128), shape(nh, 2, 2, 2, rows, width, kind=BF16), shape(count, width),
            shape(count, width, kind=BF16),
        ),
        in_specs=[smem] * 3 + [ANY] * 6 + [VM] * 4,
        out_specs=[VM, ANY, VM, ANY, VM if joined else ANY, VM, VM, ANY, ANY, ANY],
        scratch_shapes=[
            half(slots, part, width), half(slots, part, width), half(nh, 2, 2, 2, rows, width), half(nh, width, fc),
            half(nh, fc, width), full(nh, 8, fc), half(count, width), half(nh, count, 3 * hc), full(nh, count, hc),
            half(nh, count, hc), full(count, 128), full(nh, 8, count), full(count, 1), full(count, width),
            full(nh, count, fc), half(nh, count, fc), full(count, width), full(count, width), half(count, width),
            half(width, count), half(width, count), half(count, fc), half(count, hc), half(hc, count),
            full(hc, count), half(count, 3 * hc), full(count, 1), full(1, count),
            half(2, 2, 2, 2, 2, rows, width), half(2, 2, 2, 2, 2, rows, width),
            half(3, 2, 2, 2, rows, width), half(3, 2, 2, rows, width), half(3, 2, rows, width),
            half(3, rows, width), half(2, nh - 1, part, width), full(6, 16, width), full(5, 16, width),
            full(4, 1, 128), full(4, nd * nh - 1, 1, 128),
            pltpu.SemaphoreType.DMA((64,)), pltpu.SemaphoreType.DMA((120,)), pltpu.SemaphoreType.DMA((120,)),
            pltpu.SemaphoreType.DMA((4,)), pltpu.SemaphoreType.DMA((4,)), pltpu.SemaphoreType.REGULAR,
            pltpu.SemaphoreType.DMA,
        ],
        compiler_params=pltpu.CompilerParams(collective_id=0, has_side_effects=True, vmem_limit_bytes=LIMIT),
    )(lengths, order, ranges, x_in, dy_in, pw, ow, wu, wd, pb, ub, gains, shifts)


def finish_kernel(range_s, tops, out_own, out_got, dx_own, dx_got, sums, small,
                  out_o, dx_o, proj_o, bias_o, outw_o, up_o, off_o, down_o, gain_o, shift_o, range_o):
    h = lax.axis_index("head")
    nh = out_o.shape[0]
    hc = proj_o.shape[3]
    for own, got, dst in ((out_own, out_got, out_o), (dx_own, dx_got, dx_o)):
        dst[h] = own[...]
        for k in range(1, nh):
            dst[h ^ k] = got[k - 1].astype(F32)
    for i in range(3):
        proj_o[0, i] = sums[2, :, i * hc:(i + 1) * hc]

    def turned(value):
        rows = value.shape[0]
        filled = jnp.concatenate([value, jnp.zeros((-rows % 128, value.shape[1]), F32)], axis=0)
        return filled.T[:, :rows]

    outw_o[0] = turned(sums[2, :, 3 * hc:])
    up_o[0] = sums[1]
    down_o[0] = sums[0]
    width = small.shape[1]
    for k in range(nh):
        bias_o[0, 0:1, k * hc:(k + 1) * hc] = small[k:k + 1, :hc]
        bias_o[0, 1:2, k * hc:(k + 1) * hc] = small[k:k + 1, 2 * hc:3 * hc]
        off_o[0:1, k * width:(k + 1) * width] = small[4 + k:5 + k, :]
    gain_o[0] = small[8:10, :]
    shift_o[0] = small[10:14, :]
    for i in range(4):
        now = jnp.full((1, 1), range_s[0, i], F32)
        for m in range(4):
            now = DECAY * now + (1.0 - DECAY) * tops[i:i + 1, m:m + 1]
        range_o[0:1, i:i + 1] = now


def local(kernel, outs, out_specs, in_specs, scratch, *args):
    return pl.pallas_call(
        kernel,
        out_shape=outs,
        in_specs=in_specs,
        out_specs=out_specs,
        scratch_shapes=scratch,
        compiler_params=pltpu.CompilerParams(vmem_limit_bytes=LIMIT),
    )(*args)


def body(hidden_in, seq_lengths, batch_order, clip_ranges, proj_weight, proj_bias, out_weight,
         up_weight, up_bias, down_weight, norm_gains, out_biases, cotangent):
    nd, nh = lax.axis_size("dp"), lax.axis_size("head")
    slots, part, width = hidden_in.shape
    hc = proj_bias.shape[2]
    fc = up_bias.shape[1]
    joined = nd == 8
    out_own, out_got, dx_own, dx_got, sums, small, tops, _, _, _ = layer(
        joined, seq_lengths, batch_order, clip_ranges, hidden_in, cotangent, proj_weight[0].transpose(0, 2, 1),
        out_weight[0], up_weight[0], down_weight[0], proj_bias[0], up_bias, norm_gains[0], out_biases[0])

    def shape(*dims):
        return jax.ShapeDtypeStruct(dims, F32)

    if joined:
        outs = local(
            finish_kernel,
            (shape(slots, part, width), shape(slots, part, width), shape(1, 3, width // nd, hc),
             shape(1, 2, nh * hc), shape(1, hc, width // nd), shape(1, width // nd, fc), shape(1, nh * fc),
             shape(1, width // nd, fc), shape(1, 2, width), shape(1, 4, width), shape(1, 4)),
            [VM] * 11, [pl.BlockSpec(memory_space=pltpu.SMEM)] + [VM] * 7, [],
            clip_ranges, tops, out_own, out_got, dx_own, dx_got, sums, small)
        return (*outs[:7], outs[7].swapaxes(1, 2), *outs[8:])
    h = lax.axis_index("head")
    sums, small = settle_plain(sums.reshape(3, nh, width, width), small, h)
    index = h ^ jnp.arange(nh)
    hidden_out = jnp.concatenate([out_own[None], out_got.astype(F32)])[index]
    input_grad = jnp.concatenate([dx_own[None], dx_got.astype(F32)])[index]
    now = clip_ranges
    for m in range(slots):
        now = DECAY * now + (1.0 - DECAY) * tops[None, :4, m]
    return (
        hidden_out, input_grad, sums[2][:, : 3 * hc].reshape(1, -1, 3, hc).transpose(0, 2, 1, 3),
        jnp.stack([small[:4, :hc].reshape(-1), small[:4, 2 * hc: 3 * hc].reshape(-1)])[None],
        sums[2][:, 3 * hc:].T[None], sums[1][None], small[4:8].reshape(1, -1), sums[0].T[None],
        small[None, 8:10], small[None, 10:14], now,
    )


def solution(mesh):
    in_specs = (
        P("dp", "head", None), P("dp", None), P("dp", None), P(),
        P(None, None, None, "head"), P(None, None, "head"), P(None, "head", None),
        P(None, None, "head"), P(None, "head"), P(None, "head", None), P(), P(),
        P("dp", "head", None),
    )
    out_specs = (
        P("dp", "head", None), P("dp", "head", None), P(None, None, "dp", "head"), P(),
        P(None, "head", "dp"), P(None, "dp", "head"), P(), P(None, "head", "dp"), P(), P(), P(),
    )
    return jax.shard_map(body, mesh=mesh, in_specs=in_specs, out_specs=out_specs, check_vma=False)
```

```python
import functools
import jax
import jax.numpy as jnp
from jax import lax
from jax.experimental import pallas as pl
from jax.experimental.pallas import tpu as pltpu
from jax.sharding import PartitionSpec as P

HEAD_DIM = 64
EPSILON = 1e-06
MASK_FILL = -1e30
DECAY = 0.9
ROOT = 0.3989422804014327
MESH = pl.DeviceIdType.MESH
BF16 = jnp.bfloat16
F32 = jnp.float32
ANY = pl.BlockSpec(memory_space=pl.ANY)
VM = pl.BlockSpec(memory_space=pltpu.VMEM)


def remote(src, dst, send_sem, recv_sem, where):
    return pltpu.make_async_remote_copy(
        src_ref=src, dst_ref=dst, send_sem=send_sem, recv_sem=recv_sem,
        device_id=where, device_id_type=MESH,
    )


def settle_plain(grads, small, head_pos):
    order = head_pos ^ jnp.arange(grads.shape[1])
    part = lax.psum_scatter(grads[:, order].astype(F32), "head", scatter_dimension=1, tiled=True)[:, 0]
    return lax.psum_scatter(part, "dp", scatter_dimension=1, tiled=True), lax.psum(small, ("dp", "head"))


NN = ((1,), (0,))
NT = ((1,), (1,))
TN = ((0,), (0,))
LIMIT = 63 * 1024 * 1024


def dot(a, b, dims):
    return lax.dot_general(a, b, (dims, ((), ())), preferred_element_type=F32)


def norm_parts(z):
    centred = z - jnp.mean(z, axis=-1, keepdims=True)
    inv = lax.rsqrt(jnp.mean(centred * centred, axis=-1, keepdims=True) + EPSILON)
    return centred * inv, inv


def norm_back(dn, n, inv):
    return (dn - jnp.mean(dn, axis=-1, keepdims=True)
            - n * jnp.mean(dn * n, axis=-1, keepdims=True)) * inv


def span_top(values, live):
    return jnp.max(jnp.abs(values) * live, axis=0, keepdims=True)


def lane_top(row):
    return jnp.max(row, axis=1, keepdims=True)


class Wires:
    def __init__(self, send_sem, recv_sem):
        self.send_sem, self.recv_sem = send_sem, recv_sem
        self.sent = []
        self.count = 0

    def go(self, src, dst, where):
        i = self.count
        self.count += 1
        copy = remote(src, dst, self.send_sem.at[i], self.recv_sem.at[i], where)
        copy.start()
        self.sent.append(copy)
        return copy

    def leave(self, copy):
        rest = [item for item in self.sent if item is not copy]
        if len(rest) < len(self.sent):
            copy.wait_send()
        self.sent = rest

    def drain(self, late):
        for copy in self.sent[:-late]:
            copy.wait_send()
        self.sent = self.sent[-late:]

    def finish(self):
        for copy in self.sent:
            copy.wait_send()


class Spool:
    def __init__(self, sem):
        self.sem = sem
        self.count = 0
        self.open = []

    def go(self, src, dst):
        copy = pltpu.make_async_copy(src, dst, self.sem.at[self.count])
        self.count += 1
        copy.start()
        self.open.append(copy)
        return copy

    def wait(self, copy):
        copy.wait()
        self.open = [item for item in self.open if item is not copy]

    def finish(self):
        for copy in self.open:
            copy.wait()


def own_micro(order_s, h, count):
    m_own = jnp.int32(0)
    for m in range(count):
        m_own = m_own + jnp.where(order_s[0, m] == h, jnp.int32(m), jnp.int32(0))
    return m_own


def range_of(start, tops, m_own, count):
    now = jnp.full((1, 1), start, F32)
    own = now
    for m in range(1, count):
        now = DECAY * now + (1.0 - DECAY) * tops[:, m - 1: m]
        own = jnp.where(m_own == m, now, own)
    return own


AXES = ("y", "z2", "z1", "x")
WAYS = (
    (("y", "x", "z1", "z2"), ("z1", "x", "y", "z2"), ("x", "y", "z1", "z2")),
    (("y", "x", "z2", "z1"), ("x", "z1", "z2", "y"), ("z1", "x", "y", "z2")),
    (("x", "y", "z1", "z2"), ("y", "z1", "x", "z2"), ("y", "z1", "x", "z2")),
)
SHARES = ((1, 3, 2), (2, 2, 2), (2, 2, 2))
PLAN = {
    "norm": ((0, 0, 0),),
    "t3h2": ((0, 0, 2),),
    "t2h0": ((0, 0, 1),),
    "t2h1": ((1, 0, 0),),
    "t2e": ((1, 0, 1),),
    "t1h0": ((0, 1, 2), (0, 1, 0),),
    "t1h2": ((1, 0, 2),),
    "t0h1": ((1, 1, 1), (0, 1, 1),),
    "t0e": ((0, 2, 2), (2, 0, 1), (0, 2, 0),),
}
TAIL = (
    (1, 1, 0), "S1", (1, 2, 1), (0, 3, 2), (2, 0, 2), (2, 1, 1), (1, 1, 2), (0, 3, 0), (0, 2, 1), "S2",
    (1, 3, 1), (2, 0, 0), "dx2", (1, 2, 0), "dx3", (2, 1, 2), (1, 2, 2), (2, 2, 1), "S3", (1, 3, 0),
    (0, 3, 1), (2, 2, 2), (2, 1, 0), "S4", (1, 3, 2), (2, 3, 1), (2, 2, 0), (2, 3, 2), "S5", (2, 3, 0),
)


def layer_kernel(joined, nd, nh, part, len_s, order_s, range_s, x_in, dy_in, pw_in, ow_in, wu_in, wd_in, pb_ref, ub_ref,
                 gain_ref, shift_ref,
                 out_own, out_got, dx_own, dx_got, sums, small_sum, tops_o, wa_h, n1_h, a_h,
                 xl, xs, wa, wu, wd, bias, ab, qkv, c_ref, cq, lse, lse_t, inv1, y1, f_ref, gq, acc, dz, dzb, tr, tr_b,
                 df, dc_ref, kt_ref, dqt_ref, dqkv, live, mask, kept, got_core, got1, got2, got3, got4, out_stage,
                 small_now, small_got, cand, slots,
                 spool_sem, send_sem, recv_sem, top_send, top_recv, free_sem, plain_sem):
    g = lax.axis_index("dp")
    h = lax.axis_index("head")
    n = nd * nh
    count, width = y1.shape
    hc = c_ref.shape[2]
    fc = f_ref.shape[2]
    heads = hc // HEAD_DIM
    micro = nh
    sixth = width // 6
    eighth = width // 8
    scale = HEAD_DIM ** -0.5
    lanes = lax.broadcasted_iota(jnp.int32, (1, 128), 1)
    bit = {"x": lax.rem(g, 2), "z1": lax.rem(g // 2, 2), "z2": g // 4, "y": 0}
    where = {"x": (g ^ 1, h), "z1": (g ^ 2, h), "z2": (g ^ 4, h), "y": (g, h ^ 2), "core": (g, h ^ 1)}
    sibling, across = where["core"], where["y"]

    def peer(d):
        return (g ^ (d // nh), h ^ lax.rem(d, nh))

    bar = pltpu.get_barrier_semaphore()

    def hello(d, carry):
        pl.semaphore_signal(bar, inc=1, device_id=peer(n - d), device_id_type=MESH)
        return carry

    lax.fori_loop(1, n, hello, 0)
    spool = Spool(spool_sem)
    wires = Wires(send_sem, recv_sem)
    load_x = spool.go(x_in, xl)
    load_w = []
    for i in range(4):
        for x in (0, 1):
            rows = pl.ds(x * eighth, eighth)
            load_w.append(spool.go(ow_in.at[rows, :] if i == 3 else pw_in.at[i, rows, :], wa.at[0, i // 2, i % 2, x]))
    own_x = spool.go(x_in.at[h], xs.at[0])
    own_wu = spool.go(wu_in, wu.at[0])
    own_wd = spool.go(wd_in, wd.at[0])

    def block_rows(k):
        return slice(k * part, (k + 1) * part)

    m_own = own_micro(order_s, h, micro)
    length = len_s[0, h]
    for k in range(nh):
        start = (h ^ k) * part
        rows = start + lax.broadcasted_iota(jnp.int32, (part, 1), 0)
        live[block_rows(k), :] = jnp.where(rows < length, 1.0, 0.0)
        cols = start + lax.broadcasted_iota(jnp.int32, (1, part), 1)
        mask[:, block_rows(k)] = jnp.where(cols < length, 0.0, MASK_FILL)
    bias[0] = jnp.zeros_like(bias[0])
    bias[0, 0:1, :hc] = pb_ref[0:1, :].astype(F32)
    bias[0, 0:1, 2 * hc:3 * hc] = pb_ref[1:2, :].astype(F32)
    bias[0, 1:2, :] = ub_ref[...].astype(F32)
    ga, gb = gain_ref[0:1, :].astype(F32), gain_ref[1:2, :].astype(F32)
    bo, ca, bd, cb = [shift_ref[i:i + 1, :].astype(F32) for i in range(4)]
    lse[...] = jnp.zeros_like(lse)
    small_now[0] = jnp.zeros_like(small_now[0])
    tops_o[4:8, :] = jnp.zeros((4, 128), F32)

    def exchange_start(stage, row):
        cand[stage] = row

        def send(d, carry):
            remote(cand.at[stage], slots.at[stage, d - 1], top_send.at[stage], top_recv.at[stage], peer(n - d)).start()
            return carry

        lax.fori_loop(1, n, send, 0)

    def exchange_end(stage):
        pltpu.make_async_copy(slots.at[stage], slots.at[stage], top_recv.at[stage]).wait()
        top = jnp.maximum(cand[stage], jnp.max(slots[stage], axis=0))
        tops_o[stage:stage + 1, :] = top
        return range_of(range_s[0, stage], top, m_own, micro)

    def own_lane(value):
        return jnp.where(lanes == m_own, value, 0.0)

    spool.wait(load_x)
    row0 = jnp.zeros((1, 128), F32)
    local_rows = h * part + lax.broadcasted_iota(jnp.int32, (part, 1), 0)
    for s in range(micro):
        lit = jnp.where(local_rows < len_s[0, s], 1.0, 0.0)
        top = lane_top(span_top(xl[s].astype(F32), lit))
        row0 = jnp.maximum(row0, jnp.where(lanes == own_micro(order_s, s, micro), top, 0.0))
    for copy in load_w:
        spool.wait(copy)

    pl.semaphore_wait(bar, n - 1)

    mine = lax.rem(g, 4)

    def cut_view(ref):
        return lambda slot, q, i: ref.at[slot, q // 2, lax.rem(q, 2)] if i is None else ref.at[
            slot, q // 2, lax.rem(q, 2), i]

    def flat_view(ref):
        def view(slot, q, i):
            size = 2 * eighth if i is None else eighth
            start = pl.multiple_of(q * (2 * eighth) + (0 if i is None else i) * eighth, eighth)
            return ref.at[slot, pl.ds(start, size), :]

        return view

    class Weight:
        def __init__(self, land, view):
            self.land, self.view = land, view
            self.leaps, self.round, self.last = {}, {}, []

        def hand(self):
            self.core = wires.go(self.land.at[0], self.land.at[1], sibling)

        def leap(self, i):
            self.leaps[i] = wires.go(self.view(0, mine, i), self.view(2, mine, i), across)

        def pass_on(self, q, i, to):
            return wires.go(self.view(2, q, i), self.view(2, q, i), to)

        def relay(self, q, i):
            self.last.append(wires.go(self.view(2, q, i), self.view(3, q, i), sibling))

        def first(self, i):
            self.leaps[i].wait_recv()
            for e in (1, 2):
                self.round[e, i] = self.pass_on(mine, i, (g ^ e, h))
            self.relay(mine, i)

        def second(self):
            self.round[1, 0].wait_recv()
            self.round[3, 0] = self.pass_on(mine ^ 1, 0, (g ^ 2, h))
            self.round[2, 1].wait_recv()
            self.round[3, 1] = self.pass_on(mine ^ 2, 1, (g ^ 1, h))

        def third(self):
            self.round[1, 1].wait_recv()
            self.relay(mine ^ 1, None)
            self.round[2, 0].wait_recv()
            self.relay(mine ^ 2, None)

        def fourth(self):
            self.round[3, 0].wait_recv()
            self.round[3, 1].wait_recv()
            self.relay(mine ^ 3, None)

        def done(self):
            for copy in self.last:
                copy.wait_recv()

        def drained(self):
            for copy in [self.core, *self.leaps.values(), *self.round.values(), *self.last]:
                wires.leave(copy)

    way_a = Weight(wa, cut_view(wa))
    way_u = Weight(wu, flat_view(wu))
    way_d = Weight(wd, flat_view(wd))
    exchange_start(0, row0)
    way_a.hand()
    way_a.leap(0)
    way_a.leap(1)
    x_wait = [wires.go(x_in.at[h ^ k], xs.at[k], (g, h ^ k)) for k in (2, 3, 1)]
    bias_wait = [wires.go(bias.at[0], bias.at[k], (g, h ^ k)) for k in (1, 2, 3)]
    spool.wait(own_wu)
    way_u.hand()
    way_u.leap(0)
    way_u.leap(1)
    r0 = exchange_end(0)
    way_a.first(0)
    way_a.first(1)
    way_a.second()
    way_a.third()
    way_a.fourth()
    spool.wait(own_x)
    for copy in x_wait:
        copy.wait_recv()
    ri0 = 1.0 / r0
    for k in range(nh):
        ab[block_rows(k), :] = (r0 * jnp.tanh(xs[k].astype(F32) * ri0)).astype(BF16)
    save_a = spool.go(ab, a_h)
    for copy in bias_wait:
        copy.wait_recv()

    def weight_a(k):
        return wa[k].reshape(width, width)

    def block(k):
        qkv[k] = (dot(ab[...], weight_a(k)[: 3 * hc, :], NT) + bias[k, 0:1, : 3 * hc]).astype(BF16)
        for j in range(heads):
            lo = j * HEAD_DIM
            keys = qkv[k, :, hc + lo: hc + lo + HEAD_DIM]
            vals = qkv[k, :, 2 * hc + lo: 2 * hc + lo + HEAD_DIM]
            q = qkv[k, :, lo: lo + HEAD_DIM] * BF16(scale)
            s = dot(q, keys, NT) + mask[...]
            top = jnp.max(s, axis=1, keepdims=True)
            e = jnp.exp(s - top)
            den = jnp.sum(e, axis=1, keepdims=True)
            p = (e * (1.0 / den)).astype(BF16)
            c_ref[k, :, lo: lo + HEAD_DIM] = dot(p, vals, NN)
            at = k * 8 + j
            lse[:, at: at + 1] = top + jnp.log(den)
        return span_top(c_ref[k], live[...])

    best = block(0)
    way_a.core.wait_recv()
    best = jnp.maximum(best, block(1))
    way_u.first(0)
    best = jnp.maximum(best, block(2))
    way_a.done()
    best = jnp.maximum(best, block(3))
    exchange_start(1, own_lane(lane_top(best)))
    way_u.first(1)
    spool.wait(own_wd)
    way_d.leap(0)
    way_d.leap(1)
    way_d.hand()
    save_wa = spool.go(wa, wa_h)
    turned = lse[...].T
    for k in range(nh):
        lse_t[k] = turned[k * 8:(k + 1) * 8, :]
    r1 = exchange_end(1)
    way_d.first(0)

    ri1 = 1.0 / r1
    for k in range(nh):
        cq[k] = (r1 * jnp.tanh(c_ref[k] * ri1)).astype(BF16)
        o1 = dot(cq[k], weight_a(k)[3 * hc:, :], NN)
        if k == 0:
            acc[...] = o1
        else:
            acc[...] += o1
    best = jnp.zeros((1, width), F32)
    for k in range(nh):
        rows = block_rows(k)
        nn, inv = norm_parts(xs[k].astype(F32) + (acc[rows, :] + bo))
        dz[rows, :] = nn
        inv1[rows, :] = inv
        y = nn * ga + ca
        y1[rows, :] = y
        best = jnp.maximum(best, span_top(y, live[rows, :]))
    exchange_start(2, own_lane(lane_top(best)))
    way_u.second()
    save_n1 = spool.go(dz, n1_h)
    way_u.third()
    way_d.first(1)
    own_dy = spool.go(dy_in.at[h], xl.at[0])
    dy_wait = [wires.go(dy_in.at[h ^ k], xl.at[k], (g, h ^ k)) for k in (2, 3, 1)]
    spool.wait(save_a)
    for k in range(nh):
        t = jnp.tanh(c_ref[k] * ri1)
        c_ref[k] = 1.0 - t * t
    r2 = exchange_end(2)
    ri2 = 1.0 / r2
    ab[...] = (r2 * jnp.tanh(y1[...] * ri2)).astype(BF16)

    def widen(k):
        f = dot(ab[...], wu[k], NN) + bias[k, 1:2, :]
        f_ref[k] = f
        return span_top(f * (0.5 * (1.0 + lax.erf(f * (0.5 ** 0.5)))), live[...])

    best = widen(0)
    way_u.core.wait_recv()
    best = jnp.maximum(best, widen(1))
    way_u.fourth()
    best = jnp.maximum(best, widen(2))
    way_u.done()
    best = jnp.maximum(best, widen(3))
    exchange_start(3, own_lane(lane_top(best)))
    way_d.second()
    for k in range(nh):
        tr_b[:, block_rows(k)] = ab[block_rows(k), :].astype(F32).T.astype(BF16)
    load_a = spool.go(a_h, ab)
    for k in range(nh):
        f = f_ref[k]
        cdf = 0.5 * (1.0 + lax.erf(f * (0.5 ** 0.5)))
        gq[k] = (cdf + f * (jnp.exp(-0.5 * f * f) * ROOT)).astype(BF16)
        f_ref[k] = f * cdf
    wires.drain(24)
    r3 = exchange_end(3)
    ri3 = 1.0 / r3

    def squash(k):
        t = jnp.tanh(f_ref[k] * ri3)
        f_ref[k] = gq[k].astype(F32) * (1.0 - t * t)
        gq[k] = (r3 * t).astype(BF16)

    def lower(k):
        o2 = dot(gq[k], wd[k], NN)
        if k == 0:
            acc[...] = o2
        else:
            acc[...] += o2

    squash(0)
    lower(0)
    squash(1)
    way_d.third()
    way_d.core.wait_recv()
    lower(1)
    squash(2)
    way_d.fourth()
    lower(2)
    squash(3)
    way_d.done()
    lower(3)
    spool.wait(own_dy)
    for copy in dy_wait:
        copy.wait_recv()
    spool.wait(save_n1)

    zero = jnp.zeros((1, width), F32)
    s_gb = s_cb = s_bd = zero
    tail = []
    for k in (2, 3, 1, 0):
        rows = block_rows(k)
        nn, inv = norm_parts(y1[rows, :] + (acc[rows, :] + bd))
        out = nn * gb + cb
        if k == 0:
            out_own[...] = out
        else:
            out_stage[0, k - 1] = out.astype(BF16)
            tail.append(wires.go(out_stage.at[0, k - 1], out_got.at[k - 1], (g, h ^ k)))
        dy = xl[k].astype(F32)
        d = norm_back(dy * gb, nn, inv)
        dz[rows, :] = d
        dzb[rows, :] = d.astype(BF16)
        tr[:, rows] = d.T.astype(BF16)
        s_gb = s_gb + jnp.sum(dy * nn, axis=0, keepdims=True)
        s_cb = s_cb + jnp.sum(dy, axis=0, keepdims=True)
        s_bd = s_bd + jnp.sum(d, axis=0, keepdims=True)

    way_a.drained()
    spool.wait(save_wa)
    core = {}
    eighths = [(r * eighth, (r // 4, (r // 2) % 2, r % 2)) for r in range(8)]

    def spread(block_no, value):
        for at, spot in eighths:
            wa[(block_no, *spot)] = value[at: at + eighth, :].astype(BF16)

    def plain(chunk, k, value):
        spread(0, value)
        copy = pltpu.make_async_copy(wa.at[0], sums.at[chunk, k], plain_sem)
        copy.start()
        copy.wait()

    def home(chunk, index):
        if chunk < 2:
            return kept, (chunk, *index)
        first = pl.ds(2, 2) if isinstance(index[0], slice) else 2 + index[0]
        return wa, (first, *index[1:])

    def give(chunk, j, block_no, k, value):
        if not joined:
            plain(chunk, k, value)
            return
        spread(block_no, value)
        if (chunk, j) == (2, 1):
            pl.semaphore_wait(free_sem, 1)
        core[chunk, j] = wires.go(wa.at[block_no], got_core.at[chunk % 2, j], sibling)

    def keep(chunk, j, k, value):
        if not joined:
            plain(chunk, k, value)
            return
        core[chunk, j].wait_recv()
        for at, spot in eighths:
            ref, index = home(chunk, (j, *spot))
            ref[index] = (value[at: at + eighth, :] + got_core[(chunk % 2, j, *spot)].astype(F32)).astype(BF16)

    got = (None, got1, got2, got3, got4)
    pending = {}

    def region(way, step, last):
        index = []
        for axis in AXES:
            at = way.index(axis)
            if at == step:
                index.append(last)
            else:
                index.append(bit[axis] if at < step else slice(None))
        return index

    def columns(chunk, i):
        share = SHARES[chunk]
        return sum(share[:i]) * sixth, share[i] * sixth

    def send_way(chunk, step, i, j=None):
        axis = WAYS[chunk][i][step]
        index = region(WAYS[chunk][i], step, 1 if axis == "y" else 1 - bit[axis])
        dst = got[step + 1].at[chunk]
        if j is not None:
            index[0] = j
            dst = dst.at[j]
        ref, index = home(chunk, index)
        cols = pl.ds(*columns(chunk, i))
        dst = dst.at[(*[slice(None)] * (len(dst.shape) - 1), cols)]
        pending.setdefault((chunk, step, i), []).append(
            wires.go(ref.at[(*index, slice(None), cols)], dst, where[axis]))

    def send_first(chunk, j):
        if not joined:
            return
        for i, way in enumerate(WAYS[chunk]):
            if way[0] != "y":
                send_way(chunk, 0, i, j)
            elif j == 1:
                send_way(chunk, 0, i)

    def pump(chunk, step, *ways):
        for i in ways:
            way = WAYS[chunk][i]
            for copy in pending[chunk, step, i]:
                copy.wait_recv()
            start, size = columns(chunk, i)
            cols = slice(start, start + size)
            index = region(way, step, bit[way[step]])
            spots = [()]
            for item in index:
                if isinstance(item, slice):
                    spots = [s + (v,) for s in spots for v in (0, 1)]
            for spot in spots:
                left = iter(spot)
                ref, full = home(chunk, [next(left) if isinstance(item, slice) else item for item in index])
                value = (ref[(*full, slice(None), cols)].astype(F32)
                         + got[step + 1][(chunk, *spot, slice(None), cols)].astype(F32))
                if step == 3:
                    sums[chunk, :, cols] = value
                else:
                    ref[(*full, slice(None), cols)] = value.astype(BF16)
            if step < 3:
                send_way(chunk, step + 1, i)

    def pumps(place):
        if joined:
            for job in PLAN.get(place, ()):
                pump(*job)

    for k in (3, 1):
        give(0, k // 2, k // 2, k, dot(tr[...], gq[k], NN))
    way_d.drained()
    load_wa = {}
    turns = (3, 2, 1, 0)

    def units(k, first):
        d = (dot(dzb[...], wd[k], NT) * f_ref[k]).astype(BF16)
        df[...] = d
        small_now[0, pl.ds(4 + (h ^ k), 1), :] = jnp.sum(d.astype(F32), axis=0, keepdims=True)
        load_wa[k] = [
            spool.go(wa_h.at[(k, *spot)], wd.at[k, pl.ds(at, eighth), :]) for at, spot in eighths]
        part_sum = dot(df[...], wu[k], NT)
        if first:
            acc[...] = part_sum
        else:
            acc[...] += part_sum
        return dot(tr_b[...], df[...], NN)

    for k in (3, 1):
        give(1, k // 2, 2 + k // 2, k, units(k, k == 3))
    load_n1 = spool.go(n1_h, f_ref.at[1])
    for k in (2, 0):
        keep(0, k // 2, k, dot(tr[...], gq[k], NN))
        send_first(0, k // 2)
    if joined:
        pl.semaphore_signal(free_sem, inc=1, device_id=sibling, device_id_type=MESH)
    for k in (2, 0):
        keep(1, k // 2, k, units(k, False))
        send_first(1, k // 2)
        pumps(f"u{k}")

    spool.wait(load_n1)
    s_ga = s_ca = s_bo = zero
    for k in range(nh):
        rows = block_rows(k)
        t = jnp.tanh(y1[rows, :] * ri2)
        dy1 = dz[rows, :] + acc[rows, :] * (1.0 - t * t)
        nn = f_ref[1, rows, :]
        d = norm_back(dy1 * ga, nn, inv1[rows, :])
        dz[rows, :] = d
        dzb[rows, :] = d.astype(BF16)
        tr[:, rows] = d.T.astype(BF16)
        s_ga = s_ga + jnp.sum(dy1 * nn, axis=0, keepdims=True)
        s_ca = s_ca + jnp.sum(dy1, axis=0, keepdims=True)
        s_bo = s_bo + jnp.sum(d, axis=0, keepdims=True)
    for i, row in enumerate((s_ga, s_gb, s_bo, s_ca, s_bd, s_cb)):
        small_now[0, 8 + i: 9 + i, :] = row
    spool.wait(load_a)
    for k in range(nh):
        tr_b[:, block_rows(k)] = ab[block_rows(k), :].astype(F32).T.astype(BF16)
    pumps("norm")

    def turn(i):
        k = turns[i]
        for copy in load_wa[k]:
            spool.wait(copy)
        dc_ref[...] = (dot(dzb[...], wd[k, 3 * hc:, :], NT) * c_ref[k]).astype(BF16)
        kt_ref[...] = qkv[k, :, hc: 2 * hc].astype(F32).T.astype(BF16)
        for j in range(heads):
            lo = j * HEAD_DIM
            keys = qkv[k, :, hc + lo: hc + lo + HEAD_DIM]
            vals = qkv[k, :, 2 * hc + lo: 2 * hc + lo + HEAD_DIM]
            q = qkv[k, :, lo: lo + HEAD_DIM] * BF16(scale)
            dc = dc_ref[:, lo: lo + HEAD_DIM]
            s = dot(keys, q, NT)
            p = jnp.where(live[...] > 0.0, jnp.exp(s - lse_t[k, j: j + 1, :]), 0.0)
            pd = p * dot(vals, dc, NT)
            delta = jnp.sum(pd, axis=0, keepdims=True)
            ds = (pd - p * delta).astype(BF16)
            dqkv[:, 2 * hc + lo: 2 * hc + lo + HEAD_DIM] = dot(p.astype(BF16), dc, NN).astype(BF16)
            dqkv[:, hc + lo: hc + lo + HEAD_DIM] = dot(ds, q, NN).astype(BF16)
            dqt_ref[lo: lo + HEAD_DIM, :] = dot(kt_ref[lo: lo + HEAD_DIM, :], ds, NN) * scale
            pumps(f"t{k}h{j}")
        dqkv[:, :hc] = dqt_ref[...].T.astype(BF16)
        small_now[0, pl.ds(h ^ k, 1), : 3 * hc] = jnp.sum(dqkv[...].astype(F32), axis=0, keepdims=True)
        da = dot(dqkv[...], wd[k, : 3 * hc, :], NN)
        if i == 0:
            acc[...] = da
        else:
            acc[...] += da
        return jnp.concatenate([dot(tr_b[...], dqkv[...], NN), dot(tr[...], cq[k], NN)], axis=1)

    def sent(chunk, j):
        if joined:
            wires.leave(core[chunk, j])

    for i, k in enumerate(turns):
        j = k // 2
        value = turn(i)
        if k % 2:
            sent(0, j)
            give(2, j, j, k, value)
        else:
            sent(1, j)
            keep(2, j, k, value)
            send_first(2, j)
        pumps(f"t{k}e")
    small_ways = ("core", "y", "x", "z1", "z2")
    small_copy = {}

    def small_step(i):
        if not joined:
            return
        if i > 0:
            small_copy[i - 1].wait_recv()
            small_now[i] = small_now[i - 1] + small_got[i - 1]
        if i < 5:
            small_copy[i] = wires.go(small_now.at[i], small_got.at[i], where[small_ways[i]])

    small_step(0)
    for k in (2, 3, 1, 0):
        rows = block_rows(k)
        t = jnp.tanh(xs[k].astype(F32) * ri0)
        d = dz[rows, :] + acc[rows, :] * (1.0 - t * t)
        if k == 0:
            dx_own[...] = d
        else:
            out_stage[1, k - 1] = d.astype(BF16)

    def send_dx(k):
        tail.append(wires.go(out_stage.at[1, k - 1], dx_got.at[k - 1], (g, h ^ k)))

    for stage in range(4):
        pltpu.make_async_copy(slots.at[stage], slots.at[stage], top_send.at[stage]).wait()
    for job in TAIL:
        wires.drain(16)
        if job == "dx2":
            send_dx(2)
        elif job == "dx3":
            send_dx(3)
            send_dx(1)
        elif isinstance(job, str):
            small_step(int(job[1:]))
        elif joined:
            pump(*job)
    small_sum[...] = small_now[5 if joined else 0]
    for copy in tail:
        copy.wait_recv()
    wires.finish()
    spool.finish()


def layer(joined, lengths, order, ranges, x_in, dy_in, pw, ow, wu, wd, pb, ub, gains, shifts):
    nd, nh = lax.axis_size("dp"), lax.axis_size("head")
    slots, part, width = x_in.shape
    count = slots * part
    hc, fc = ow.shape[0], wu.shape[1]
    rows = width // 8

    def shape(*dims, kind=F32):
        return jax.ShapeDtypeStruct(dims, kind)

    def half(*dims):
        return pltpu.VMEM(dims, BF16)

    def full(*dims):
        return pltpu.VMEM(dims, F32)

    smem = pl.BlockSpec(memory_space=pltpu.SMEM)
    return pl.pallas_call(
        functools.partial(layer_kernel, joined, nd, nh, part),
        out_shape=(
            shape(part, width), shape(nh - 1, part, width, kind=BF16), shape(part, width),
            shape(nh - 1, part, width, kind=BF16),
            shape(3, rows, width) if joined else shape(3, nh, 2, 2, 2, rows, width, kind=BF16),
            shape(16, width), shape(8, 128), shape(nh, 2, 2, 2, rows, width, kind=BF16), shape(count, width),
            shape(count, width, kind=BF16),
        ),
        in_specs=[smem] * 3 + [ANY] * 6 + [VM] * 4,
        out_specs=[VM, ANY, VM, ANY, VM if joined else ANY, VM, VM, ANY, ANY, ANY],
        scratch_shapes=[
            half(slots, part, width), half(slots, part, width), half(nh, 2, 2, 2, rows, width), half(nh, width, fc),
            half(nh, fc, width), full(nh, 8, fc), half(count, width), half(nh, count, 3 * hc), full(nh, count, hc),
            half(nh, count, hc), full(count, 128), full(nh, 8, count), full(count, 1), full(count, width),
            full(nh, count, fc), half(nh, count, fc), full(count, width), full(count, width), half(count, width),
            half(width, count), half(width, count), half(count, fc), half(count, hc), half(hc, count),
            full(hc, count), half(count, 3 * hc), full(count, 1), full(1, count),
            half(2, 2, 2, 2, 2, rows, width), half(2, 2, 2, 2, 2, rows, width),
            half(3, 2, 2, 2, rows, width), half(3, 2, 2, rows, width), half(3, 2, rows, width),
            half(3, rows, width), half(2, nh - 1, part, width), full(6, 16, width), full(5, 16, width),
            full(4, 1, 128), full(4, nd * nh - 1, 1, 128),
            pltpu.SemaphoreType.DMA((64,)), pltpu.SemaphoreType.DMA((120,)), pltpu.SemaphoreType.DMA((120,)),
            pltpu.SemaphoreType.DMA((4,)), pltpu.SemaphoreType.DMA((4,)), pltpu.SemaphoreType.REGULAR,
            pltpu.SemaphoreType.DMA,
        ],
        compiler_params=pltpu.CompilerParams(collective_id=0, has_side_effects=True, vmem_limit_bytes=LIMIT),
    )(lengths, order, ranges, x_in, dy_in, pw, ow, wu, wd, pb, ub, gains, shifts)


def finish_kernel(range_s, tops, out_own, out_got, dx_own, dx_got, sums, small,
                  out_o, dx_o, proj_o, bias_o, outw_o, up_o, off_o, down_o, gain_o, shift_o, range_o):
    h = lax.axis_index("head")
    nh = out_o.shape[0]
    hc = proj_o.shape[3]
    for own, got, dst in ((out_own, out_got, out_o), (dx_own, dx_got, dx_o)):
        dst[h] = own[...]
        for k in range(1, nh):
            dst[h ^ k] = got[k - 1].astype(F32)
    for i in range(3):
        proj_o[0, i] = sums[2, :, i * hc:(i + 1) * hc]

    def turned(value):
        rows = value.shape[0]
        filled = jnp.concatenate([value, jnp.zeros((-rows % 128, value.shape[1]), F32)], axis=0)
        return filled.T[:, :rows]

    outw_o[0] = turned(sums[2, :, 3 * hc:])
    up_o[0] = sums[1]
    down_o[0] = sums[0]
    width = small.shape[1]
    for k in range(nh):
        bias_o[0, 0:1, k * hc:(k + 1) * hc] = small[k:k + 1, :hc]
        bias_o[0, 1:2, k * hc:(k + 1) * hc] = small[k:k + 1, 2 * hc:3 * hc]
        off_o[0:1, k * width:(k + 1) * width] = small[4 + k:5 + k, :]
    gain_o[0] = small[8:10, :]
    shift_o[0] = small[10:14, :]
    for i in range(4):
        now = jnp.full((1, 1), range_s[0, i], F32)
        for m in range(4):
            now = DECAY * now + (1.0 - DECAY) * tops[i:i + 1, m:m + 1]
        range_o[0:1, i:i + 1] = now


def local(kernel, outs, out_specs, in_specs, scratch, *args):
    return pl.pallas_call(
        kernel,
        out_shape=outs,
        in_specs=in_specs,
        out_specs=out_specs,
        scratch_shapes=scratch,
        compiler_params=pltpu.CompilerParams(vmem_limit_bytes=LIMIT),
    )(*args)


def body(hidden_in, seq_lengths, batch_order, clip_ranges, proj_weight, proj_bias, out_weight,
         up_weight, up_bias, down_weight, norm_gains, out_biases, cotangent):
    nd, nh = lax.axis_size("dp"), lax.axis_size("head")
    slots, part, width = hidden_in.shape
    hc = proj_bias.shape[2]
    fc = up_bias.shape[1]
    joined = nd == 8
    out_own, out_got, dx_own, dx_got, sums, small, tops, _, _, _ = layer(
        joined, seq_lengths, batch_order, clip_ranges, hidden_in, cotangent, proj_weight[0].transpose(0, 2, 1),
        out_weight[0], up_weight[0], down_weight[0], proj_bias[0], up_bias, norm_gains[0], out_biases[0])

    def shape(*dims):
        return jax.ShapeDtypeStruct(dims, F32)

    if joined:
        outs = local(
            finish_kernel,
            (shape(slots, part, width), shape(slots, part, width), shape(1, 3, width // nd, hc),
             shape(1, 2, nh * hc), shape(1, hc, width // nd), shape(1, width // nd, fc), shape(1, nh * fc),
             shape(1, width // nd, fc), shape(1, 2, width), shape(1, 4, width), shape(1, 4)),
            [VM] * 11, [pl.BlockSpec(memory_space=pltpu.SMEM)] + [VM] * 7, [],
            clip_ranges, tops, out_own, out_got, dx_own, dx_got, sums, small)
        return (*outs[:7], outs[7].swapaxes(1, 2), *outs[8:])
    h = lax.axis_index("head")
    sums, small = settle_plain(sums.reshape(3, nh, width, width), small, h)
    index = h ^ jnp.arange(nh)
    hidden_out = jnp.concatenate([out_own[None], out_got.astype(F32)])[index]
    input_grad = jnp.concatenate([dx_own[None], dx_got.astype(F32)])[index]
    now = clip_ranges
    for m in range(slots):
        now = DECAY * now + (1.0 - DECAY) * tops[None, :4, m]
    return (
        hidden_out, input_grad, sums[2][:, : 3 * hc].reshape(1, -1, 3, hc).transpose(0, 2, 1, 3),
        jnp.stack([small[:4, :hc].reshape(-1), small[:4, 2 * hc: 3 * hc].reshape(-1)])[None],
        sums[2][:, 3 * hc:].T[None], sums[1][None], small[4:8].reshape(1, -1), sums[0].T[None],
        small[None, 8:10], small[None, 10:14], now,
    )


def solution(mesh):
    in_specs = (
        P("dp", "head", None), P("dp", None), P("dp", None), P(),
        P(None, None, None, "head"), P(None, None, "head"), P(None, "head", None),
        P(None, None, "head"), P(None, "head"), P(None, "head", None), P(), P(),
        P("dp", "head", None),
    )
    out_specs = (
        P("dp", "head", None), P("dp", "head", None), P(None, None, "dp", "head"), P(),
        P(None, "head", "dp"), P(None, "dp", "head"), P(), P(None, "head", "dp"), P(), P(), P(),
    )
    return jax.shard_map(body, mesh=mesh, in_specs=in_specs, out_specs=out_specs, check_vma=False)
```

```python
import functools
import jax
import jax.numpy as jnp
from jax import lax
from jax.experimental import pallas as pl
from jax.experimental.pallas import tpu as pltpu
from jax.sharding import PartitionSpec as P

HEAD_DIM = 64
EPSILON = 1e-06
MASK_FILL = -1e30
DECAY = 0.9
ROOT = 0.3989422804014327
MESH = pl.DeviceIdType.MESH
BF16 = jnp.bfloat16
F32 = jnp.float32
ANY = pl.BlockSpec(memory_space=pl.ANY)
VM = pl.BlockSpec(memory_space=pltpu.VMEM)


def remote(src, dst, send_sem, recv_sem, where):
    return pltpu.make_async_remote_copy(
        src_ref=src, dst_ref=dst, send_sem=send_sem, recv_sem=recv_sem,
        device_id=where, device_id_type=MESH,
    )


def settle_plain(grads, small, head_pos):
    order = head_pos ^ jnp.arange(grads.shape[1])
    part = lax.psum_scatter(grads[:, order].astype(F32), "head", scatter_dimension=1, tiled=True)[:, 0]
    return lax.psum_scatter(part, "dp", scatter_dimension=1, tiled=True), lax.psum(small, ("dp", "head"))


NN = ((1,), (0,))
NT = ((1,), (1,))
TN = ((0,), (0,))
LIMIT = 63 * 1024 * 1024


def dot(a, b, dims):
    return lax.dot_general(a, b, (dims, ((), ())), preferred_element_type=F32)


def norm_parts(z):
    centred = z - jnp.mean(z, axis=-1, keepdims=True)
    inv = lax.rsqrt(jnp.mean(centred * centred, axis=-1, keepdims=True) + EPSILON)
    return centred * inv, inv


def norm_back(dn, n, inv):
    return (dn - jnp.mean(dn, axis=-1, keepdims=True)
            - n * jnp.mean(dn * n, axis=-1, keepdims=True)) * inv


def span_top(values, live):
    return jnp.max(jnp.abs(values) * live, axis=0, keepdims=True)


def lane_top(row):
    return jnp.max(row, axis=1, keepdims=True)


class Wires:
    def __init__(self, send_sem, recv_sem):
        self.send_sem, self.recv_sem = send_sem, recv_sem
        self.sent = []
        self.count = 0

    def go(self, src, dst, where):
        i = self.count
        self.count += 1
        copy = remote(src, dst, self.send_sem.at[i], self.recv_sem.at[i], where)
        copy.start()
        self.sent.append(copy)
        return copy

    def leave(self, copy):
        rest = [item for item in self.sent if item is not copy]
        if len(rest) < len(self.sent):
            copy.wait_send()
        self.sent = rest

    def drain(self, late):
        for copy in self.sent[:-late]:
            copy.wait_send()
        self.sent = self.sent[-late:]

    def finish(self):
        for copy in self.sent:
            copy.wait_send()


class Spool:
    def __init__(self, sem):
        self.sem = sem
        self.count = 0
        self.open = []

    def go(self, src, dst):
        copy = pltpu.make_async_copy(src, dst, self.sem.at[self.count])
        self.count += 1
        copy.start()
        self.open.append(copy)
        return copy

    def wait(self, copy):
        copy.wait()
        self.open = [item for item in self.open if item is not copy]

    def finish(self):
        for copy in self.open:
            copy.wait()


def own_micro(order_s, h, count):
    m_own = jnp.int32(0)
    for m in range(count):
        m_own = m_own + jnp.where(order_s[0, m] == h, jnp.int32(m), jnp.int32(0))
    return m_own


def range_of(start, tops, m_own, count):
    now = jnp.full((1, 1), start, F32)
    own = now
    for m in range(1, count):
        now = DECAY * now + (1.0 - DECAY) * tops[:, m - 1: m]
        own = jnp.where(m_own == m, now, own)
    return own


AXES = ("y", "z2", "z1", "x")
WAYS = (
    (("x", "z1", "y", "z2"), ("y", "x", "z2", "z1"), ("z1", "y", "z2", "x")),
    (("x", "y", "z1", "z2"), ("y", "z1", "z2", "x"), ("z1", "x", "y", "z2")),
    (("x", "y", "z1", "z2"), ("z1", "y", "x", "z2"), ("y", "x", "z1", "z2")),
)
SHARES = ((2, 3, 1), (2, 1, 3), (2, 2, 2))
PLAN = {
    "norm": ((0, 0, 2),),
    "t3h2": ((0, 0, 0),),
    "t2h1": ((0, 0, 1),),
    "t2e": ((1, 0, 2), (1, 0, 0),),
    "t1h0": ((1, 0, 1),),
    "t1h1": ((0, 1, 2),),
    "t1h2": ((0, 1, 0),),
    "t1e": ((0, 1, 1),),
    "t0e": ((1, 1, 1), (2, 0, 2),),
}
TAIL = (
    (0, 2, 2), "S1", (1, 1, 0), (1, 1, 2), (0, 2, 0), "S2", (2, 0, 1), (0, 2, 1), (2, 0, 0), "dx2", (1, 2, 1),
    (1, 2, 2), (1, 2, 0), (0, 3, 1), (0, 3, 0), (2, 1, 2), "dx3", (0, 3, 2), (2, 1, 1), "S3", (1, 3, 1),
    (1, 3, 2), (2, 2, 2), (2, 2, 1), (2, 1, 0), "S4", (1, 3, 0), (2, 3, 2), (2, 2, 0), (2, 3, 1), "S5",
    (2, 3, 0),
)


def layer_kernel(joined, nd, nh, part, len_s, order_s, range_s, x_in, dy_in, pw_in, ow_in, wu_in, wd_in, pb_ref, ub_ref,
                 gain_ref, shift_ref,
                 out_own, out_got, dx_own, dx_got, sums, small_sum, tops_o, wa_h, n1_h,
                 xl, xs, wa, wu, wd, bias, ab, qkv, c_ref, cq, lse, lse_t, inv1, y1, f_ref, gq, acc, dz, dzb, tr, tr_b, a_t,
                 df, dc_ref, kt_ref, dqt_ref, dqkv, live, mask, kept, got_core, got1, got2, got3, got4, out_stage,
                 small_now, small_got, cand, slots,
                 spool_sem, send_sem, recv_sem, top_send, top_recv, free_sem, plain_sem):
    g = lax.axis_index("dp")
    h = lax.axis_index("head")
    n = nd * nh
    count, width = y1.shape
    hc = c_ref.shape[2]
    fc = f_ref.shape[2]
    heads = hc // HEAD_DIM
    micro = nh
    sixth = width // 6
    eighth = width // 8
    scale = HEAD_DIM ** -0.5
    lanes = lax.broadcasted_iota(jnp.int32, (1, 128), 1)
    bit = {"x": lax.rem(g, 2), "z1": lax.rem(g // 2, 2), "z2": g // 4, "y": 0}
    where = {"x": (g ^ 1, h), "z1": (g ^ 2, h), "z2": (g ^ 4, h), "y": (g, h ^ 2), "core": (g, h ^ 1)}
    sibling, across = where["core"], where["y"]

    def peer(d):
        return (g ^ (d // nh), h ^ lax.rem(d, nh))

    bar = pltpu.get_barrier_semaphore()

    def hello(d, carry):
        pl.semaphore_signal(bar, inc=1, device_id=peer(n - d), device_id_type=MESH)
        return carry

    lax.fori_loop(1, n, hello, 0)
    spool = Spool(spool_sem)
    wires = Wires(send_sem, recv_sem)
    load_x = spool.go(x_in, xl)
    load_w = []
    for i in range(4):
        for x in (0, 1):
            rows = pl.ds(x * eighth, eighth)
            load_w.append(spool.go(ow_in.at[rows, :] if i == 3 else pw_in.at[i, rows, :], wa.at[0, i // 2, i % 2, x]))
    own_x = spool.go(x_in.at[h], xs.at[0])
    own_wu = spool.go(wu_in, wu.at[0])
    own_wd = spool.go(wd_in, wd.at[0])

    def block_rows(k):
        return slice(k * part, (k + 1) * part)

    m_own = own_micro(order_s, h, micro)
    length = len_s[0, h]
    for k in range(nh):
        start = (h ^ k) * part
        rows = start + lax.broadcasted_iota(jnp.int32, (part, 1), 0)
        live[block_rows(k), :] = jnp.where(rows < length, 1.0, 0.0)
        cols = start + lax.broadcasted_iota(jnp.int32, (1, part), 1)
        mask[:, block_rows(k)] = jnp.where(cols < length, 0.0, MASK_FILL)
    bias[0] = jnp.zeros_like(bias[0])
    bias[0, 0:1, :hc] = pb_ref[0:1, :].astype(F32)
    bias[0, 0:1, 2 * hc:3 * hc] = pb_ref[1:2, :].astype(F32)
    bias[0, 1:2, :] = ub_ref[...].astype(F32)
    ga, gb = gain_ref[0:1, :].astype(F32), gain_ref[1:2, :].astype(F32)
    bo, ca, bd, cb = [shift_ref[i:i + 1, :].astype(F32) for i in range(4)]
    lse[...] = jnp.zeros_like(lse)
    small_now[0] = jnp.zeros_like(small_now[0])
    tops_o[4:8, :] = jnp.zeros((4, 128), F32)

    def exchange_start(stage, row):
        cand[stage] = row

        def send(d, carry):
            remote(cand.at[stage], slots.at[stage, d - 1], top_send.at[stage], top_recv.at[stage], peer(n - d)).start()
            return carry

        lax.fori_loop(1, n, send, 0)

    def exchange_end(stage):
        pltpu.make_async_copy(slots.at[stage], slots.at[stage], top_recv.at[stage]).wait()
        top = jnp.maximum(cand[stage], jnp.max(slots[stage], axis=0))
        tops_o[stage:stage + 1, :] = top
        return range_of(range_s[0, stage], top, m_own, micro)

    def own_lane(value):
        return jnp.where(lanes == m_own, value, 0.0)

    spool.wait(load_x)
    row0 = jnp.zeros((1, 128), F32)
    local_rows = h * part + lax.broadcasted_iota(jnp.int32, (part, 1), 0)
    for s in range(micro):
        lit = jnp.where(local_rows < len_s[0, s], 1.0, 0.0)
        top = lane_top(span_top(xl[s].astype(F32), lit))
        row0 = jnp.maximum(row0, jnp.where(lanes == own_micro(order_s, s, micro), top, 0.0))
    for copy in load_w:
        spool.wait(copy)

    pl.semaphore_wait(bar, n - 1)

    mine = lax.rem(g, 4)

    def cut_view(ref):
        return lambda slot, q, i: ref.at[slot, q // 2, lax.rem(q, 2)] if i is None else ref.at[
            slot, q // 2, lax.rem(q, 2), i]

    def flat_view(ref):
        def view(slot, q, i):
            size = 2 * eighth if i is None else eighth
            start = pl.multiple_of(q * (2 * eighth) + (0 if i is None else i) * eighth, eighth)
            return ref.at[slot, pl.ds(start, size), :]

        return view

    class Weight:
        def __init__(self, land, view):
            self.land, self.view = land, view
            self.leaps, self.round, self.last = {}, {}, []

        def hand(self):
            self.core = wires.go(self.land.at[0], self.land.at[1], sibling)

        def leap(self, i):
            self.leaps[i] = wires.go(self.view(0, mine, i), self.view(2, mine, i), across)

        def pass_on(self, q, i, to):
            return wires.go(self.view(2, q, i), self.view(2, q, i), to)

        def relay(self, q, i):
            self.last.append(wires.go(self.view(2, q, i), self.view(3, q, i), sibling))

        def first(self, i):
            self.leaps[i].wait_recv()
            for e in (1, 2):
                self.round[e, i] = self.pass_on(mine, i, (g ^ e, h))
            self.relay(mine, i)

        def second(self):
            self.round[1, 0].wait_recv()
            self.round[3, 0] = self.pass_on(mine ^ 1, 0, (g ^ 2, h))
            self.round[2, 1].wait_recv()
            self.round[3, 1] = self.pass_on(mine ^ 2, 1, (g ^ 1, h))

        def third(self):
            self.round[1, 1].wait_recv()
            self.relay(mine ^ 1, None)
            self.round[2, 0].wait_recv()
            self.relay(mine ^ 2, None)

        def fourth(self):
            self.round[3, 0].wait_recv()
            self.round[3, 1].wait_recv()
            self.relay(mine ^ 3, None)

        def done(self):
            for copy in self.last:
                copy.wait_recv()

        def drained(self):
            for copy in [self.core, *self.leaps.values(), *self.round.values(), *self.last]:
                wires.leave(copy)

    way_a = Weight(wa, cut_view(wa))
    way_u = Weight(wu, flat_view(wu))
    way_d = Weight(wd, flat_view(wd))
    exchange_start(0, row0)
    way_a.hand()
    way_a.leap(0)
    way_a.leap(1)
    x_wait = [wires.go(x_in.at[h ^ k], xs.at[k], (g, h ^ k)) for k in (2, 3, 1)]
    bias_wait = [wires.go(bias.at[0], bias.at[k], (g, h ^ k)) for k in (1, 2, 3)]
    spool.wait(own_wu)
    way_u.hand()
    way_u.leap(0)
    way_u.leap(1)
    r0 = exchange_end(0)
    way_a.first(0)
    way_a.first(1)
    way_a.second()
    way_a.third()
    way_a.fourth()
    spool.wait(own_x)
    for copy in x_wait:
        copy.wait_recv()
    ri0 = 1.0 / r0
    for k in range(nh):
        ab[block_rows(k), :] = (r0 * jnp.tanh(xs[k].astype(F32) * ri0)).astype(BF16)
    for copy in bias_wait:
        copy.wait_recv()

    def weight_a(k):
        return wa[k].reshape(width, width)

    def block(k):
        qkv[k] = (dot(ab[...], weight_a(k)[: 3 * hc, :], NT) + bias[k, 0:1, : 3 * hc]).astype(BF16)
        for j in range(heads):
            lo = j * HEAD_DIM
            keys = qkv[k, :, hc + lo: hc + lo + HEAD_DIM]
            vals = qkv[k, :, 2 * hc + lo: 2 * hc + lo + HEAD_DIM]
            q = qkv[k, :, lo: lo + HEAD_DIM] * BF16(scale)
            s = dot(q, keys, NT) + mask[...]
            top = jnp.max(s, axis=1, keepdims=True)
            e = jnp.exp(s - top)
            den = jnp.sum(e, axis=1, keepdims=True)
            p = (e * (1.0 / den)).astype(BF16)
            c_ref[k, :, lo: lo + HEAD_DIM] = dot(p, vals, NN)
            at = k * 8 + j
            lse[:, at: at + 1] = top + jnp.log(den)
        return span_top(c_ref[k], live[...])

    best = block(0)
    way_a.core.wait_recv()
    best = jnp.maximum(best, block(1))
    way_u.first(0)
    best = jnp.maximum(best, block(2))
    way_a.done()
    best = jnp.maximum(best, block(3))
    exchange_start(1, own_lane(lane_top(best)))
    way_u.first(1)
    spool.wait(own_wd)
    way_d.leap(0)
    way_d.leap(1)
    way_d.hand()
    save_wa = spool.go(wa, wa_h)
    turned = lse[...].T
    for k in range(nh):
        lse_t[k] = turned[k * 8:(k + 1) * 8, :]
    for k in range(nh):
        a_t[:, block_rows(k)] = ab[block_rows(k), :].astype(F32).T.astype(BF16)
    r1 = exchange_end(1)
    way_d.first(0)

    ri1 = 1.0 / r1
    for k in range(nh):
        cq[k] = (r1 * jnp.tanh(c_ref[k] * ri1)).astype(BF16)
        o1 = dot(cq[k], weight_a(k)[3 * hc:, :], NN)
        if k == 0:
            acc[...] = o1
        else:
            acc[...] += o1
    best = jnp.zeros((1, width), F32)
    for k in range(nh):
        rows = block_rows(k)
        nn, inv = norm_parts(xs[k].astype(F32) + (acc[rows, :] + bo))
        dz[rows, :] = nn
        inv1[rows, :] = inv
        y = nn * ga + ca
        y1[rows, :] = y
        best = jnp.maximum(best, span_top(y, live[rows, :]))
    exchange_start(2, own_lane(lane_top(best)))
    way_u.second()
    save_n1 = spool.go(dz, n1_h)
    way_u.third()
    way_d.first(1)
    own_dy = spool.go(dy_in.at[h], xl.at[0])
    dy_wait = [wires.go(dy_in.at[h ^ k], xl.at[k], (g, h ^ k)) for k in (2, 3, 1)]
    for k in range(nh):
        t = jnp.tanh(c_ref[k] * ri1)
        c_ref[k] = 1.0 - t * t
    r2 = exchange_end(2)
    ri2 = 1.0 / r2
    ab[...] = (r2 * jnp.tanh(y1[...] * ri2)).astype(BF16)

    def widen(k):
        f = dot(ab[...], wu[k], NN) + bias[k, 1:2, :]
        f_ref[k] = f
        return span_top(f * (0.5 * (1.0 + lax.erf(f * (0.5 ** 0.5)))), live[...])

    best = widen(0)
    way_u.core.wait_recv()
    best = jnp.maximum(best, widen(1))
    way_u.fourth()
    best = jnp.maximum(best, widen(2))
    way_u.done()
    best = jnp.maximum(best, widen(3))
    exchange_start(3, own_lane(lane_top(best)))
    way_d.second()
    for k in range(nh):
        tr_b[:, block_rows(k)] = ab[block_rows(k), :].astype(F32).T.astype(BF16)
    for k in range(nh):
        f = f_ref[k]
        cdf = 0.5 * (1.0 + lax.erf(f * (0.5 ** 0.5)))
        gq[k] = (cdf + f * (jnp.exp(-0.5 * f * f) * ROOT)).astype(BF16)
        f_ref[k] = f * cdf
    wires.drain(24)
    r3 = exchange_end(3)
    ri3 = 1.0 / r3

    def squash(k):
        t = jnp.tanh(f_ref[k] * ri3)
        f_ref[k] = gq[k].astype(F32) * (1.0 - t * t)
        gq[k] = (r3 * t).astype(BF16)

    def lower(k):
        o2 = dot(gq[k], wd[k], NN)
        if k == 0:
            acc[...] = o2
        else:
            acc[...] += o2

    squash(0)
    lower(0)
    squash(1)
    way_d.third()
    way_d.core.wait_recv()
    lower(1)
    squash(2)
    way_d.fourth()
    lower(2)
    squash(3)
    way_d.done()
    lower(3)
    spool.wait(own_dy)
    for copy in dy_wait:
        copy.wait_recv()
    spool.wait(save_n1)

    zero = jnp.zeros((1, width), F32)
    s_gb = s_cb = s_bd = zero
    tail = []
    for k in (2, 3, 1, 0):
        rows = block_rows(k)
        nn, inv = norm_parts(y1[rows, :] + (acc[rows, :] + bd))
        out = nn * gb + cb
        if k == 0:
            out_own[...] = out
        else:
            out_stage[0, k - 1] = out.astype(BF16)
            tail.append(wires.go(out_stage.at[0, k - 1], out_got.at[k - 1], (g, h ^ k)))
        dy = xl[k].astype(F32)
        d = norm_back(dy * gb, nn, inv)
        dz[rows, :] = d
        dzb[rows, :] = d.astype(BF16)
        tr[:, rows] = d.T.astype(BF16)
        s_gb = s_gb + jnp.sum(dy * nn, axis=0, keepdims=True)
        s_cb = s_cb + jnp.sum(dy, axis=0, keepdims=True)
        s_bd = s_bd + jnp.sum(d, axis=0, keepdims=True)

    way_a.drained()
    spool.wait(save_wa)
    core = {}
    eighths = [(r * eighth, (r // 4, (r // 2) % 2, r % 2)) for r in range(8)]

    def spread(block_no, value):
        for at, spot in eighths:
            wa[(block_no, *spot)] = value[at: at + eighth, :].astype(BF16)

    def plain(chunk, k, value):
        spread(0, value)
        copy = pltpu.make_async_copy(wa.at[0], sums.at[chunk, k], plain_sem)
        copy.start()
        copy.wait()

    def home(chunk, index):
        if chunk < 2:
            return kept, (chunk, *index)
        first = pl.ds(2, 2) if isinstance(index[0], slice) else 2 + index[0]
        return wa, (first, *index[1:])

    def give(chunk, j, block_no, k, value):
        if not joined:
            plain(chunk, k, value)
            return
        spread(block_no, value)
        if (chunk, j) == (2, 1):
            pl.semaphore_wait(free_sem, 1)
        core[chunk, j] = wires.go(wa.at[block_no], got_core.at[chunk % 2, j], sibling)

    def keep(chunk, j, k, value):
        if not joined:
            plain(chunk, k, value)
            return
        core[chunk, j].wait_recv()
        for at, spot in eighths:
            ref, index = home(chunk, (j, *spot))
            ref[index] = (value[at: at + eighth, :] + got_core[(chunk % 2, j, *spot)].astype(F32)).astype(BF16)

    got = (None, got1, got2, got3, got4)
    pending = {}

    def region(way, step, last):
        index = []
        for axis in AXES:
            at = way.index(axis)
            if at == step:
                index.append(last)
            else:
                index.append(bit[axis] if at < step else slice(None))
        return index

    def columns(chunk, i):
        share = SHARES[chunk]
        return sum(share[:i]) * sixth, share[i] * sixth

    def send_way(chunk, step, i, j=None):
        axis = WAYS[chunk][i][step]
        index = region(WAYS[chunk][i], step, 1 if axis == "y" else 1 - bit[axis])
        dst = got[step + 1].at[chunk]
        if j is not None:
            index[0] = j
            dst = dst.at[j]
        ref, index = home(chunk, index)
        cols = pl.ds(*columns(chunk, i))
        dst = dst.at[(*[slice(None)] * (len(dst.shape) - 1), cols)]
        pending.setdefault((chunk, step, i), []).append(
            wires.go(ref.at[(*index, slice(None), cols)], dst, where[axis]))

    def send_first(chunk, j):
        if not joined:
            return
        for i, way in enumerate(WAYS[chunk]):
            if way[0] != "y":
                send_way(chunk, 0, i, j)
            elif j == 1:
                send_way(chunk, 0, i)

    def pump(chunk, step, *ways):
        for i in ways:
            way = WAYS[chunk][i]
            for copy in pending[chunk, step, i]:
                copy.wait_recv()
            start, size = columns(chunk, i)
            cols = slice(start, start + size)
            index = region(way, step, bit[way[step]])
            spots = [()]
            for item in index:
                if isinstance(item, slice):
                    spots = [s + (v,) for s in spots for v in (0, 1)]
            for spot in spots:
                left = iter(spot)
                ref, full = home(chunk, [next(left) if isinstance(item, slice) else item for item in index])
                value = (ref[(*full, slice(None), cols)].astype(F32)
                         + got[step + 1][(chunk, *spot, slice(None), cols)].astype(F32))
                if step == 3:
                    sums[chunk, :, cols] = value
                else:
                    ref[(*full, slice(None), cols)] = value.astype(BF16)
            if step < 3:
                send_way(chunk, step + 1, i)

    def pumps(place):
        if joined:
            for job in PLAN.get(place, ()):
                pump(*job)

    for k in (3, 1):
        give(0, k // 2, k // 2, k, dot(tr[...], gq[k], NN))
    way_d.drained()
    load_wa = {}
    turns = (3, 2, 1, 0)

    def units(k, first):
        d = (dot(dzb[...], wd[k], NT) * f_ref[k]).astype(BF16)
        df[...] = d
        small_now[0, pl.ds(4 + (h ^ k), 1), :] = jnp.sum(d.astype(F32), axis=0, keepdims=True)
        load_wa[k] = [
            spool.go(wa_h.at[(k, *spot)], wd.at[k, pl.ds(at, eighth), :]) for at, spot in eighths]
        part_sum = dot(df[...], wu[k], NT)
        if first:
            acc[...] = part_sum
        else:
            acc[...] += part_sum
        return dot(tr_b[...], df[...], NN)

    for k in (3, 1):
        give(1, k // 2, 2 + k // 2, k, units(k, k == 3))
    load_n1 = spool.go(n1_h, f_ref.at[1])
    for k in (2, 0):
        keep(0, k // 2, k, dot(tr[...], gq[k], NN))
        send_first(0, k // 2)
    if joined:
        pl.semaphore_signal(free_sem, inc=1, device_id=sibling, device_id_type=MESH)
    for k in (2, 0):
        keep(1, k // 2, k, units(k, False))
        send_first(1, k // 2)
        pumps(f"u{k}")

    spool.wait(load_n1)
    s_ga = s_ca = s_bo = zero
    for k in range(nh):
        rows = block_rows(k)
        t = jnp.tanh(y1[rows, :] * ri2)
        dy1 = dz[rows, :] + acc[rows, :] * (1.0 - t * t)
        nn = f_ref[1, rows, :]
        d = norm_back(dy1 * ga, nn, inv1[rows, :])
        dz[rows, :] = d
        dzb[rows, :] = d.astype(BF16)
        tr[:, rows] = d.T.astype(BF16)
        s_ga = s_ga + jnp.sum(dy1 * nn, axis=0, keepdims=True)
        s_ca = s_ca + jnp.sum(dy1, axis=0, keepdims=True)
        s_bo = s_bo + jnp.sum(d, axis=0, keepdims=True)
    for i, row in enumerate((s_ga, s_gb, s_bo, s_ca, s_bd, s_cb)):
        small_now[0, 8 + i: 9 + i, :] = row
    pumps("norm")

    def turn(i):
        k = turns[i]
        for copy in load_wa[k]:
            spool.wait(copy)
        dc_ref[...] = (dot(dzb[...], wd[k, 3 * hc:, :], NT) * c_ref[k]).astype(BF16)
        kt_ref[...] = qkv[k, :, hc: 2 * hc].astype(F32).T.astype(BF16)
        for j in range(heads):
            lo = j * HEAD_DIM
            keys = qkv[k, :, hc + lo: hc + lo + HEAD_DIM]
            vals = qkv[k, :, 2 * hc + lo: 2 * hc + lo + HEAD_DIM]
            q = qkv[k, :, lo: lo + HEAD_DIM] * BF16(scale)
            dc = dc_ref[:, lo: lo + HEAD_DIM]
            s = dot(keys, q, NT)
            p = jnp.where(live[...] > 0.0, jnp.exp(s - lse_t[k, j: j + 1, :]), 0.0)
            pd = p * dot(vals, dc, NT)
            delta = jnp.sum(pd, axis=0, keepdims=True)
            ds = (pd - p * delta).astype(BF16)
            dqkv[:, 2 * hc + lo: 2 * hc + lo + HEAD_DIM] = dot(p.astype(BF16), dc, NN).astype(BF16)
            dqkv[:, hc + lo: hc + lo + HEAD_DIM] = dot(ds, q, NN).astype(BF16)
            dqt_ref[lo: lo + HEAD_DIM, :] = dot(kt_ref[lo: lo + HEAD_DIM, :], ds, NN) * scale
            pumps(f"t{k}h{j}")
        dqkv[:, :hc] = dqt_ref[...].T.astype(BF16)
        small_now[0, pl.ds(h ^ k, 1), : 3 * hc] = jnp.sum(dqkv[...].astype(F32), axis=0, keepdims=True)
        da = dot(dqkv[...], wd[k, : 3 * hc, :], NN)
        if i == 0:
            acc[...] = da
        else:
            acc[...] += da
        return jnp.concatenate([dot(a_t[...], dqkv[...], NN), dot(tr[...], cq[k], NN)], axis=1)

    def sent(chunk, j):
        if joined:
            wires.leave(core[chunk, j])

    for i, k in enumerate(turns):
        j = k // 2
        value = turn(i)
        if k % 2:
            sent(0, j)
            give(2, j, j, k, value)
        else:
            sent(1, j)
            keep(2, j, k, value)
            send_first(2, j)
        pumps(f"t{k}e")
    small_ways = ("core", "y", "x", "z1", "z2")
    small_copy = {}

    def small_step(i):
        if not joined:
            return
        if i > 0:
            small_copy[i - 1].wait_recv()
            small_now[i] = small_now[i - 1] + small_got[i - 1]
        if i < 5:
            small_copy[i] = wires.go(small_now.at[i], small_got.at[i], where[small_ways[i]])

    small_step(0)
    for k in (2, 3, 1, 0):
        rows = block_rows(k)
        t = jnp.tanh(xs[k].astype(F32) * ri0)
        d = dz[rows, :] + acc[rows, :] * (1.0 - t * t)
        if k == 0:
            dx_own[...] = d
        else:
            out_stage[1, k - 1] = d.astype(BF16)

    def send_dx(k):
        tail.append(wires.go(out_stage.at[1, k - 1], dx_got.at[k - 1], (g, h ^ k)))

    for stage in range(4):
        pltpu.make_async_copy(slots.at[stage], slots.at[stage], top_send.at[stage]).wait()
    for job in TAIL:
        wires.drain(16)
        if job == "dx2":
            send_dx(2)
        elif job == "dx3":
            send_dx(3)
            send_dx(1)
        elif isinstance(job, str):
            small_step(int(job[1:]))
        elif joined:
            pump(*job)
    small_sum[...] = small_now[5 if joined else 0]
    for copy in tail:
        copy.wait_recv()
    wires.finish()
    spool.finish()


def layer(joined, lengths, order, ranges, x_in, dy_in, pw, ow, wu, wd, pb, ub, gains, shifts):
    nd, nh = lax.axis_size("dp"), lax.axis_size("head")
    slots, part, width = x_in.shape
    count = slots * part
    hc, fc = ow.shape[0], wu.shape[1]
    rows = width // 8

    def shape(*dims, kind=F32):
        return jax.ShapeDtypeStruct(dims, kind)

    def half(*dims):
        return pltpu.VMEM(dims, BF16)

    def full(*dims):
        return pltpu.VMEM(dims, F32)

    smem = pl.BlockSpec(memory_space=pltpu.SMEM)
    return pl.pallas_call(
        functools.partial(layer_kernel, joined, nd, nh, part),
        out_shape=(
            shape(part, width), shape(nh - 1, part, width, kind=BF16), shape(part, width),
            shape(nh - 1, part, width, kind=BF16),
            shape(3, rows, width) if joined else shape(3, nh, 2, 2, 2, rows, width, kind=BF16),
            shape(16, width), shape(8, 128), shape(nh, 2, 2, 2, rows, width, kind=BF16), shape(count, width),
        ),
        in_specs=[smem] * 3 + [ANY] * 6 + [VM] * 4,
        out_specs=[VM, ANY, VM, ANY, VM if joined else ANY, VM, VM, ANY, ANY],
        scratch_shapes=[
            half(slots, part, width), half(slots, part, width), half(nh, 2, 2, 2, rows, width), half(nh, width, fc),
            half(nh, fc, width), full(nh, 8, fc), half(count, width), half(nh, count, 3 * hc), full(nh, count, hc),
            half(nh, count, hc), full(count, 128), full(nh, 8, count), full(count, 1), full(count, width),
            full(nh, count, fc), half(nh, count, fc), full(count, width), full(count, width), half(count, width),
            half(width, count), half(width, count), half(width, count), half(count, fc), half(count, hc), half(hc, count),
            full(hc, count), half(count, 3 * hc), full(count, 1), full(1, count),
            half(2, 2, 2, 2, 2, rows, width), half(2, 2, 2, 2, 2, rows, width),
            half(3, 2, 2, 2, rows, width), half(3, 2, 2, rows, width), half(3, 2, rows, width),
            half(3, rows, width), half(2, nh - 1, part, width), full(6, 16, width), full(5, 16, width),
            full(4, 1, 128), full(4, nd * nh - 1, 1, 128),
            pltpu.SemaphoreType.DMA((64,)), pltpu.SemaphoreType.DMA((120,)), pltpu.SemaphoreType.DMA((120,)),
            pltpu.SemaphoreType.DMA((4,)), pltpu.SemaphoreType.DMA((4,)), pltpu.SemaphoreType.REGULAR,
            pltpu.SemaphoreType.DMA,
        ],
        compiler_params=pltpu.CompilerParams(collective_id=0, has_side_effects=True, vmem_limit_bytes=LIMIT),
    )(lengths, order, ranges, x_in, dy_in, pw, ow, wu, wd, pb, ub, gains, shifts)


def finish_kernel(range_s, tops, out_own, out_got, dx_own, dx_got, sums, small,
                  out_o, dx_o, proj_o, bias_o, outw_o, up_o, off_o, down_o, gain_o, shift_o, range_o):
    h = lax.axis_index("head")
    nh = out_o.shape[0]
    hc = proj_o.shape[3]
    for own, got, dst in ((out_own, out_got, out_o), (dx_own, dx_got, dx_o)):
        dst[h] = own[...]
        for k in range(1, nh):
            dst[h ^ k] = got[k - 1].astype(F32)
    for i in range(3):
        proj_o[0, i] = sums[2, :, i * hc:(i + 1) * hc]

    def turned(value):
        rows = value.shape[0]
        filled = jnp.concatenate([value, jnp.zeros((-rows % 128, value.shape[1]), F32)], axis=0)
        return filled.T[:, :rows]

    outw_o[0] = turned(sums[2, :, 3 * hc:])
    up_o[0] = sums[1]
    down_o[0] = sums[0]
    width = small.shape[1]
    for k in range(nh):
        bias_o[0, 0:1, k * hc:(k + 1) * hc] = small[k:k + 1, :hc]
        bias_o[0, 1:2, k * hc:(k + 1) * hc] = small[k:k + 1, 2 * hc:3 * hc]
        off_o[0:1, k * width:(k + 1) * width] = small[4 + k:5 + k, :]
    gain_o[0] = small[8:10, :]
    shift_o[0] = small[10:14, :]
    for i in range(4):
        now = jnp.full((1, 1), range_s[0, i], F32)
        for m in range(4):
            now = DECAY * now + (1.0 - DECAY) * tops[i:i + 1, m:m + 1]
        range_o[0:1, i:i + 1] = now


def local(kernel, outs, out_specs, in_specs, scratch, *args):
    return pl.pallas_call(
        kernel,
        out_shape=outs,
        in_specs=in_specs,
        out_specs=out_specs,
        scratch_shapes=scratch,
        compiler_params=pltpu.CompilerParams(vmem_limit_bytes=LIMIT),
    )(*args)


def body(hidden_in, seq_lengths, batch_order, clip_ranges, proj_weight, proj_bias, out_weight,
         up_weight, up_bias, down_weight, norm_gains, out_biases, cotangent):
    nd, nh = lax.axis_size("dp"), lax.axis_size("head")
    slots, part, width = hidden_in.shape
    hc = proj_bias.shape[2]
    fc = up_bias.shape[1]
    joined = nd == 8
    out_own, out_got, dx_own, dx_got, sums, small, tops, _, _ = layer(
        joined, seq_lengths, batch_order, clip_ranges, hidden_in, cotangent, proj_weight[0].transpose(0, 2, 1),
        out_weight[0], up_weight[0], down_weight[0], proj_bias[0], up_bias, norm_gains[0], out_biases[0])

    def shape(*dims):
        return jax.ShapeDtypeStruct(dims, F32)

    if joined:
        outs = local(
            finish_kernel,
            (shape(slots, part, width), shape(slots, part, width), shape(1, 3, width // nd, hc),
             shape(1, 2, nh * hc), shape(1, hc, width // nd), shape(1, width // nd, fc), shape(1, nh * fc),
             shape(1, width // nd, fc), shape(1, 2, width), shape(1, 4, width), shape(1, 4)),
            [VM] * 11, [pl.BlockSpec(memory_space=pltpu.SMEM)] + [VM] * 7, [],
            clip_ranges, tops, out_own, out_got, dx_own, dx_got, sums, small)
        return (*outs[:7], outs[7].swapaxes(1, 2), *outs[8:])
    h = lax.axis_index("head")
    sums, small = settle_plain(sums.reshape(3, nh, width, width), small, h)
    index = h ^ jnp.arange(nh)
    hidden_out = jnp.concatenate([out_own[None], out_got.astype(F32)])[index]
    input_grad = jnp.concatenate([dx_own[None], dx_got.astype(F32)])[index]
    now = clip_ranges
    for m in range(slots):
        now = DECAY * now + (1.0 - DECAY) * tops[None, :4, m]
    return (
        hidden_out, input_grad, sums[2][:, : 3 * hc].reshape(1, -1, 3, hc).transpose(0, 2, 1, 3),
        jnp.stack([small[:4, :hc].reshape(-1), small[:4, 2 * hc: 3 * hc].reshape(-1)])[None],
        sums[2][:, 3 * hc:].T[None], sums[1][None], small[4:8].reshape(1, -1), sums[0].T[None],
        small[None, 8:10], small[None, 10:14], now,
    )


def solution(mesh):
    in_specs = (
        P("dp", "head", None), P("dp", None), P("dp", None), P(),
        P(None, None, None, "head"), P(None, None, "head"), P(None, "head", None),
        P(None, None, "head"), P(None, "head"), P(None, "head", None), P(), P(),
        P("dp", "head", None),
    )
    out_specs = (
        P("dp", "head", None), P("dp", "head", None), P(None, None, "dp", "head"), P(),
        P(None, "head", "dp"), P(None, "dp", "head"), P(), P(None, "head", "dp"), P(), P(), P(),
    )
    return jax.shard_map(body, mesh=mesh, in_specs=in_specs, out_specs=out_specs, check_vma=False)
```
